32 devices in a mesh: tok: 4 (over x, core), feat: 8 (over z, y).
Axes of the slice: x: 2, y: 2, z: 4, core: 2. Of those that a mesh axis runs over, the one named last changes fastest.
Arguments:
- inputs: bfloat16 [9248, 1024], P(('tok', 'feat')), may hold values from -6 to 6
- valid: int32 [16], P('tok'), may hold values 0 or 1
- cotangent: bfloat16 [9248, 1024], P(('tok', 'feat')), may hold values from -6 to 6
- w_query: bfloat16 [1024, 1024], P('feat'), may hold values from -0.1875 to 0.1875
- w_key: bfloat16 [1024, 1024], P('feat'), may hold values from -0.1875 to 0.1875
- w_value: bfloat16 [1024, 1024], P('feat'), may hold values from -0.1875 to 0.1875
- b_query: bfloat16 [1024], P('feat'), may hold values from -3 to 3
- b_value: bfloat16 [1024], P('feat'), may hold values from -0.59765625 to 0.59765625
- w_attn_out: bfloat16 [1024, 1024], P('feat'), may hold values from -2 to 2
- b_attn_out: bfloat16 [1024], replicated, may hold values from -0.59765625 to 0.59765625
- w_mlp_in: bfloat16 [1024, 4096], P(None, 'feat'), may hold values from -0.1875 to 0.1875
- b_mlp_in: bfloat16 [4096], P('feat'), may hold values from -3 to 3
- w_mlp_out: bfloat16 [4096, 1024], P('feat'), may hold values from -0.1875 to 0.1875
- b_mlp_out: bfloat16 [1024], replicated, may hold values from -0.59765625 to 0.59765625
- attention_norm_gain: bfloat16 [1024], replicated, may hold values from 0.5 to 1.5
- attention_norm_shift: bfloat16 [1024], replicated, may hold values from -0.59765625 to 0.59765625
- feedforward_norm_gain: bfloat16 [1024], replicated, may hold values from 0.5 to 1.5
- feedforward_norm_shift: bfloat16 [1024], replicated, may hold values from -0.59765625 to 0.59765625
Outputs:
- output: float32 [9248, 1024], P(('tok', 'feat'))
- layer_input_gradient: float32 [9248, 1024], P(('tok', 'feat'))
- grad_w_query: float32 [1024, 1024], P('feat')
- grad_w_key: float32 [1024, 1024], P('feat')
- grad_w_value: float32 [1024, 1024], P('feat')
- grad_b_query: float32 [1024], P('feat')
- grad_b_value: float32 [1024], P('feat')
- grad_w_attn_out: float32 [1024, 1024], P('feat')
- grad_b_attn_out: float32 [1024], replicated
- grad_w_mlp_in: float32 [1024, 4096], P(None, 'feat')
- grad_b_mlp_in: float32 [4096], P('feat')
- grad_w_mlp_out: float32 [4096, 1024], P('feat')
- grad_b_mlp_out: float32 [1024], replicated
- attention_gain_gradient: float32 [1024], replicated
- grad_s_attn: float32 [1024], replicated
- feedforward_gain_gradient: float32 [1024], replicated
- grad_s_mlp: float32 [1024], replicated
- stream_rms: float32 [4], replicated
The draws below stay inside these ranges and needn't reach their ends.
Inputs may be any that keep to these rules, and one draw needn't show every extreme that they name: `valid`: 1 marks a real image, 0 a padded one.
All inputs are finite; a program needn't handle non-finite values. No bound on the sum of `valid` on one device may be relied on, other than what follows from the above.
Results may differ from the reference program's by a relative error of at most 0.017.
Values may be sent and summed in bfloat16 or wider, within the bound.
No kernel may reach another device: no remote copies, remote signals or barrier semaphores. Data moves between devices by JAX's collectives and lax.ppermute only.
A program may use at most 128 MiB of HBM per device.

```python
import jax
import jax.numpy as jnp
from jax import lax

D = 1024
H = 16
DH = 64
FF = 4096
SEQ = 577
IMG_DEV = 4
ROWS_DEV = 289
IMAGES = 16
TOKENS = 9248
N_TOK = 4
N_FEAT = 8


def place_ends(drawn, own_key, low, high):
    dims = drawn.shape
    spot = [jax.random.randint(jax.random.fold_in(own_key, axis), (), 0, dims[axis]) for axis in range(len(dims))]
    drawn = drawn.at[tuple(spot)].set(low)
    longest = dims.index(max(dims))
    spot[longest] = (spot[longest] + 1) % dims[longest]
    return drawn.at[tuple(spot)].set(high)


def block_levels(key, extent, cuts, low, high):
    factor_of, own = 1.0, jax.random.fold_in(key, 6)
    for dim, shards_of in cuts:
        steps = jnp.exp(jax.random.uniform(jax.random.fold_in(own, dim), (shards_of,), jnp.float32, low / len(cuts), high / len(cuts)))
        factor_of = factor_of * jnp.repeat(steps, extent[dim] // shards_of).reshape([-1 if axis == dim else 1 for axis in range(len(extent))])
    return factor_of


def centred(stream_key, shape, width, bound, shards=(), dtype=jnp.bfloat16):
    array = jax.random.normal(stream_key, shape, jnp.float32) * width
    if len(shards) > 0:
        array = block_levels(stream_key, shape, shards, -0.22, 0.18) * array
    return jnp.clip(array, min=-bound, max=bound).astype(dtype)


def setup_inputs(seed: int = 0) -> dict:
    seeds = jax.random.split(jax.random.key(seed), 19)
    return {
        "inputs": centred(seeds[0], (TOKENS, D), 1.0, 6.0, ((0, 32),)),
        "valid": place_ends((jax.random.randint(seeds[1], (IMAGES,), 0, 8) < 7).astype(jnp.int32), jax.random.fold_in(seeds[1], 1), 0, 1),
        "cotangent": centred(seeds[2], (TOKENS, D), 1.0, 6.0, ((0, 32),)),
        "w_query": centred(seeds[3], (D, D), D ** -0.5, 0.1875, ((0, 8),)),
        "w_key": centred(seeds[4], (D, D), D ** -0.5, 0.1875, ((0, 8),)),
        "w_value": centred(seeds[5], (D, D), D ** -0.5, 0.1875, ((0, 8),)),
        "b_query": centred(seeds[6], (D,), 0.5, 3.0, ((0, 8),)),
        "b_value": centred(seeds[7], (D,), 0.1, 0.59765625, ((0, 8),)),
        "w_attn_out": centred(seeds[8], (D, D), (max(D // 128, 2)) ** -0.5, 2.0, ((0, 8),)),
        "b_attn_out": centred(seeds[9], (D,), 0.1, 0.59765625),
        "w_mlp_in": centred(seeds[10], (D, FF), D ** -0.5, 0.1875, ((1, 8),)),
        "b_mlp_in": centred(seeds[11], (FF,), 0.5, 3.0, ((0, 8),)),
        "w_mlp_out": centred(seeds[12], (FF, D), (FF // 4) ** -0.5, 0.1875, ((0, 8),)),
        "b_mlp_out": centred(seeds[13], (D,), 0.1, 0.59765625),
        "attention_norm_gain": jnp.clip(1.0 + 0.1 * jax.random.normal(seeds[14], (D,), jnp.float32), 0.5, 1.5).astype(jnp.bfloat16),
        "attention_norm_shift": centred(seeds[15], (D,), 0.1, 0.59765625),
        "feedforward_norm_gain": jnp.clip(1.0 + 0.1 * jax.random.normal(seeds[16], (D,), jnp.float32), 0.5, 1.5).astype(jnp.bfloat16),
        "feedforward_norm_shift": centred(seeds[17], (D,), 0.1, 0.59765625),
    }


@jax.custom_vjp
def low(v):
    return lax.optimization_barrier(v.astype(jnp.bfloat16)).astype(jnp.float32)

@jax.custom_vjp
def low_back(v):
    return v

def low_keep(v):
    return (low(v), None)

def low_pass(kept, grad):
    return (grad,)

def back_keep(v):
    return (v, None)

def back_low(kept, grad):
    return (low(grad),)
low.defvjp(low_keep, low_pass)
low_back.defvjp(back_keep, back_low)
EPSILON = 1e-05
SLOPE = 1.702

def matmul(left, right):
    return jnp.dot(left, right, precision=lax.Precision.HIGHEST, preferred_element_type=jnp.float32)

def norm_rows(values, norm_gain, shift):
    center = lax.optimization_barrier(jnp.mean(values, axis=-1, keepdims=True))
    spread = lax.optimization_barrier(jnp.mean(values * values, axis=-1, keepdims=True)) - center * center
    return (values - center) * lax.rsqrt(spread + EPSILON) * norm_gain + shift

def image_layer(x_img, params):
    w_query, w_key, w_value, b_query, b_value, w_attn_out, b_attn_out, w_mlp_in, b_mlp_in, w_mlp_out, b_mlp_out, attention_norm_gain, attention_norm_shift, feedforward_norm_gain, feedforward_norm_shift = params
    normed = low(norm_rows(x_img, attention_norm_gain, attention_norm_shift))
    queries = low(low_back(matmul(normed, w_query.T) + b_query))
    key_rows = low(low_back(matmul(normed, w_key.T)))
    value_rows = low(low_back(matmul(normed, w_value.T) + b_value))
    query_heads = queries.reshape(SEQ, H, DH).transpose(1, 0, 2)
    key_heads = key_rows.reshape(SEQ, H, DH).transpose(1, 0, 2)
    value_heads = value_rows.reshape(SEQ, H, DH).transpose(1, 0, 2)
    scores = low_back(jnp.einsum('hqd,hkd->hqk', query_heads, key_heads, precision=lax.Precision.HIGHEST) * DH ** (-0.5))
    probs = low(jax.nn.softmax(scores, axis=-1))
    mixed = low(low_back(jnp.einsum('hqk,hkd->hqd', probs, value_heads, precision=lax.Precision.HIGHEST)))
    merged = mixed.transpose(1, 0, 2).reshape(SEQ, D)
    attn = low_back(matmul(merged, w_attn_out) + b_attn_out)
    middle_state = x_img + attn
    normalized_middle = low(norm_rows(middle_state, feedforward_norm_gain, feedforward_norm_shift))
    hidden = low_back(matmul(normalized_middle, w_mlp_in) + b_mlp_in)
    active = low(hidden * jax.nn.sigmoid(SLOPE * hidden))
    branch = low_back(matmul(active, w_mlp_out) + b_mlp_out)
    result = middle_state + branch
    return (result, (attn, branch))

def to_images(values):
    blocks = values.astype(jnp.float32).reshape(N_TOK, N_FEAT * ROWS_DEV, D)
    return blocks[:, :IMG_DEV * SEQ].reshape(IMAGES, SEQ, D)

def from_images(values):
    blocks = values.reshape(N_TOK, IMG_DEV * SEQ, D)
    blocks = jnp.pad(blocks, ((0, 0), (0, N_FEAT * ROWS_DEV - IMG_DEV * SEQ), (0, 0)))
    return blocks.reshape(TOKENS, D)

def reference(inputs, valid, cotangent, w_query, w_key, w_value, b_query, b_value, w_attn_out, b_attn_out, w_mlp_in, b_mlp_in, w_mlp_out, b_mlp_out, attention_norm_gain, attention_norm_shift, feedforward_norm_gain, feedforward_norm_shift):
    params = tuple((p.astype(jnp.float32) for p in (w_query, w_key, w_value, b_query, b_value, w_attn_out, b_attn_out, w_mlp_in, b_mlp_in, w_mlp_out, b_mlp_out, attention_norm_gain, attention_norm_shift, feedforward_norm_gain, feedforward_norm_shift)))
    stream = to_images(inputs)
    cot_all = to_images(cotangent)
    flags = valid.astype(jnp.float32)
    zero_grads = tuple((jnp.zeros_like(p) for p in params))

    def step(carry, item):
        grads, powers = carry
        x_img, cot_img, flag = item
        result, puller, extras = jax.vjp(image_layer, x_img, params, has_aux=True)
        attn, branch = extras
        x_grad, param_grads = puller(cot_img * flag)
        grads = tuple((total + part for total, part in zip(grads, param_grads)))
        squares = jnp.stack([jnp.sum(x_img * x_img), jnp.sum(attn * attn), jnp.sum(branch * branch), jnp.sum(result * result)])
        return ((grads, powers + flag * squares), (result, x_grad))
    (grads, powers), (results, x_grads) = lax.scan(step, (zero_grads, jnp.zeros((4,), jnp.float32)), (stream, cot_all, flags))
    counted = jnp.maximum(jnp.sum(flags) * SEQ, 1.0) * D
    stream_rms = jnp.sqrt(powers / counted)
    grad_w_query, grad_w_key, grad_w_value, grad_b_query, grad_b_value, grad_w_attn_out, grad_b_attn_out, grad_w_mlp_in, grad_b_mlp_in, grad_w_mlp_out, grad_b_mlp_out, attention_gain_gradient, grad_s_attn, feedforward_gain_gradient, grad_s_mlp = grads
    output = from_images(results)
    layer_input_gradient = from_images(x_grads)
    return (output, layer_input_gradient, grad_w_query, grad_w_key, grad_w_value, grad_b_query, grad_b_value, grad_w_attn_out, grad_b_attn_out, grad_w_mlp_in, grad_b_mlp_in, grad_w_mlp_out, grad_b_mlp_out, attention_gain_gradient, grad_s_attn, feedforward_gain_gradient, grad_s_mlp, stream_rms)
```

```python
import functools

import jax
import jax.numpy as jnp
from jax import lax
from jax.experimental import pallas as pl
from jax.experimental.pallas import tpu as pltpu
from jax.sharding import PartitionSpec as P

D = 1024
DH = 64
SEQ = 577


EPSILON = 1e-05
SLOPE = 1.702


def gelu_slope(values):
    sigmoid = jax.nn.sigmoid(SLOPE * values)
    return sigmoid + SLOPE * values * sigmoid * (1.0 - sigmoid)


def column_sums(values):
    return jnp.sum(values.astype(jnp.float32), axis=0)


def split_heads(values):
    return values.reshape(values.shape[0], values.shape[1] // DH, DH)


def apply_layer_norm(values):
    center = jnp.mean(values, axis=1, keepdims=True)
    spread = jnp.mean(values * values, axis=1, keepdims=True) - center * center
    inverse_deviation = lax.rsqrt(spread + EPSILON)
    return ((values - center) * inverse_deviation, inverse_deviation)


def layer_norm_backward(normalized_gradient, centered_scaled, inverse_deviation, norm_gain):
    scaled_output = normalized_gradient * norm_gain.astype(jnp.float32)
    plain_output = jnp.mean(scaled_output, axis=1, keepdims=True)
    cross_term = jnp.mean(scaled_output * centered_scaled, axis=1, keepdims=True)
    return inverse_deviation * (scaled_output - plain_output - centered_scaled * cross_term)


def image_forward(blocks):
    query_img, key_img, value_img = blocks
    scale = DH ** (-0.5)
    query_heads = split_heads(query_img)
    key_heads = split_heads(key_img)
    value_heads = split_heads(value_img)
    scores = (
        jnp.einsum("qhd,khd->hqk", query_heads, key_heads, preferred_element_type=jnp.float32)
        * scale
    )
    top_score = jnp.max(scores, axis=-1, keepdims=True)
    weights = jnp.exp(scores - top_score)
    total = jnp.sum(weights, axis=-1, keepdims=True)
    probs = (weights / total).astype(jnp.bfloat16)
    mixed = jnp.einsum("hqk,khd->qhd", probs, value_heads, preferred_element_type=jnp.float32)
    log_total = top_score[..., 0] + jnp.log(total[..., 0])
    return (mixed.reshape(query_img.shape).astype(jnp.bfloat16), log_total)


def image_backward(blocks):
    query_img, key_img, value_img, grad_img, log_total = blocks
    scale = DH ** (-0.5)
    query_heads = split_heads(query_img)
    key_heads = split_heads(key_img)
    value_heads = split_heads(value_img)
    grad_heads = split_heads(grad_img)
    scores = (
        jnp.einsum("qhd,khd->hqk", query_heads, key_heads, preferred_element_type=jnp.float32)
        * scale
    )
    probs = jnp.exp(scores - log_total[..., None])
    probs_low = probs.astype(jnp.bfloat16)
    grad_probs = jnp.einsum(
        "qhd,khd->hqk", grad_heads, value_heads, preferred_element_type=jnp.float32
    )
    grad_value = jnp.einsum(
        "hqk,qhd->khd", probs_low, grad_heads, preferred_element_type=jnp.float32
    )
    inner = jnp.sum(probs * grad_probs, axis=-1, keepdims=True)
    grad_scores = (probs * (grad_probs - inner)).astype(jnp.bfloat16)
    grad_query = (
        jnp.einsum("hqk,khd->qhd", grad_scores, key_heads, preferred_element_type=jnp.float32)
        * scale
    )
    grad_key = (
        jnp.einsum("hqk,qhd->khd", grad_scores, query_heads, preferred_element_type=jnp.float32)
        * scale
    )
    shape_img = query_img.shape
    return (
        grad_query.reshape(shape_img).astype(jnp.bfloat16),
        grad_key.reshape(shape_img).astype(jnp.bfloat16),
        grad_value.reshape(shape_img).astype(jnp.bfloat16),
    )


def by_image(values, images):
    return values.reshape(images, values.shape[0] // images, values.shape[1])


def on_device_general(
    inputs,
    valid,
    cotangent,
    w_query,
    w_key,
    w_value,
    b_query,
    b_value,
    w_attn_out,
    b_attn_out,
    w_mlp_in,
    b_mlp_in,
    w_mlp_out,
    b_mlp_out,
    attention_norm_gain,
    attention_norm_shift,
    feedforward_norm_gain,
    feedforward_norm_shift,
):
    row_count, width = inputs.shape
    images = valid.shape[0]
    group_rows = images * SEQ
    parts = lax.axis_size("feat")
    extra = row_count * parts - group_rows
    width_local = w_query.shape[0]
    hidden_local = w_mlp_out.shape[0]
    global_rows = lax.axis_index("feat") * row_count + jnp.arange(row_count, dtype=jnp.int32)
    owner = global_rows // SEQ
    matches = (owner[:, None] == jnp.arange(images, dtype=jnp.int32)[None, :]).astype(jnp.float32)
    row_mask = jnp.sum(matches * valid.astype(jnp.float32)[None, :], axis=1)
    live = (global_rows < group_rows).astype(jnp.float32)[:, None]

    def padded(values):
        return jnp.pad(values, ((0, extra), (0, 0)))

    local_input_rows = inputs.astype(jnp.float32)
    first_centered_scaled, first_inverse_deviation = apply_layer_norm(local_input_rows)
    normalized_first = (
        first_centered_scaled * attention_norm_gain.astype(jnp.float32)
        + attention_norm_shift.astype(jnp.float32)
    ).astype(jnp.bfloat16)
    normed_full = lax.all_gather(normalized_first, "feat", axis=0, tiled=True)[:group_rows]
    w_qkv = jnp.concatenate([w_query, w_key, w_value], axis=0)
    projected = jnp.einsum("rd,cd->rc", normed_full, w_qkv, preferred_element_type=jnp.float32)
    queries = (projected[:, :width_local] + b_query.astype(jnp.float32)).astype(jnp.bfloat16)
    key_rows = projected[:, width_local : 2 * width_local].astype(jnp.bfloat16)
    value_rows = (projected[:, 2 * width_local :] + b_value.astype(jnp.float32)).astype(
        jnp.bfloat16
    )
    mixed, log_totals = lax.map(
        image_forward,
        (by_image(queries, images), by_image(key_rows, images), by_image(value_rows, images)),
    )
    mixed = mixed.reshape(group_rows, width_local)
    partial_out = jnp.dot(mixed, w_attn_out, preferred_element_type=jnp.float32)
    attn = lax.psum_scatter(
        padded(partial_out), "feat", scatter_dimension=0, tiled=True
    ) + b_attn_out.astype(jnp.float32)
    middle_state = local_input_rows + attn
    second_centered_scaled, second_inverse_deviation = apply_layer_norm(middle_state)
    normalized_middle = (
        second_centered_scaled * feedforward_norm_gain.astype(jnp.float32)
        + feedforward_norm_shift.astype(jnp.float32)
    ).astype(jnp.bfloat16)
    mid_full = lax.all_gather(normalized_middle, "feat", axis=0, tiled=True)[:group_rows]
    hidden = jnp.dot(mid_full, w_mlp_in, preferred_element_type=jnp.float32) + b_mlp_in.astype(
        jnp.float32
    )
    active = (hidden * jax.nn.sigmoid(SLOPE * hidden)).astype(jnp.bfloat16)
    partial_mlp = jnp.dot(active, w_mlp_out, preferred_element_type=jnp.float32)
    branch = lax.psum_scatter(
        padded(partial_mlp).astype(jnp.bfloat16), "feat", scatter_dimension=0, tiled=True
    ).astype(jnp.float32) + b_mlp_out.astype(jnp.float32)
    output = (middle_state + branch) * live
    output_gradient = cotangent.astype(jnp.float32) * row_mask[:, None]
    grad_branch = output_gradient.astype(jnp.bfloat16)
    grad_b_mlp_out = column_sums(grad_branch)
    branch_full = lax.all_gather(grad_branch, "feat", axis=0, tiled=True)[:group_rows]
    grad_w_mlp_out = jnp.einsum(
        "rf,rd->fd", active, branch_full, preferred_element_type=jnp.float32
    )
    grad_active = jnp.einsum(
        "rd,fd->rf", branch_full, w_mlp_out, preferred_element_type=jnp.float32
    )
    grad_hidden = (grad_active * gelu_slope(hidden)).astype(jnp.bfloat16)
    grad_b_mlp_in = column_sums(grad_hidden)
    grad_mlp_in_rows = jnp.einsum(
        "rf,rd->fd", grad_hidden, mid_full, preferred_element_type=jnp.float32
    )
    partial_mid = jnp.einsum("rf,df->rd", grad_hidden, w_mlp_in, preferred_element_type=jnp.float32)
    midpoint_gradient = lax.psum_scatter(
        padded(partial_mid), "feat", scatter_dimension=0, tiled=True
    )
    feedforward_gain_gradient = jnp.sum(midpoint_gradient * second_centered_scaled, axis=0)
    grad_s_mlp = jnp.sum(midpoint_gradient, axis=0)
    middle_state_gradient = output_gradient + layer_norm_backward(
        midpoint_gradient, second_centered_scaled, second_inverse_deviation, feedforward_norm_gain
    )
    grad_attn = middle_state_gradient.astype(jnp.bfloat16)
    grad_b_attn_out = column_sums(grad_attn)
    attn_full = lax.all_gather(grad_attn, "feat", axis=0, tiled=True)[:group_rows]
    grad_w_attn_out = jnp.einsum("rh,rd->hd", mixed, attn_full, preferred_element_type=jnp.float32)
    grad_mixed = jnp.einsum(
        "rd,hd->rh", attn_full, w_attn_out, preferred_element_type=jnp.float32
    ).astype(jnp.bfloat16)
    grad_query, grad_key, grad_value = lax.map(
        image_backward,
        (
            by_image(queries, images),
            by_image(key_rows, images),
            by_image(value_rows, images),
            by_image(grad_mixed, images),
            log_totals,
        ),
    )
    grad_query = grad_query.reshape(group_rows, width_local)
    grad_key = grad_key.reshape(group_rows, width_local)
    grad_value = grad_value.reshape(group_rows, width_local)
    grad_b_query = column_sums(grad_query)
    grad_b_value = column_sums(grad_value)
    grad_qkv = jnp.concatenate([grad_query, grad_key, grad_value], axis=1)
    grad_w_qkv = jnp.einsum("rc,rd->cd", grad_qkv, normed_full, preferred_element_type=jnp.float32)
    partial_in = jnp.einsum("rc,cd->rd", grad_qkv, w_qkv, preferred_element_type=jnp.float32)
    normalized_gradient = lax.psum_scatter(
        padded(partial_in).astype(jnp.bfloat16), "feat", scatter_dimension=0, tiled=True
    ).astype(jnp.float32)
    attention_gain_gradient = jnp.sum(normalized_gradient * first_centered_scaled, axis=0)
    grad_s_attn = jnp.sum(normalized_gradient, axis=0)
    layer_input_gradient = middle_state_gradient + layer_norm_backward(
        normalized_gradient, first_centered_scaled, first_inverse_deviation, attention_norm_gain
    )
    local_powers = jnp.stack(
        [
            jnp.sum(row_mask[:, None] * local_input_rows * local_input_rows),
            jnp.sum(row_mask[:, None] * attn * attn),
            jnp.sum(row_mask[:, None] * branch * branch),
            jnp.sum(row_mask[:, None] * output * output),
        ]
    )
    local_count = jnp.sum(row_mask)
    bias_entries = jnp.concatenate([grad_b_query, grad_b_value, grad_b_mlp_in])
    bias_row = jnp.pad(bias_entries, (0, width - bias_entries.shape[0]))[None, :]
    packed = jnp.concatenate(
        [grad_w_qkv, grad_w_attn_out, grad_mlp_in_rows, grad_w_mlp_out, bias_row], axis=0
    )
    packed_rows = packed.shape[0]
    tok_parts = lax.axis_size("tok")
    fill_rows = (tok_parts - packed_rows % tok_parts) % tok_parts
    packed = jnp.pad(packed, ((0, fill_rows), (0, 0)))
    shares = lax.psum_scatter(
        packed.astype(jnp.bfloat16), "tok", scatter_dimension=0, tiled=True
    ).astype(jnp.float32)
    summed = lax.all_gather(shares.astype(jnp.bfloat16), "tok", axis=0, tiled=True).astype(
        shares.dtype
    )[:packed_rows]
    offset = 0
    grad_w_query = summed[offset : offset + width_local]
    offset += width_local
    grad_w_key = summed[offset : offset + width_local]
    offset += width_local
    grad_w_value = summed[offset : offset + width_local]
    offset += width_local
    grad_w_attn_out = summed[offset : offset + width_local]
    offset += width_local
    grad_w_mlp_in = summed[offset : offset + hidden_local].T
    offset += hidden_local
    grad_w_mlp_out = summed[offset : offset + hidden_local]
    offset += hidden_local
    bias_sums = summed[offset]
    grad_b_query = bias_sums[:width_local]
    grad_b_value = bias_sums[width_local : 2 * width_local]
    grad_b_mlp_in = bias_sums[2 * width_local : 2 * width_local + hidden_local]
    (
        grad_b_attn_out,
        grad_b_mlp_out,
        attention_gain_gradient,
        grad_s_attn,
        feedforward_gain_gradient,
        grad_s_mlp,
        powers,
        counted,
    ) = lax.psum(
        (
            grad_b_attn_out,
            grad_b_mlp_out,
            attention_gain_gradient,
            grad_s_attn,
            feedforward_gain_gradient,
            grad_s_mlp,
            local_powers,
            local_count,
        ),
        ("tok", "feat"),
    )
    stream_rms = jnp.sqrt(powers / (jnp.maximum(counted, 1.0) * D))
    return (
        output,
        layer_input_gradient,
        grad_w_query,
        grad_w_key,
        grad_w_value,
        grad_b_query,
        grad_b_value,
        grad_w_attn_out,
        grad_b_attn_out,
        grad_w_mlp_in,
        grad_b_mlp_in,
        grad_w_mlp_out,
        grad_b_mlp_out,
        attention_gain_gradient,
        grad_s_attn,
        feedforward_gain_gradient,
        grad_s_mlp,
        stream_rms,
    )


BF16 = jnp.bfloat16
F32 = jnp.float32
AXES = ("tok", "feat")
SLOTS = (0, 1, 3, 2)
PAIRS = ((0, 1), (3, 2))
VMEM_BYTES = 48 * 1024 * 1024


def route(move):
    found = []
    for tok in range(4):
        for feat in range(8):
            target = move(tok // 2, tok % 2, feat // 2, feat % 2)
            if target is not None:
                x, c, z, y = target
                found.append((tok * 8 + feat, (2 * x + c) * 8 + 2 * z + y))
    return found


SWAP_X = route(lambda x, c, z, y: (1 - x, c, z, y))
SWAP_C = route(lambda x, c, z, y: (x, 1 - c, z, y))
SWAP_Y = route(lambda x, c, z, y: (x, c, z, 1 - y))
SHIFT_Z = [route(lambda x, c, z, y, s=s: (x, c, (z + s) % 4, y)) for s in range(4)]
FLIP_Z = [route(lambda x, c, z, y, s=s: (x, c, z ^ s, y)) for s in range(4)]
NEXT = [(t * 8 + f, t * 8 + f + 1) for t in range(4) for f in range(7)]
PREVIOUS = [(t * 8 + f + 1, t * 8 + f) for t in range(4) for f in range(7)]


def send(values, pairs):
    return lax.ppermute(values, AXES, pairs)


def nt(left, right):
    return lax.dot_general(left, right, (((1,), (1,)), ((), ())), preferred_element_type=F32)


def nn(left, right):
    return lax.dot_general(left, right, (((1,), (0,)), ((), ())), preferred_element_type=F32)


def tn(left, right):
    return lax.dot_general(left, right, (((0,), (0,)), ((), ())), preferred_element_type=F32)


def forward_kernel(half, limits_ref, qkv_ref, mixed_ref, probs_ref):
    rows = 2 * half
    key_index = lax.broadcasted_iota(jnp.int32, (rows, 1), 0)
    first, second = limits_ref[0], limits_ref[1]
    real = (key_index < first) | ((key_index >= half) & (key_index < half + second))
    penalty = jnp.where(real, 0.0, -1e30)
    outs = []
    for h in range(2):
        q = qkv_ref[:, h * DH : (h + 1) * DH] * jnp.asarray(DH ** (-0.5), BF16)
        k = qkv_ref[:, 2 * DH + h * DH : 2 * DH + (h + 1) * DH]
        v = qkv_ref[:, 4 * DH + h * DH : 4 * DH + (h + 1) * DH]
        scores = nt(k, q) + penalty
        top = jnp.max(scores, axis=0, keepdims=True)
        weights = jnp.exp(scores - top)
        total = jnp.sum(weights, axis=0, keepdims=True)
        probs = (weights * (1.0 / total)).astype(BF16)
        probs_ref[0, h] = probs
        outs.append(tn(v, probs))
    mixed_ref[...] = jnp.concatenate(outs, axis=0).T.astype(BF16)


def backward_kernel(qkv_ref, probs_ref, grad_ref, out_ref, sums_ref):
    scale = jnp.asarray(DH ** (-0.5), BF16)
    dq, dk, dv = [], [], []
    for h in range(2):
        q = qkv_ref[:, h * DH : (h + 1) * DH] * scale
        k = qkv_ref[:, 2 * DH + h * DH : 2 * DH + (h + 1) * DH] * scale
        v = qkv_ref[:, 4 * DH + h * DH : 4 * DH + (h + 1) * DH]
        g = grad_ref[:, h * DH : (h + 1) * DH]
        probs = probs_ref[0, h]
        grad_probs = nt(v, g)
        wide = probs.astype(F32)
        inner = jnp.sum(wide * grad_probs, axis=0, keepdims=True)
        grad_scores = (wide * (grad_probs - inner)).astype(BF16)
        dv.append(nn(probs, g))
        dk.append(nn(grad_scores, q))
        dq.append(tn(k, grad_scores))
    query = jnp.concatenate(dq, axis=0).T.astype(BF16)
    value = jnp.concatenate(dv, axis=1).astype(BF16)
    out_ref[:, : 2 * DH] = query
    out_ref[:, 2 * DH : 4 * DH] = jnp.concatenate(dk, axis=1).astype(BF16)
    out_ref[:, 4 * DH :] = value
    query_sum = jnp.sum(query.astype(F32), axis=0, keepdims=True)
    value_sum = jnp.sum(value.astype(F32), axis=0, keepdims=True)
    sums_ref[0] = jnp.concatenate([query_sum, value_sum, jnp.zeros((6, 2 * DH), F32)], axis=0)


def attention_forward(limits, qkv, half):
    rows = 2 * half
    count = qkv.shape[0] // rows
    return pl.pallas_call(
        functools.partial(forward_kernel, half),
        grid=(count,),
        in_specs=[
            pl.BlockSpec(memory_space=pltpu.SMEM),
            pl.BlockSpec((rows, 6 * DH), lambda i: (i, 0)),
        ],
        out_specs=[
            pl.BlockSpec((rows, 2 * DH), lambda i: (i, 0)),
            pl.BlockSpec((1, 2, rows, rows), lambda i: (i, 0, 0, 0)),
        ],
        out_shape=[
            jax.ShapeDtypeStruct((count * rows, 2 * DH), BF16),
            jax.ShapeDtypeStruct((count, 2, rows, rows), BF16),
        ],
        compiler_params=pltpu.CompilerParams(vmem_limit_bytes=VMEM_BYTES),
        cost_estimate=pl.CostEstimate(
            flops=count * 8 * rows * rows * DH,
            bytes_accessed=count * rows * (rows * 4 + 16 * DH),
            transcendentals=count * 2 * rows * rows,
        ),
    )(limits, qkv)


def attention_backward(qkv, probs, grad, half):
    rows = 2 * half
    count = qkv.shape[0] // rows
    return pl.pallas_call(
        backward_kernel,
        grid=(count,),
        in_specs=[
            pl.BlockSpec((rows, 6 * DH), lambda i: (i, 0)),
            pl.BlockSpec((1, 2, rows, rows), lambda i: (i, 0, 0, 0)),
            pl.BlockSpec((rows, 2 * DH), lambda i: (i, 0)),
        ],
        out_specs=[
            pl.BlockSpec((rows, 6 * DH), lambda i: (i, 0)),
            pl.BlockSpec((1, 8, 2 * DH), lambda i: (i, 0, 0)),
        ],
        out_shape=[
            jax.ShapeDtypeStruct((count * rows, 6 * DH), BF16),
            jax.ShapeDtypeStruct((count, 8, 2 * DH), F32),
        ],
        compiler_params=pltpu.CompilerParams(vmem_limit_bytes=VMEM_BYTES),
        cost_estimate=pl.CostEstimate(
            flops=count * 16 * rows * rows * DH,
            bytes_accessed=count * rows * (rows * 4 + 28 * DH),
            transcendentals=0,
        ),
    )(qkv, probs, grad)


def gather_rows(values):
    across = send(values, SWAP_Y)
    return jnp.concatenate([values, across, send(values, SWAP_C), send(across, SWAP_C)], axis=0)


def scatter_rows(product, half):
    other = product(2 * half, 4 * half).astype(BF16)
    from_core = send(other, SWAP_C)
    far = (product(half, 2 * half) + from_core[half:].astype(F32)).astype(BF16)
    from_y = send(far, SWAP_Y)
    near = product(0, half) + from_core[:half].astype(F32)
    return near + from_y.astype(F32)


def in_order(flag, own, other, axis):
    first = jnp.where(flag == 0, own, other)
    second = jnp.where(flag == 0, other, own)
    return jnp.stack([first, second], axis=axis)


def on_device(
    inputs,
    valid,
    cotangent,
    w_query,
    w_key,
    w_value,
    b_query,
    b_value,
    w_attn_out,
    b_attn_out,
    w_mlp_in,
    b_mlp_in,
    w_mlp_out,
    b_mlp_out,
    attention_norm_gain,
    attention_norm_shift,
    feedforward_norm_gain,
    feedforward_norm_shift,
):
    rows, width = inputs.shape
    images = valid.shape[0]
    heads_local = w_query.shape[0] // DH
    hidden_local = w_mlp_out.shape[0]
    shape = (lax.axis_size("tok"), lax.axis_size("feat"), images, heads_local)
    if shape != (4, 8, 4, 2) or 2 * rows != SEQ + 1 or hidden_local % 512 or width % 128:
        return on_device_general(
            inputs,
            valid,
            cotangent,
            w_query,
            w_key,
            w_value,
            b_query,
            b_value,
            w_attn_out,
            b_attn_out,
            w_mlp_in,
            b_mlp_in,
            w_mlp_out,
            b_mlp_out,
            attention_norm_gain,
            attention_norm_shift,
            feedforward_norm_gain,
            feedforward_norm_shift,
        )
    tok, feat = lax.axis_index("tok"), lax.axis_index("feat")
    x, c, z, y = tok // 2, tok % 2, feat // 2, feat % 2
    half = (rows + 15) // 16 * 16
    quarter = hidden_local // 4
    part = DH // 2

    def cut(values, start, size):
        return lax.dynamic_slice_in_dim(values, start, size, 0)

    def attention_piece(side):
        at = c * DH + side * part
        bias = jnp.concatenate(
            [
                cut(b_query, at, part),
                cut(b_value, at, part),
                cut(b_mlp_in, (2 * c + side) * quarter, quarter),
            ]
        )
        bias = jnp.pad(bias[None, :], ((0, 7), (0, width - bias.shape[0])))
        return jnp.concatenate(
            [cut(w, at, part) for w in (w_query, w_key, w_value, w_attn_out)] + [bias], axis=0
        )

    attn_own = {0: attention_piece(x)}
    attn_other = {0: attention_piece(1 - x)}
    for s in (1, 3, 2):
        attn_own[s] = send(attn_own[0], SHIFT_Z[s])

    edge = send(jnp.concatenate([inputs[rows - 4 :], cotangent[rows - 4 :]], axis=0), NEXT)
    count = rows - y
    present = lax.broadcasted_iota(jnp.int32, (half, 1), 0) < count

    def aligned(values, before):
        ext = jnp.concatenate([before, values, jnp.zeros((half - rows, width), BF16)], axis=0)
        return jnp.where(present, lax.dynamic_slice_in_dim(ext, 4 - z, half, 0), 0)

    stream = aligned(inputs, edge[:4]).astype(F32)
    first_hat, first_inverse = apply_layer_norm(stream)
    normed = (
        first_hat * attention_norm_gain.astype(F32) + attention_norm_shift.astype(F32)
    ).astype(BF16)
    normed_all = gather_rows(normed)
    flag = lax.dynamic_index_in_dim(valid, z, 0, keepdims=False).astype(F32)
    grad_branch = (aligned(cotangent, edge[4:]).astype(F32) * flag).astype(BF16)
    output_gradient = grad_branch.astype(F32)

    both = send(jnp.stack([attn_own[1], attn_own[3]]), SWAP_X)
    attn_other[1], attn_other[3] = both[0], both[1]
    attn_other[2] = send(attn_own[2], SWAP_X)

    hidden_half = lax.dynamic_slice_in_dim(w_mlp_in, 2 * c * quarter, 2 * quarter, 1).T
    out_half = cut(w_mlp_out, 2 * c * quarter, 2 * quarter)

    def mlp_piece(side):
        return jnp.concatenate(
            [cut(hidden_half, side * quarter, quarter), cut(out_half, side * quarter, quarter)],
            axis=0,
        )

    mlp_own = {0: mlp_piece(x)}
    mlp_other = {0: mlp_piece(1 - x)}
    for s in (1, 3, 2):
        mlp_own[s] = send(mlp_own[0], SHIFT_Z[s])
    both = send(jnp.stack([mlp_own[1], mlp_own[3]]), SWAP_X)
    mlp_other[1], mlp_other[3] = both[0], both[1]
    mlp_other[2] = send(mlp_own[2], SWAP_X)

    def attention_rows(matrix, slots):
        at = slice(matrix * part, (matrix + 1) * part)
        return [side[s][at] for s in slots for side in (attn_own, attn_other)]

    def bias_of(first, size, slots, sides=(0, 1)):
        taken = []
        for s in slots:
            for side in (attn_own, attn_other):
                taken.append(side[s][4 * part, first : first + size])
        return taken

    limits = jnp.stack([rows - y, rows - 1 + y]).astype(jnp.int32)
    w_pairs, qkv_pairs, mixed_pairs, prob_pairs = [], [], [], []
    for slots in PAIRS:
        w_pair = jnp.concatenate([r for m in range(3) for r in attention_rows(m, slots)], axis=0)
        bias = jnp.concatenate(
            bias_of(0, part, slots)
            + [jnp.zeros((2 * DH,), BF16)]
            + bias_of(part, part, slots)
        )
        qkv = (nt(normed_all, w_pair) + bias.astype(F32)).astype(BF16)
        mixed, probs = attention_forward(limits, qkv, half)
        w_pairs.append(w_pair)
        qkv_pairs.append(qkv)
        mixed_pairs.append(mixed)
        prob_pairs.append(probs)
    w_out = jnp.concatenate(attention_rows(3, SLOTS), axis=0)
    mixed = jnp.concatenate(mixed_pairs, axis=1)
    attn = scatter_rows(lambda lo, hi: nn(mixed[lo:hi], w_out), half) + b_attn_out.astype(F32)

    middle = stream + attn
    second_hat, second_inverse = apply_layer_norm(middle)
    normed_middle = (
        second_hat * feedforward_norm_gain.astype(F32) + feedforward_norm_shift.astype(F32)
    ).astype(BF16)
    middle_all = gather_rows(normed_middle)
    branch_all = gather_rows(grad_branch)

    w_in = jnp.concatenate([side[s][:quarter] for side in (mlp_own, mlp_other) for s in SLOTS])
    w_mid = jnp.concatenate([side[s][quarter:] for side in (mlp_own, mlp_other) for s in SLOTS])
    bias_in = jnp.concatenate(
        [
            side[s][4 * part, 2 * part : 2 * part + quarter]
            for side in (attn_own, attn_other)
            for s in SLOTS
        ]
    )
    hidden = nt(middle_all, w_in) + bias_in.astype(F32)
    active = (hidden * jax.nn.sigmoid(SLOPE * hidden)).astype(BF16)
    grad_active = nt(branch_all, w_mid)
    grad_hidden = (grad_active * gelu_slope(hidden)).astype(BF16)
    midpoint_gradient = scatter_rows(lambda lo, hi: nn(grad_hidden[lo:hi], w_in), half)
    grad_b_mlp_in = column_sums(grad_hidden)

    halves = hidden_local

    def exchange(left, right):
        other = tn(left[:, halves:], right).astype(BF16)
        received = send(other, SWAP_X)
        return (tn(left[:, :halves], right) + received.astype(F32)).astype(BF16)

    grad_out_half = exchange(active, branch_all)
    grad_in_half = exchange(grad_hidden, middle_all)

    def to_owner(pieces):
        total = pieces[0].astype(F32)
        for s in (1, 3, 2):
            total = total + send(pieces[s], SHIFT_Z[4 - s]).astype(F32)
        return total.astype(BF16)

    mlp_sum = to_owner(
        {
            s: jnp.concatenate(
                [g[i * quarter : (i + 1) * quarter] for g in (grad_in_half, grad_out_half)], axis=0
            )
            for i, s in enumerate(SLOTS)
        }
    ).reshape(2, quarter, width)
    mlp_sum = in_order(x, mlp_sum, send(mlp_sum, SWAP_X), 1)
    mlp_sum = in_order(c, mlp_sum, send(mlp_sum, SWAP_C), 1)
    mlp_sum = mlp_sum.reshape(2, hidden_local, width).astype(F32)

    branch = scatter_rows(lambda lo, hi: nn(active[lo:hi], w_mid), half) + b_mlp_out.astype(F32)
    output = middle + branch

    feedforward_gain_gradient = jnp.sum(midpoint_gradient * second_hat, axis=0)
    grad_s_mlp = jnp.sum(midpoint_gradient, axis=0)
    middle_gradient = output_gradient + layer_norm_backward(
        midpoint_gradient, second_hat, second_inverse, feedforward_norm_gain
    )
    grad_attn = middle_gradient.astype(BF16)
    attn_all = gather_rows(grad_attn)
    grad_mixed = nt(attn_all, w_out).astype(BF16)
    grad_w_out = tn(mixed, attn_all).reshape(2, 2, 2, part, width)

    attn_pieces, sum_pairs, grad_pairs = {}, [None, None], [None, None]
    for p in (1, 0):
        grad_qkv, sums = attention_backward(
            qkv_pairs[p], prob_pairs[p], grad_mixed[:, p * 2 * DH : (p + 1) * 2 * DH], half
        )
        grad_pairs[p] = grad_qkv
        sum_pairs[p] = jnp.sum(sums, axis=0)
        grad_w = tn(grad_qkv, normed_all).reshape(3, 2, 2, part, width)
        grad_w = jnp.concatenate([grad_w, grad_w_out[p][None]], axis=0)
        received = send(grad_w[:, :, 1].astype(BF16), SWAP_X)
        summed = (grad_w[:, :, 0] + received.astype(F32)).astype(BF16)
        for i, s in enumerate(PAIRS[p]):
            attn_pieces[s] = summed[:, i]
    grad_all = jnp.concatenate(grad_pairs, axis=1)
    w_all = jnp.concatenate(w_pairs, axis=0)
    normed_gradient = scatter_rows(lambda lo, hi: nn(grad_all[lo:hi], w_all), half)
    attention_gain_gradient = jnp.sum(normed_gradient * first_hat, axis=0)
    grad_s_attn = jnp.sum(normed_gradient, axis=0)
    layer_input_gradient = middle_gradient + layer_norm_backward(
        normed_gradient, first_hat, first_inverse, attention_norm_gain
    )
    attn_sum = to_owner(attn_pieces)
    attn_sum = in_order(x, attn_sum, send(attn_sum, SWAP_X), 1)
    attn_sum = in_order(c, attn_sum, send(attn_sum, SWAP_C), 1)
    attn_sum = attn_sum.reshape(4, 2 * DH, width).astype(F32)

    heads = send(jnp.concatenate([output[:4], layer_input_gradient[:4]], axis=0), PREVIOUS)

    def own_rows(values, after):
        ext = lax.dynamic_update_slice_in_dim(values, after, count, 0)
        return lax.dynamic_slice_in_dim(ext, z, rows, 0)

    output_rows = own_rows(output, heads[:4])
    gradient_rows = own_rows(layer_input_gradient, heads[4:])

    mask = jnp.where(present, flag, 0.0)
    powers = [jnp.sum(mask * v * v) for v in (stream, attn, branch, output)]
    powers = jnp.stack(powers + [flag * count.astype(F32)])
    slot_of = jnp.asarray(SLOTS, jnp.int32)
    four = jnp.arange(4, dtype=jnp.int32)
    two = jnp.arange(2, dtype=jnp.int32)
    by_z = (four[:, None] == (z - slot_of[None, :]) % 4).astype(F32)
    by_x = (two[:, None] == (two[None, :] + x) % 2).astype(F32)
    place = ((two[:, None] == y) & (two[None, :] == c)).astype(F32)

    def spread(values):
        found = jnp.sum(
            by_z[:, None, :, None, None] * by_x[None, :, None, :, None] * values[None, None],
            axis=(2, 3),
        )
        found = place[None, :, :, None, None] * found[:, None, None]
        return found.reshape(-1, width)

    def slot_sums(row):
        return jnp.concatenate([s[row].reshape(2, 2, part) for s in sum_pairs], axis=0)

    hidden_sums = grad_b_mlp_in.reshape(2, 4, quarter).transpose(1, 0, 2)
    small = jnp.concatenate(
        [
            jnp.stack(
                [
                    column_sums(grad_attn),
                    column_sums(grad_branch),
                    attention_gain_gradient,
                    grad_s_attn,
                    feedforward_gain_gradient,
                    grad_s_mlp,
                    jnp.pad(powers, (0, width - 5)),
                ]
            ),
            spread(slot_sums(0)),
            spread(slot_sums(1)),
            spread(hidden_sums),
        ],
        axis=0,
    )
    for pairs in (SWAP_C, SWAP_X, SWAP_Y, FLIP_Z[1], FLIP_Z[2]):
        small = small + send(small, pairs)
    stream_rms = jnp.sqrt(small[6, :4] / (jnp.maximum(small[6, 4], 1.0) * D))
    grad_b_query = cut(small[7], feat * heads_local * DH, heads_local * DH)
    grad_b_value = cut(small[8], feat * heads_local * DH, heads_local * DH)
    grad_b_mlp_in = cut(small[9:].reshape(-1), feat * hidden_local, hidden_local)
    return (
        output_rows,
        gradient_rows,
        attn_sum[0],
        attn_sum[1],
        attn_sum[2],
        grad_b_query,
        grad_b_value,
        attn_sum[3],
        small[0],
        mlp_sum[0].T,
        grad_b_mlp_in,
        mlp_sum[1],
        small[1],
        small[2],
        small[3],
        small[4],
        small[5],
        stream_rms,
    )


def solution(mesh):
    in_specs = (
        P(("tok", "feat"), None),
        P("tok"),
        P(("tok", "feat"), None),
        P("feat", None),
        P("feat", None),
        P("feat", None),
        P("feat"),
        P("feat"),
        P("feat", None),
        P(),
        P(None, "feat"),
        P("feat"),
        P("feat", None),
        P(),
        P(),
        P(),
        P(),
        P(),
    )
    out_specs = (
        P(("tok", "feat"), None),
        P(("tok", "feat"), None),
        P("feat", None),
        P("feat", None),
        P("feat", None),
        P("feat"),
        P("feat"),
        P("feat", None),
        P(),
        P(None, "feat"),
        P("feat"),
        P("feat", None),
        P(),
        P(),
        P(),
        P(),
        P(),
        P(),
    )
    return jax.shard_map(
        on_device, mesh=mesh, in_specs=in_specs, out_specs=out_specs, check_vma=False
    )
```

```python
import functools

import jax
import jax.numpy as jnp
from jax import lax
from jax.experimental import pallas as pl
from jax.experimental.pallas import tpu as pltpu
from jax.sharding import PartitionSpec as P

D = 1024
DH = 64
SEQ = 577


EPSILON = 1e-05
SLOPE = 1.702


def gelu_slope(values):
    sigmoid = jax.nn.sigmoid(SLOPE * values)
    return sigmoid + SLOPE * values * sigmoid * (1.0 - sigmoid)


def column_sums(values):
    return jnp.sum(values.astype(jnp.float32), axis=0)


def split_heads(values):
    return values.reshape(values.shape[0], values.shape[1] // DH, DH)


def apply_layer_norm(values):
    center = jnp.mean(values, axis=1, keepdims=True)
    spread = jnp.mean(values * values, axis=1, keepdims=True) - center * center
    inverse_deviation = lax.rsqrt(spread + EPSILON)
    return ((values - center) * inverse_deviation, inverse_deviation)


def layer_norm_backward(normalized_gradient, centered_scaled, inverse_deviation, norm_gain):
    scaled_output = normalized_gradient * norm_gain.astype(jnp.float32)
    plain_output = jnp.mean(scaled_output, axis=1, keepdims=True)
    cross_term = jnp.mean(scaled_output * centered_scaled, axis=1, keepdims=True)
    return inverse_deviation * (scaled_output - plain_output - centered_scaled * cross_term)


def image_forward(blocks):
    query_img, key_img, value_img = blocks
    scale = DH ** (-0.5)
    query_heads = split_heads(query_img)
    key_heads = split_heads(key_img)
    value_heads = split_heads(value_img)
    scores = (
        jnp.einsum("qhd,khd->hqk", query_heads, key_heads, preferred_element_type=jnp.float32)
        * scale
    )
    top_score = jnp.max(scores, axis=-1, keepdims=True)
    weights = jnp.exp(scores - top_score)
    total = jnp.sum(weights, axis=-1, keepdims=True)
    probs = (weights / total).astype(jnp.bfloat16)
    mixed = jnp.einsum("hqk,khd->qhd", probs, value_heads, preferred_element_type=jnp.float32)
    log_total = top_score[..., 0] + jnp.log(total[..., 0])
    return (mixed.reshape(query_img.shape).astype(jnp.bfloat16), log_total)


def image_backward(blocks):
    query_img, key_img, value_img, grad_img, log_total = blocks
    scale = DH ** (-0.5)
    query_heads = split_heads(query_img)
    key_heads = split_heads(key_img)
    value_heads = split_heads(value_img)
    grad_heads = split_heads(grad_img)
    scores = (
        jnp.einsum("qhd,khd->hqk", query_heads, key_heads, preferred_element_type=jnp.float32)
        * scale
    )
    probs = jnp.exp(scores - log_total[..., None])
    probs_low = probs.astype(jnp.bfloat16)
    grad_probs = jnp.einsum(
        "qhd,khd->hqk", grad_heads, value_heads, preferred_element_type=jnp.float32
    )
    grad_value = jnp.einsum(
        "hqk,qhd->khd", probs_low, grad_heads, preferred_element_type=jnp.float32
    )
    inner = jnp.sum(probs * grad_probs, axis=-1, keepdims=True)
    grad_scores = (probs * (grad_probs - inner)).astype(jnp.bfloat16)
    grad_query = (
        jnp.einsum("hqk,khd->qhd", grad_scores, key_heads, preferred_element_type=jnp.float32)
        * scale
    )
    grad_key = (
        jnp.einsum("hqk,qhd->khd", grad_scores, query_heads, preferred_element_type=jnp.float32)
        * scale
    )
    shape_img = query_img.shape
    return (
        grad_query.reshape(shape_img).astype(jnp.bfloat16),
        grad_key.reshape(shape_img).astype(jnp.bfloat16),
        grad_value.reshape(shape_img).astype(jnp.bfloat16),
    )


def by_image(values, images):
    return values.reshape(images, values.shape[0] // images, values.shape[1])


def on_device_general(
    inputs,
    valid,
    cotangent,
    w_query,
    w_key,
    w_value,
    b_query,
    b_value,
    w_attn_out,
    b_attn_out,
    w_mlp_in,
    b_mlp_in,
    w_mlp_out,
    b_mlp_out,
    attention_norm_gain,
    attention_norm_shift,
    feedforward_norm_gain,
    feedforward_norm_shift,
):
    row_count, width = inputs.shape
    images = valid.shape[0]
    group_rows = images * SEQ
    parts = lax.axis_size("feat")
    extra = row_count * parts - group_rows
    width_local = w_query.shape[0]
    hidden_local = w_mlp_out.shape[0]
    global_rows = lax.axis_index("feat") * row_count + jnp.arange(row_count, dtype=jnp.int32)
    owner = global_rows // SEQ
    matches = (owner[:, None] == jnp.arange(images, dtype=jnp.int32)[None, :]).astype(jnp.float32)
    row_mask = jnp.sum(matches * valid.astype(jnp.float32)[None, :], axis=1)
    live = (global_rows < group_rows).astype(jnp.float32)[:, None]

    def padded(values):
        return jnp.pad(values, ((0, extra), (0, 0)))

    local_input_rows = inputs.astype(jnp.float32)
    first_centered_scaled, first_inverse_deviation = apply_layer_norm(local_input_rows)
    normalized_first = (
        first_centered_scaled * attention_norm_gain.astype(jnp.float32)
        + attention_norm_shift.astype(jnp.float32)
    ).astype(jnp.bfloat16)
    normed_full = lax.all_gather(normalized_first, "feat", axis=0, tiled=True)[:group_rows]
    w_qkv = jnp.concatenate([w_query, w_key, w_value], axis=0)
    projected = jnp.einsum("rd,cd->rc", normed_full, w_qkv, preferred_element_type=jnp.float32)
    queries = (projected[:, :width_local] + b_query.astype(jnp.float32)).astype(jnp.bfloat16)
    key_rows = projected[:, width_local : 2 * width_local].astype(jnp.bfloat16)
    value_rows = (projected[:, 2 * width_local :] + b_value.astype(jnp.float32)).astype(
        jnp.bfloat16
    )
    mixed, log_totals = lax.map(
        image_forward,
        (by_image(queries, images), by_image(key_rows, images), by_image(value_rows, images)),
    )
    mixed = mixed.reshape(group_rows, width_local)
    partial_out = jnp.dot(mixed, w_attn_out, preferred_element_type=jnp.float32)
    attn = lax.psum_scatter(
        padded(partial_out), "feat", scatter_dimension=0, tiled=True
    ) + b_attn_out.astype(jnp.float32)
    middle_state = local_input_rows + attn
    second_centered_scaled, second_inverse_deviation = apply_layer_norm(middle_state)
    normalized_middle = (
        second_centered_scaled * feedforward_norm_gain.astype(jnp.float32)
        + feedforward_norm_shift.astype(jnp.float32)
    ).astype(jnp.bfloat16)
    mid_full = lax.all_gather(normalized_middle, "feat", axis=0, tiled=True)[:group_rows]
    hidden = jnp.dot(mid_full, w_mlp_in, preferred_element_type=jnp.float32) + b_mlp_in.astype(
        jnp.float32
    )
    active = (hidden * jax.nn.sigmoid(SLOPE * hidden)).astype(jnp.bfloat16)
    partial_mlp = jnp.dot(active, w_mlp_out, preferred_element_type=jnp.float32)
    branch = lax.psum_scatter(
        padded(partial_mlp).astype(jnp.bfloat16), "feat", scatter_dimension=0, tiled=True
    ).astype(jnp.float32) + b_mlp_out.astype(jnp.float32)
    output = (middle_state + branch) * live
    output_gradient = cotangent.astype(jnp.float32) * row_mask[:, None]
    grad_branch = output_gradient.astype(jnp.bfloat16)
    grad_b_mlp_out = column_sums(grad_branch)
    branch_full = lax.all_gather(grad_branch, "feat", axis=0, tiled=True)[:group_rows]
    grad_w_mlp_out = jnp.einsum(
        "rf,rd->fd", active, branch_full, preferred_element_type=jnp.float32
    )
    grad_active = jnp.einsum(
        "rd,fd->rf", branch_full, w_mlp_out, preferred_element_type=jnp.float32
    )
    grad_hidden = (grad_active * gelu_slope(hidden)).astype(jnp.bfloat16)
    grad_b_mlp_in = column_sums(grad_hidden)
    grad_mlp_in_rows = jnp.einsum(
        "rf,rd->fd", grad_hidden, mid_full, preferred_element_type=jnp.float32
    )
    partial_mid = jnp.einsum("rf,df->rd", grad_hidden, w_mlp_in, preferred_element_type=jnp.float32)
    midpoint_gradient = lax.psum_scatter(
        padded(partial_mid), "feat", scatter_dimension=0, tiled=True
    )
    feedforward_gain_gradient = jnp.sum(midpoint_gradient * second_centered_scaled, axis=0)
    grad_s_mlp = jnp.sum(midpoint_gradient, axis=0)
    middle_state_gradient = output_gradient + layer_norm_backward(
        midpoint_gradient, second_centered_scaled, second_inverse_deviation, feedforward_norm_gain
    )
    grad_attn = middle_state_gradient.astype(jnp.bfloat16)
    grad_b_attn_out = column_sums(grad_attn)
    attn_full = lax.all_gather(grad_attn, "feat", axis=0, tiled=True)[:group_rows]
    grad_w_attn_out = jnp.einsum("rh,rd->hd", mixed, attn_full, preferred_element_type=jnp.float32)
    grad_mixed = jnp.einsum(
        "rd,hd->rh", attn_full, w_attn_out, preferred_element_type=jnp.float32
    ).astype(jnp.bfloat16)
    grad_query, grad_key, grad_value = lax.map(
        image_backward,
        (
            by_image(queries, images),
            by_image(key_rows, images),
            by_image(value_rows, images),
            by_image(grad_mixed, images),
            log_totals,
        ),
    )
    grad_query = grad_query.reshape(group_rows, width_local)
    grad_key = grad_key.reshape(group_rows, width_local)
    grad_value = grad_value.reshape(group_rows, width_local)
    grad_b_query = column_sums(grad_query)
    grad_b_value = column_sums(grad_value)
    grad_qkv = jnp.concatenate([grad_query, grad_key, grad_value], axis=1)
    grad_w_qkv = jnp.einsum("rc,rd->cd", grad_qkv, normed_full, preferred_element_type=jnp.float32)
    partial_in = jnp.einsum("rc,cd->rd", grad_qkv, w_qkv, preferred_element_type=jnp.float32)
    normalized_gradient = lax.psum_scatter(
        padded(partial_in).astype(jnp.bfloat16), "feat", scatter_dimension=0, tiled=True
    ).astype(jnp.float32)
    attention_gain_gradient = jnp.sum(normalized_gradient * first_centered_scaled, axis=0)
    grad_s_attn = jnp.sum(normalized_gradient, axis=0)
    layer_input_gradient = middle_state_gradient + layer_norm_backward(
        normalized_gradient, first_centered_scaled, first_inverse_deviation, attention_norm_gain
    )
    local_powers = jnp.stack(
        [
            jnp.sum(row_mask[:, None] * local_input_rows * local_input_rows),
            jnp.sum(row_mask[:, None] * attn * attn),
            jnp.sum(row_mask[:, None] * branch * branch),
            jnp.sum(row_mask[:, None] * output * output),
        ]
    )
    local_count = jnp.sum(row_mask)
    bias_entries = jnp.concatenate([grad_b_query, grad_b_value, grad_b_mlp_in])
    bias_row = jnp.pad(bias_entries, (0, width - bias_entries.shape[0]))[None, :]
    packed = jnp.concatenate(
        [grad_w_qkv, grad_w_attn_out, grad_mlp_in_rows, grad_w_mlp_out, bias_row], axis=0
    )
    packed_rows = packed.shape[0]
    tok_parts = lax.axis_size("tok")
    fill_rows = (tok_parts - packed_rows % tok_parts) % tok_parts
    packed = jnp.pad(packed, ((0, fill_rows), (0, 0)))
    shares = lax.psum_scatter(
        packed.astype(jnp.bfloat16), "tok", scatter_dimension=0, tiled=True
    ).astype(jnp.float32)
    summed = lax.all_gather(shares.astype(jnp.bfloat16), "tok", axis=0, tiled=True).astype(
        shares.dtype
    )[:packed_rows]
    offset = 0
    grad_w_query = summed[offset : offset + width_local]
    offset += width_local
    grad_w_key = summed[offset : offset + width_local]
    offset += width_local
    grad_w_value = summed[offset : offset + width_local]
    offset += width_local
    grad_w_attn_out = summed[offset : offset + width_local]
    offset += width_local
    grad_w_mlp_in = summed[offset : offset + hidden_local].T
    offset += hidden_local
    grad_w_mlp_out = summed[offset : offset + hidden_local]
    offset += hidden_local
    bias_sums = summed[offset]
    grad_b_query = bias_sums[:width_local]
    grad_b_value = bias_sums[width_local : 2 * width_local]
    grad_b_mlp_in = bias_sums[2 * width_local : 2 * width_local + hidden_local]
    (
        grad_b_attn_out,
        grad_b_mlp_out,
        attention_gain_gradient,
        grad_s_attn,
        feedforward_gain_gradient,
        grad_s_mlp,
        powers,
        counted,
    ) = lax.psum(
        (
            grad_b_attn_out,
            grad_b_mlp_out,
            attention_gain_gradient,
            grad_s_attn,
            feedforward_gain_gradient,
            grad_s_mlp,
            local_powers,
            local_count,
        ),
        ("tok", "feat"),
    )
    stream_rms = jnp.sqrt(powers / (jnp.maximum(counted, 1.0) * D))
    return (
        output,
        layer_input_gradient,
        grad_w_query,
        grad_w_key,
        grad_w_value,
        grad_b_query,
        grad_b_value,
        grad_w_attn_out,
        grad_b_attn_out,
        grad_w_mlp_in,
        grad_b_mlp_in,
        grad_w_mlp_out,
        grad_b_mlp_out,
        attention_gain_gradient,
        grad_s_attn,
        feedforward_gain_gradient,
        grad_s_mlp,
        stream_rms,
    )


BF16 = jnp.bfloat16
F32 = jnp.float32
AXES = ("tok", "feat")
SLOTS = (0, 1, 3, 2)
PAIRS = ((0, 1), (3, 2))
CHUNK = 16
PART = DH // 2


def route(move):
    found = []
    for tok in range(4):
        for feat in range(8):
            target = move(tok // 2, tok % 2, feat // 2, feat % 2)
            if target is not None:
                x, c, z, y = target
                found.append((tok * 8 + feat, (2 * x + c) * 8 + 2 * z + y))
    return found


SWAP_X = route(lambda x, c, z, y: (1 - x, c, z, y))
SWAP_C = route(lambda x, c, z, y: (x, 1 - c, z, y))
SWAP_Y = route(lambda x, c, z, y: (x, c, z, 1 - y))
UP_Z = route(lambda x, c, z, y: (x, c, (z + 1) % 4, y))
DOWN_Z = route(lambda x, c, z, y: (x, c, (z + 3) % 4, y))
FLIP_Z = [route(lambda x, c, z, y, s=s: (x, c, z ^ s, y)) for s in range(4)]
NEXT = [(t * 8 + f, t * 8 + f + 1) for t in range(4) for f in range(7)]
PREVIOUS = [(t * 8 + f + 1, t * 8 + f) for t in range(4) for f in range(7)]


def send(values, pairs):
    return lax.ppermute(values, AXES, pairs)


def nt(left, right):
    return lax.dot_general(left, right, (((1,), (1,)), ((), ())), preferred_element_type=F32)


def nn(left, right):
    return lax.dot_general(left, right, (((1,), (0,)), ((), ())), preferred_element_type=F32)


def tn(left, right):
    return lax.dot_general(left, right, (((0,), (0,)), ((), ())), preferred_element_type=F32)


SMEM = pl.BlockSpec(memory_space=pltpu.SMEM)
HBM = pl.BlockSpec(memory_space=pltpu.HBM)
VMEM = pl.BlockSpec(memory_space=pltpu.VMEM)


def kernel_call(body, operands, specs, outs, scratch=(), after=(), vmem=12):
    count, extra = len(operands), len(after)

    def kernel(*refs):
        body(*refs[:count], *refs[count + extra :])

    return pl.pallas_call(
        kernel,
        in_specs=list(specs) + [VMEM] * extra,
        out_specs=[VMEM] * len(outs),
        out_shape=[jax.ShapeDtypeStruct(shape, dtype) for shape, dtype in outs],
        scratch_shapes=list(scratch),
        compiler_params=pltpu.CompilerParams(
            vmem_limit_bytes=vmem * 2**20, fuse_transposed_lhs_in_matmul=True
        ),
        cost_estimate=pl.CostEstimate(flops=10**10, bytes_accessed=2**16, transcendentals=0),
    )(*operands, *after)


def coordinates():
    tok, feat = lax.axis_index("tok"), lax.axis_index("feat")
    return tok // 2, tok % 2, feat // 2, feat % 2


def chunks(half):
    return [slice(at, at + CHUNK) for at in range(0, half, CHUNK)]


def row_of(vector):
    return vector[...].astype(F32).reshape(1, vector.shape[0])


def folded(values):
    return values[:8] + values[8:]


def moment_norm(values):
    center = jnp.mean(values, axis=1, keepdims=True)
    spread = jnp.mean(values * values, axis=1, keepdims=True) - center * center
    inverse = lax.rsqrt(spread + EPSILON)
    return (values - center) * inverse, inverse


def attention_weights_kernel(wq, wk, wv, wo, b_query, b_value, b_hidden, *refs):
    own, other, both, query, value, hidden, sems = refs
    piece = own.shape[0]
    x, c, _, _ = coordinates()
    width = own.shape[1]
    copies = []
    for source, target in ((b_query, query), (b_value, value), (b_hidden, hidden)):
        copies.append(pltpu.make_async_copy(source, target, sems.at[len(copies)]))
    targets = ((own, 0, x), (other, 0, 1 - x), (both, 0, x), (both, piece, 1 - x))
    for out, first, side in targets:
        at = pl.multiple_of(c * DH + side * PART, PART)
        for m, w in enumerate((wq, wk, wv, wo)):
            copies.append(
                pltpu.make_async_copy(
                    w.at[pl.ds(at, PART)], out.at[pl.ds(first + m * PART, PART)], sems.at[len(copies)]
                )
            )
    for copy in copies:
        copy.start()
    for copy in copies[:3]:
        copy.wait()
    parts = [row_of(vector) for vector in (query, value, hidden)]
    taken = sum(part.shape[1] for part in parts)
    bias = jnp.concatenate(parts + [jnp.zeros((1, width - taken), F32)], axis=1)
    bias = jnp.broadcast_to(bias, (16, width)).astype(BF16)
    for out, first, _ in targets:
        out[first + 4 * PART : first + piece, :] = bias
    for copy in copies[3:]:
        copy.wait()


def edge_kernel(inputs, cotangent, edge):
    rows = inputs.shape[0]
    at = (rows - 8) // 16 * 16
    for i, values in enumerate((inputs, cotangent)):
        edge[8 * i : 8 * i + 8, :] = values[at:, :].astype(F32)[rows - 8 - at :].astype(BF16)


def mlp_weights_kernel(w_in, w_out, own, other, both):
    x, c, _, _ = coordinates()
    quarter = own.shape[0] // 2
    for out, first, side in ((own, 0, x), (other, 2 * quarter, 1 - x)):
        at = pl.multiple_of((2 * c + side) * quarter, quarter)
        found = w_in[:, pl.ds(at, quarter)].T
        rest = w_out[pl.ds(at, quarter), :]
        out[:quarter, :] = found
        out[quarter:, :] = rest
        both[first : first + quarter, :] = found
        both[first + quarter : first + 2 * quarter, :] = rest


def halves_of(refs, count):
    own_zero, other_zero, own_one, other_one, both, own_two, other_two = refs
    own = [own_zero, own_one, both.at[pl.ds(0, count)], own_two]
    return own, [other_zero, other_one, both.at[pl.ds(count, count)], other_two]


def entry_kernel(
    valid, inputs, cotangent, edge, gain_vector, shift_vector, stream, normed, branch, again, ext
):
    _, _, z, y = coordinates()
    rows = inputs.shape[0]
    half = stream.shape[0]
    gain, shift = row_of(gain_vector), row_of(shift_vector)
    flag = valid[z].astype(F32)

    def aligned(at):
        found = pltpu.roll(ext[at.start : at.stop + 8, :], CHUNK + z, 0)[:CHUNK]
        index = at.start + lax.broadcasted_iota(jnp.int32, (CHUNK, 1), 0)
        return jnp.where(index < rows - y, found, 0.0)

    def fill(values, first):
        ext[0:8, :] = edge[...].astype(F32)[first : first + 8]
        ext[8 : 8 + rows, :] = values[...].astype(F32)

    fill(inputs, 0)
    for at in chunks(half):
        found = aligned(at)
        stream[at, :] = found.astype(BF16)
        hat, _ = moment_norm(found)
        normed[at, :] = (hat * gain + shift).astype(BF16)
    fill(cotangent, 8)
    for at in chunks(half):
        branch[at, :] = (aligned(at) * flag).astype(BF16)
        again[at, :] = branch[at, :]


def softmax_columns(scores):
    top = jnp.max(scores, axis=0, keepdims=True)
    weights = jnp.exp(scores - top)
    return weights * (1.0 / jnp.sum(weights, axis=0, keepdims=True))


def forward_body(rows, halves, w_in, w_out, bias, qkv, probs, mixed, partials):
    half = halves[0].shape[0]
    _, _, _, y = coordinates()
    entry = jnp.concatenate([halves[0][...], halves[1][...]], axis=0)
    qkv[...] = (nt(entry, w_in) + bias).astype(BF16)
    key_index = lax.broadcasted_iota(jnp.int32, (2 * half, 1), 0)
    first = rows - y
    second = half + rows - 1 + y
    real = (key_index < first) | ((key_index >= half) & (key_index < second))
    penalty = jnp.where(real, 0.0, -1e30)
    for p in range(2):
        outs = []
        for h in (2 * p, 2 * p + 1):
            at = slice(h * DH, (h + 1) * DH)
            q = qkv[:, at] * jnp.asarray(DH ** (-0.5), BF16)
            k = qkv[:, 4 * DH + h * DH : 4 * DH + (h + 1) * DH]
            v = qkv[:, 8 * DH + h * DH : 8 * DH + (h + 1) * DH]
            found = softmax_columns(nt(k, q) + penalty).astype(BF16)
            probs[h] = found
            outs.append(tn(v, found))
        mixed[:, 2 * DH * p : 2 * DH * (p + 1)] = jnp.concatenate(outs, axis=0).T.astype(BF16)
    found = nn(mixed[...], w_out).astype(BF16)
    at = 0
    for out in partials:
        out[...] = found[at : at + out.shape[0]]
        at += out.shape[0]


def ordered_bias(row, first):
    x, c, _, _ = coordinates()
    block = jnp.where(c == 0, row[:, first : first + DH], row[:, first + DH : first + 2 * DH])
    swapped = jnp.concatenate([block[:, PART:], block[:, :PART]], axis=1)
    return jnp.where(x == 0, block, swapped)


def first_forward_kernel(rows, *refs):
    halves, refs = refs[:2], refs[2:]
    own, other = halves_of(refs[:7], refs[0].shape[0])
    refs = refs[7:]
    qkv, probs, mixed, partial, w_in, w_out, bias = refs
    for m in range(4):
        target = w_out if m == 3 else w_in
        for k in range(4):
            at = (0 if m == 3 else m * 4 * DH) + k * DH
            target[at : at + PART, :] = own[k][m * PART : (m + 1) * PART, :]
            target[at + PART : at + DH, :] = other[k][m * PART : (m + 1) * PART, :]
    rows_of = [own[k][4 * PART :, :].astype(F32)[0:1] for k in range(4)]
    query = jnp.concatenate([ordered_bias(r, 0) for r in rows_of], axis=1)
    value = jnp.concatenate([ordered_bias(r, 2 * DH) for r in rows_of], axis=1)
    bias[...] = jnp.broadcast_to(
        jnp.concatenate([query, jnp.zeros_like(query), value], axis=1), bias.shape
    )
    forward_body(
        rows,
        halves,
        w_in[...],
        w_out[...],
        bias[0:1, :],
        qkv,
        probs,
        mixed,
        (partial,),
    )


def second_forward_kernel(rows, near, far, w_in, w_out, bias, *refs):
    qkv, probs, mixed, *partials = refs
    forward_body(
        rows,
        (near, far),
        w_in[...],
        w_out[...],
        bias[0:1, :],
        qkv,
        probs,
        mixed,
        partials,
    )


def real_rows(at, rows, y):
    return at.start + lax.broadcasted_iota(jnp.int32, (CHUNK, 1), 0) < rows - y


def middle_kernel(
    rows,
    valid,
    partial,
    from_core,
    from_y,
    stream,
    bias_vector,
    gain_vector,
    shift_vector,
    middle,
    normed,
    powers,
):
    _, _, z, y = coordinates()
    bias, gain, shift = row_of(bias_vector), row_of(gain_vector), row_of(shift_vector)
    total = jnp.zeros((8, middle.shape[1]), F32)
    for at in chunks(middle.shape[0]):
        attn = partial[at, :].astype(F32) + from_core[at, :].astype(F32)
        attn = attn + from_y[at, :].astype(F32) + bias
        found = stream[at, :].astype(F32) + attn
        middle[at, :] = found
        hat, _ = moment_norm(found)
        normed[at, :] = (hat * gain + shift).astype(BF16)
        total = total + folded(jnp.where(real_rows(at, rows, y), attn * attn, 0.0))
    powers[...] = total * valid[z].astype(F32)


def mlp_kernel(near, far, grad_near, grad_far, *refs):
    own, other = halves_of(refs[:7], refs[0].shape[0])
    bias_of, refs = refs[7:11], refs[11:]
    active, grad_hidden, mid_near, mid_far, out_near, out_far, sums = refs
    x, c, _, _ = coordinates()
    half = near.shape[0]
    quarter = own[0].shape[0] // 2
    w_in = [ref[:quarter, :] for side in (own, other) for ref in side]
    w_out = [ref[quarter:, :] for side in (own, other) for ref in side]
    bias = []
    for side in (x, 1 - x):
        at = pl.multiple_of(4 * DH + (2 * c + side) * quarter, quarter)
        for k in range(4):
            bias.append(bias_of[k][4 * PART :, pl.ds(at, quarter)].astype(F32)[0:1])
    bias = jnp.concatenate(bias, axis=1)
    rows = jnp.concatenate([near[...], far[...]], axis=0)
    grads = jnp.concatenate([grad_near[...], grad_far[...]], axis=0)
    size = 2 * quarter
    for n in range(4):
        at = slice(n * size, (n + 1) * size)
        pair = slice(2 * n, 2 * n + 2)
        u = nt(rows, jnp.concatenate(w_in[pair], axis=0)) + bias[:, at]
        gate = jax.nn.sigmoid(SLOPE * u)
        act = u * gate
        active[:, at] = act.astype(BF16)
        slope = gate + SLOPE * act * (1.0 - gate)
        found = (nt(grads, jnp.concatenate(w_out[pair], axis=0)) * slope).astype(BF16)
        grad_hidden[:, at] = found
        sums[:, at] = jnp.broadcast_to(
            jnp.sum(found.astype(F32), axis=0, keepdims=True), (8, size)
        )
    found = nn(grad_hidden[...], jnp.concatenate(w_in, axis=0)).astype(BF16)
    mid_near[...] = found[:half]
    mid_far[...] = found[half:]
    found = nn(active[...], jnp.concatenate(w_out, axis=0)).astype(BF16)
    out_near[...] = found[:half]
    out_far[...] = found[half:]


def products_kernel(split, left_first, left_second, *refs):
    pieces, outs = refs[:4], refs[4:]
    right = jnp.concatenate([piece[...] for piece in pieces], axis=0)
    hidden = left_first.shape[1] // 2
    quarter = hidden // 4
    for side in (1, 0):
        at = slice(side * hidden, (side + 1) * hidden)
        left = jnp.concatenate([left_first[:, at], left_second[:, at]], axis=0)
        found = tn(left, right).astype(BF16)
        if split:
            for k in range(4):
                outs[k][side * quarter : (side + 1) * quarter, :] = found[
                    k * quarter : (k + 1) * quarter
                ]
        else:
            outs[side][...] = found


def far_sum_kernel(values, received, out):
    first = received.shape[0] - out.shape[0]
    for at in chunks(out.shape[0]):
        moved = slice(first + at.start, first + at.stop)
        out[at, :] = (values[at, :].astype(F32) + received[moved, :].astype(F32)).astype(BF16)


def add_split_kernel(keep, received, *outs):
    at = 0
    for out in outs:
        size = out.shape[0]
        out[...] = (
            keep[at : at + size, :].astype(F32) + received[at : at + size, :].astype(F32)
        ).astype(BF16)
        at += size


def output_kernel(
    rows,
    valid,
    partial,
    from_core,
    from_y,
    middle,
    stream,
    bias_vector,
    attn_power,
    sums,
    output,
    heads,
    small,
):
    _, _, z, y = coordinates()
    bias = row_of(bias_vector)
    width = middle.shape[1]
    totals = [jnp.zeros((8, width), F32) for _ in range(3)]
    for at in chunks(middle.shape[0]):
        branch = partial[at, :].astype(F32) + from_core[at, :].astype(F32)
        branch = branch + from_y[at, :].astype(F32) + bias
        found = middle[at, :] + branch
        output[at, :] = found
        entry = stream[at, :].astype(F32)
        real = real_rows(at, rows, y)
        for i, v in enumerate((entry, branch, found)):
            totals[i] = totals[i] + folded(jnp.where(real, v * v, 0.0))
    heads[...] = output[0:8, :]
    flag = valid[z]
    lane = lax.broadcasted_iota(jnp.int32, (1, width), 1)
    entry = jnp.where(lane == 4, (flag * (rows - y)).astype(F32), 0.0)
    powers = [totals[0] * flag.astype(F32), attn_power[...]]
    powers += [total * flag.astype(F32) for total in totals[1:]]
    for i, power in enumerate(powers):
        whole = jnp.sum(jnp.sum(power, axis=0, keepdims=True), axis=1, keepdims=True)
        entry = entry + jnp.where(lane == i, whole, 0.0)
    row = lax.broadcasted_iota(jnp.int32, (8, 1), 0)
    small[...] = jnp.where(row == 6, entry, sums[...])


def norm_back(grad, hat, inverse, gain):
    scaled = grad * gain
    plain = jnp.mean(scaled, axis=1, keepdims=True)
    cross = jnp.mean(scaled * hat, axis=1, keepdims=True)
    return inverse * (scaled - plain - hat * cross)


def middle_back_kernel(
    partial, from_core, from_y, middle, branch, gain_vector, grad, low, sums
):
    width = middle.shape[1]
    gain = row_of(gain_vector)
    totals = [jnp.zeros((8, width), F32) for _ in range(4)]
    for at in chunks(middle.shape[0]):
        found = partial[at, :].astype(F32) + from_core[at, :].astype(F32)
        found = found + from_y[at, :].astype(F32)
        hat, inverse = moment_norm(middle[at, :])
        gy = branch[at, :].astype(F32)
        total = gy + norm_back(found, hat, inverse, gain)
        grad[at, :] = total
        rounded = total.astype(BF16)
        low[at, :] = rounded
        for i, v in enumerate((rounded.astype(F32), gy, found * hat, found)):
            totals[i] = totals[i] + folded(v)
    sums[...] = jnp.concatenate(
        [jnp.sum(v, axis=0, keepdims=True) for v in totals] + [jnp.zeros((4, width), F32)], axis=0
    )


def backward_kernel(pair, *refs):
    grads, normed, refs = refs[:4], refs[4:8], refs[8:]
    w_out, qkv_own, qkv_other, probs_own, probs_other = refs[:5]
    mixed_own, mixed_other, sums_chip, sums_distant = refs[5:9]
    out_own, out_other, give, keep = refs[9:]
    half = grads[0].shape[0]
    rows = 2 * half
    lanes = 2 * DH
    first = pair * lanes
    scale = jnp.asarray(DH ** (-0.5), BF16)
    grad_rows = jnp.concatenate([ref[...] for ref in grads], axis=0)
    wide = nt(grad_rows, w_out[first : first + lanes, :]).astype(BF16)
    hidden_sums = sums_chip[0:1, :] + sums_distant[0:1, :]
    totals = []
    images = ((qkv_own, probs_own, out_own), (qkv_other, probs_other, out_other))
    for image, (qkv, probs, out) in enumerate(images):
        dq, dk, dv = [], [], []
        for h in range(2):
            at = first + h * DH
            q = qkv[:, at : at + DH] * scale
            k = qkv[:, 4 * DH + at : 4 * DH + at + DH] * scale
            v = qkv[:, 8 * DH + at : 8 * DH + at + DH]
            g = wide[image * rows : (image + 1) * rows, h * DH : (h + 1) * DH]
            found = probs[2 * pair + h]
            grad_probs = nt(v, g)
            scores = found.astype(F32)
            product = scores * grad_probs
            inner = jnp.sum(product, axis=0, keepdims=True)
            grad_scores = (product - scores * inner).astype(BF16)
            dv.append(nn(found, g))
            dk.append(nn(grad_scores, q))
            dq.append(tn(k, grad_scores))
        query = jnp.concatenate(dq, axis=0).T.astype(BF16)
        value = jnp.concatenate(dv, axis=1).astype(BF16)
        out[:, :lanes] = query
        out[:, lanes : 2 * lanes] = jnp.concatenate(dk, axis=1).astype(BF16)
        out[:, 2 * lanes :] = value
        totals.append(
            [jnp.sum(v.astype(F32), axis=0, keepdims=True) for v in (query, value)]
        )
    query_sum, value_sum = (totals[0][i] + totals[1][i] for i in range(2))
    stacked = jnp.concatenate([out_own[...], out_other[...]], axis=0)
    grad_w = tn(stacked, jnp.concatenate([ref[...] for ref in normed], axis=0)).astype(BF16)
    mixed = jnp.concatenate(
        [ref[:, first : first + lanes] for ref in (mixed_own, mixed_other)], axis=0
    )
    grad_o = tn(mixed, grad_rows).astype(BF16)
    size = 4 * PART + 16
    quarter = hidden_sums.shape[1] // 8
    width = give.shape[1]
    for side, out in enumerate((keep, give)):
        for i in range(2):
            for m in range(4):
                source = grad_o if m == 3 else grad_w
                at = (0 if m == 3 else m * lanes) + i * DH + side * PART
                out[i * size + m * PART : i * size + (m + 1) * PART, :] = source[at : at + PART]
            at = i * DH + side * PART
            block = (side * 4 + 2 * pair + i) * quarter
            row = jnp.concatenate(
                [
                    query_sum[:, at : at + PART],
                    value_sum[:, at : at + PART],
                    jnp.zeros((1, DH), F32),
                    hidden_sums[:, block : block + quarter],
                    jnp.zeros((1, width - lanes - quarter), F32),
                ],
                axis=1,
            )
            out[i * size + 4 * PART : (i + 1) * size, :] = jnp.broadcast_to(row, (16, width)).astype(
                BF16
            )


def entry_product_kernel(first_pair, second_pair, w_in, *outs):
    lanes = 2 * DH
    joined = jnp.concatenate(
        [
            ref[:, m * lanes : (m + 1) * lanes]
            for m in range(3)
            for ref in (first_pair, second_pair)
        ],
        axis=1,
    )
    found = nn(joined, w_in[...]).astype(BF16)
    at = 0
    for out in outs:
        out[...] = found[at : at + out.shape[0]]
        at += out.shape[0]


def entry_back_kernel(
    rows,
    valid,
    partial,
    from_core,
    from_y,
    stream,
    grad_middle,
    gain_vector,
    middle_sums,
    grad,
    heads,
    small,
):
    width = stream.shape[1]
    gain = row_of(gain_vector)
    totals = [jnp.zeros((8, width), F32) for _ in range(2)]
    for at in chunks(stream.shape[0]):
        found = partial[at, :].astype(F32) + from_core[at, :].astype(F32)
        found = found + from_y[at, :].astype(F32)
        hat, inverse = moment_norm(stream[at, :].astype(F32))
        grad[at, :] = grad_middle[at, :] + norm_back(found, hat, inverse, gain)
        for i, v in enumerate((found * hat, found)):
            totals[i] = totals[i] + folded(v)
    heads[...] = grad[0:8, :]
    small[...] = jnp.concatenate(
        [middle_sums[0:2, :]]
        + [jnp.sum(v, axis=0, keepdims=True) for v in totals]
        + [middle_sums[2:4, :], middle_sums[6:8, :]],
        axis=0,
    )


def exit_kernel(output, grad, after, output_rows, grad_rows, ext):
    _, _, z, y = coordinates()
    half = output.shape[0]
    rows = output_rows.shape[0]
    count = rows - y
    index = lax.broadcasted_iota(jnp.int32, (half, 1), 0)
    ext[8:, :] = jnp.zeros((half - 8, ext.shape[1]), F32)
    for values, at, out in ((output, 0, output_rows), (grad, 8, grad_rows)):
        ext[0:8, :] = after[at : at + 8, :]
        moved = pltpu.roll(values[...], half - z, 0)
        beyond = pltpu.roll(ext[...], count - z, 0)
        out[...] = jnp.where(index < count - z, moved, beyond)[:rows]


def attention_gradients_kernel(own, across, core, core_across, *outs):
    x, c, _, _ = coordinates()
    query, value, hidden = outs[4:]
    pieces = ((own, c, x), (across, c, 1 - x), (core, 1 - c, x), (core_across, 1 - c, 1 - x))
    for ref, c_of, x_of in pieces:
        at = pl.multiple_of(c_of * DH + x_of * PART, PART)
        for m in range(4):
            outs[m][pl.ds(at, PART), :] = ref[m * PART : (m + 1) * PART, :].astype(F32)
    rows = [ref[4 * PART :, :].astype(F32)[0:1] for ref, _, _ in pieces]
    natural = []
    for c_of in range(2):
        for x_of in range(2):
            same = jnp.where(x == x_of, rows[0], rows[1])
            changed = jnp.where(x == x_of, rows[2], rows[3])
            natural.append(jnp.where(c == c_of, same, changed))
    quarter = hidden.shape[0] // 4
    for out, at, size in ((query, 0, PART), (value, PART, PART), (hidden, 2 * DH, quarter)):
        found = jnp.concatenate([row[:, at : at + size] for row in natural], axis=1)
        out[...] = found.reshape(out.shape)


def mlp_in_gradient_kernel(own, across, core, core_across, out):
    x, c, _, _ = coordinates()
    pieces = ((own, c, x), (across, c, 1 - x), (core, 1 - c, x), (core_across, 1 - c, 1 - x))
    for ref, c_of, x_of in pieces:
        quarter = ref.shape[0]
        at = pl.multiple_of((2 * c_of + x_of) * quarter, quarter)
        out[:, pl.ds(at, quarter)] = ref[...].astype(F32).T


def swapped_sum_kernel(own, received, out):
    size = own.shape[0] // 2
    out[:size, :] = (own[:size, :].astype(F32) + received[size:, :].astype(F32)).astype(BF16)
    out[size:, :] = (own[size:, :].astype(F32) + received[:size, :].astype(F32)).astype(BF16)


def mlp_out_gradient_kernel(own, core, out):
    x, c, _, _ = coordinates()
    for ref, c_of in ((own, c), (core, 1 - c)):
        quarter = ref.shape[0] // 2
        for i, side in enumerate((x, 1 - x)):
            at = pl.multiple_of((2 * c_of + side) * quarter, quarter)
            out[pl.ds(at, quarter), :] = ref[i * quarter : (i + 1) * quarter, :].astype(F32)


def sums_kernel(small, received, *outs):
    found = small[...] + received[...]
    for i, out in enumerate(outs[:-1]):
        out[...] = found[i : i + 1].reshape(out.shape)
    outs[-1][...] = found[6:7, : outs[-1].shape[0]].reshape(outs[-1].shape)


def copy_kernel(source, target):
    target[...] = source[...]


def add_wide_kernel(first, second, out):
    out[...] = first[...] + second[...]


def add_split_last_kernel(keep, received, last, zero, one):
    size = zero.shape[0]
    zero[...] = (keep[:size, :].astype(F32) + received[:size, :].astype(F32)).astype(BF16)
    found = keep[size:, :].astype(F32) + received[size:, :].astype(F32)
    one[...] = (found + last[...].astype(F32)).astype(BF16)


def add_three_kernel(first, second, third, out):
    out[...] = (
        first[...].astype(F32) + second[...].astype(F32) + third[...].astype(F32)
    ).astype(BF16)


def on_device(
    inputs,
    valid,
    cotangent,
    w_query,
    w_key,
    w_value,
    b_query,
    b_value,
    w_attn_out,
    b_attn_out,
    w_mlp_in,
    b_mlp_in,
    w_mlp_out,
    b_mlp_out,
    attention_norm_gain,
    attention_norm_shift,
    feedforward_norm_gain,
    feedforward_norm_shift,
):
    rows, width = inputs.shape
    images = valid.shape[0]
    heads_local = w_query.shape[0] // DH
    hidden_local = w_mlp_out.shape[0]
    shape = (lax.axis_size("tok"), lax.axis_size("feat"), images, heads_local, hidden_local, width)
    if shape != (4, 8, 4, 2, 512, 1024) or 2 * rows != SEQ + 1:
        return on_device_general(
            inputs,
            valid,
            cotangent,
            w_query,
            w_key,
            w_value,
            b_query,
            b_value,
            w_attn_out,
            b_attn_out,
            w_mlp_in,
            b_mlp_in,
            w_mlp_out,
            b_mlp_out,
            attention_norm_gain,
            attention_norm_shift,
            feedforward_norm_gain,
            feedforward_norm_shift,
        )
    half = (rows + 15) // 16 * 16
    image = 2 * half
    quarter = hidden_local // 4
    piece = 4 * PART + 16
    row_block = (half, width)
    low_rows, wide_rows = (row_block, BF16), (row_block, F32)
    last = ()

    def call(body, operands, outs, scratch=(), gate=(), specs=None):
        nonlocal last
        specs = [VMEM] * len(operands) if specs is None else specs
        found = kernel_call(body, operands, specs, outs, scratch, last + tuple(gate))
        last = (min(found, key=lambda v: v.size * v.dtype.itemsize),)
        return found

    def pin(values, gate=()):
        return call(copy_kernel, (values,), [(values.shape, values.dtype)], gate=gate)[0]

    def far_sum(values, received, gate=()):
        return call(far_sum_kernel, (values, received), [low_rows], gate=gate)[0]

    def split(values, received, sizes, gate=()):
        outs = [((size, width), BF16) for size in sizes]
        return call(add_split_kernel, (values, received), outs, gate=gate)

    def add_last(values, one, three, gate=()):
        return call(add_three_kernel, (values, one, three), [(values.shape, BF16)], gate=gate)[0]

    in_hbm = [
        pltpu.with_memory_space_constraint(w, pltpu.HBM)
        for w in (w_query, w_key, w_value, w_attn_out, b_query, b_value, b_mlp_in)
    ]
    attn_own, attn_other, attn_both = call(
        attention_weights_kernel,
        in_hbm,
        [((piece, width), BF16)] * 2 + [((2 * piece, width), BF16)],
        scratch=[
            pltpu.VMEM((2 * DH,), BF16),
            pltpu.VMEM((2 * DH,), BF16),
            pltpu.VMEM((hidden_local,), BF16),
            pltpu.SemaphoreType.DMA((19,)),
        ],
        specs=[HBM] * 7,
    )
    own_one = send(attn_own, UP_Z)
    attn_three = send(attn_both, DOWN_Z)
    (edge,) = call(edge_kernel, (inputs, cotangent), [((16, width), BF16)])
    edge = send(edge, NEXT)
    mlp_own, mlp_other, mlp_both = call(
        mlp_weights_kernel,
        (w_mlp_in, w_mlp_out),
        [((2 * quarter, width), BF16)] * 2 + [((4 * quarter, width), BF16)],
    )
    stream, normed, branch_grad, branch_again = call(
        entry_kernel,
        (valid, inputs, cotangent, edge, attention_norm_gain, attention_norm_shift),
        [low_rows] * 4,
        scratch=[pltpu.VMEM((half + 8, width), F32)],
        gate=(own_one,),
        specs=[SMEM] + [VMEM] * 5,
    )
    own_two = send(own_one, UP_Z)
    other_one = send(own_one, SWAP_X)
    normed_y, normed_c = send(normed, SWAP_Y), send(normed, SWAP_C)
    mlp_first = pin(mlp_own, (attn_three, normed_c))
    mlp_one = send(mlp_first, UP_Z)
    pin(edge, (own_two, other_one))
    other_two = send(own_two, SWAP_X)
    branch_again = pin(branch_again, (normed_y,))
    normed_yc = send(normed_y, SWAP_C)
    branch_y, branch_c = send(branch_again, SWAP_Y), send(branch_again, SWAP_C)
    attn_pieces = (attn_own, attn_other, own_one, other_one, attn_three, own_two, other_two)

    head_out = [
        ((image, 12 * DH), BF16),
        ((4, image, image), BF16),
        ((image, 4 * DH), BF16),
    ]
    qkv_other, probs_other, mixed_other, partial_other, w_heads, w_out, head_bias = call(
        functools.partial(first_forward_kernel, rows),
        (normed_c, normed_yc) + attn_pieces,
        head_out
        + [((image, width), BF16)]
        + [((12 * DH, width), BF16), ((4 * DH, width), BF16), ((8, 12 * DH), F32)],
        gate=(branch_c,),
    )
    from_core = send(partial_other, SWAP_C)
    mlp_both = pin(mlp_both, (mlp_one,))
    mlp_three = send(mlp_both, DOWN_Z)
    mlp_two = send(mlp_one, UP_Z)
    mlp_other_one = send(mlp_one, SWAP_X)
    qkv_own, probs_own, mixed_own, partial_near, partial_far = call(
        functools.partial(second_forward_kernel, rows),
        (normed, normed_y, w_heads, w_out, head_bias),
        head_out + [low_rows] * 2,
    )
    attn_far = far_sum(partial_far, from_core, (branch_y,))
    from_y = send(attn_far, SWAP_Y)
    branch_yc = send(branch_y, SWAP_C)
    middle, normed_middle, attn_power = call(
        functools.partial(middle_kernel, rows),
        (valid, partial_near, from_core, from_y, stream)
        + (b_attn_out, feedforward_norm_gain, feedforward_norm_shift),
        [wide_rows, low_rows, ((8, width), F32)],
        gate=(mlp_other_one, branch_yc),
        specs=[SMEM] + [VMEM] * 7,
    )
    middle_y, middle_c = send(normed_middle, SWAP_Y), send(normed_middle, SWAP_C)
    pin(attn_power, (mlp_two, middle_c))
    mlp_other_two = send(mlp_two, SWAP_X)

    middle_yc = send(middle_y, SWAP_C)
    pieces = (mlp_own, mlp_other, mlp_one, mlp_other_one, mlp_three, mlp_two, mlp_other_two)
    pieces += (attn_own, own_one, attn_three, own_two)
    mlp_out = (
        [((image, 8 * quarter), BF16)] * 2 + [low_rows] * 4 + [((8, 8 * quarter), F32)]
    )
    chip = call(
        mlp_kernel,
        (normed_middle, middle_c, branch_grad, branch_c) + pieces,
        mlp_out,
        gate=(middle_y,),
    )
    mid_core, out_core = send(chip[3], SWAP_C), send(chip[5], SWAP_C)
    distant = call(mlp_kernel, (middle_y, middle_yc, branch_y, branch_yc) + pieces, mlp_out)
    out_distant = send(distant[5], SWAP_C)
    mid_far = far_sum(distant[2], send(distant[3], SWAP_C), (mid_core, out_core))
    mid_y = send(mid_far, SWAP_Y)

    grad_out = call(
        functools.partial(products_kernel, True),
        (chip[0], distant[0], branch_grad, branch_c, branch_y, branch_yc),
        [((2 * quarter, width), BF16)] * 4,
        gate=(out_distant,),
    )
    grad_out = dict(zip(SLOTS, grad_out))
    out_two = send(grad_out[2], DOWN_Z)
    out_three = send(grad_out[3], UP_Z)
    grad_in_keep, grad_in_give = call(
        functools.partial(products_kernel, False),
        (chip[1], distant[1], normed_middle, middle_c, middle_y, middle_yc),
        [((4 * quarter, width), BF16)] * 2,
    )
    in_received = send(grad_in_give, SWAP_X)
    grad_middle, grad_attn, middle_sums = call(
        middle_back_kernel,
        (chip[2], mid_core, mid_y, middle, branch_grad, feedforward_norm_gain),
        [wide_rows, low_rows, ((8, width), F32)],
    )
    grad_y, grad_c = send(grad_attn, SWAP_Y), send(grad_attn, SWAP_C)
    out_far = far_sum(distant[4], out_distant)
    (one,) = split(grad_out[1], out_two, (2 * quarter,), (grad_c,))
    out_one = send(one, DOWN_Z)
    grad_yc = send(grad_y, SWAP_C)

    def backward(p, gate=()):
        return call(
            functools.partial(backward_kernel, p),
            (grad_attn, grad_y, grad_c, grad_yc, normed, normed_y, normed_c, normed_yc)
            + (w_out, qkv_own, qkv_other, probs_own, probs_other)
            + (mixed_own, mixed_other, chip[6], distant[6]),
            [((image, 6 * DH), BF16)] * 2 + [((2 * piece, width), BF16)] * 2,
            gate=gate,
        )

    second_own, second_other, give, keep = backward(1, (out_three,))
    received = send(give, SWAP_X)
    out_y = send(pin(out_far, (out_one,)), SWAP_Y)
    in_pieces = split(grad_in_keep, in_received, (quarter,) * 4)
    in_pieces = dict(zip(SLOTS, in_pieces))
    in_two = send(in_pieces[2], DOWN_Z)
    in_three = send(in_pieces[3], UP_Z)
    first_own, first_other, give_first, keep_first = backward(0)
    received_first = send(give_first, SWAP_X)
    (one,) = split(in_pieces[1], in_two, (quarter,), (out_y,))
    in_one = send(one, DOWN_Z)
    (entry_other,) = call(
        entry_product_kernel, (first_other, second_other, w_heads), [((image, width), BF16)]
    )
    entry_core = send(entry_other, SWAP_C)
    three, two = split(keep, received, (piece,) * 2, (in_three,))
    attn_two = send(two, DOWN_Z)
    attn_three = send(three, UP_Z)
    entry_near, entry_far = call(
        entry_product_kernel, (first_own, second_own, w_heads), [low_rows] * 2
    )
    entry_far = far_sum(entry_far, entry_core, (in_one,))
    entry_y = send(entry_far, SWAP_Y)
    output, output_heads, power_sums = call(
        functools.partial(output_kernel, rows),
        (valid, chip[4], out_core, out_y, middle, stream, b_mlp_out, attn_power, middle_sums),
        [wide_rows, ((8, width), F32), ((8, width), F32)],
        specs=[SMEM] + [VMEM] * 8,
    )
    out_total = call(
        add_three_kernel,
        (grad_out[0], out_one, out_three),
        [((2 * quarter, width), BF16)],
        gate=(received_first,),
    )[0]
    out_across = send(out_total, SWAP_X)
    zero, one = call(
        add_split_last_kernel,
        (keep_first, received_first, attn_two),
        [((piece, width), BF16)] * 2,
    )
    attn_one = send(one, DOWN_Z)
    in_total = add_last(in_pieces[0], in_one, in_three)
    gradient, heads, small = call(
        functools.partial(entry_back_kernel, rows),
        (valid, entry_near, entry_core, entry_y, stream, grad_middle)
        + (attention_norm_gain, power_sums),
        [wide_rows, ((8, width), F32), ((8, width), F32)],
        gate=(attn_three,),
        specs=[SMEM] + [VMEM] * 7,
    )

    def add_small(received, gate=()):
        return call(add_wide_kernel, (small, received), [(small.shape, F32)], gate=gate)[0]

    in_across, in_core = send(in_total, SWAP_X), send(in_total, SWAP_C)
    heads_after = send(jnp.concatenate([output_heads, heads]), PREVIOUS)
    small = add_small(send(small, SWAP_C), (in_core,))
    small_y = send(small, SWAP_Y)
    (out_whole,) = call(
        swapped_sum_kernel, (out_total, out_across), [((2 * quarter, width), BF16)]
    )
    out_core = send(out_whole, SWAP_C)
    attn_total = add_last(zero, attn_one, attn_three, (heads_after,))
    attn_across, attn_core = send(attn_total, SWAP_X), send(attn_total, SWAP_C)
    small = add_small(small_y, (out_core, attn_core))
    small_z = send(small, FLIP_Z[1])
    output_rows, gradient_rows = call(
        exit_kernel,
        (output, gradient, heads_after),
        [((rows, width), F32)] * 2,
        scratch=[pltpu.VMEM((half, width), F32)],
    )
    small = add_small(small_z, (in_across,))
    small_z = send(small, FLIP_Z[2])
    in_last = send(in_across, SWAP_C)
    (grad_w_mlp_out,) = call(
        mlp_out_gradient_kernel, (out_whole, out_core), [((hidden_local, width), F32)]
    )
    small = add_small(small_z, (attn_across,))
    small_x = send(small, SWAP_X)
    attn_last = send(attn_across, SWAP_C)
    (grad_w_mlp_in,) = call(
        mlp_in_gradient_kernel,
        (in_total, in_across, in_core, in_last),
        [((width, hidden_local), F32)],
    )
    attn_grads = call(
        attention_gradients_kernel,
        (attn_total, attn_across, attn_core, attn_last),
        [((2 * DH, width), F32)] * 4
        + [((2 * DH,), F32), ((2 * DH,), F32), ((hidden_local,), F32)],
    )
    *vectors, powers = call(
        sums_kernel, (small, small_x), [((width,), F32)] * 6 + [((2 * DH,), F32)]
    )
    stream_rms = jnp.sqrt(powers[:4] / (jnp.maximum(powers[4], 1.0) * D))
    return (
        output_rows,
        gradient_rows,
        attn_grads[0],
        attn_grads[1],
        attn_grads[2],
        attn_grads[4],
        attn_grads[5],
        attn_grads[3],
        vectors[0],
        grad_w_mlp_in,
        attn_grads[6],
        grad_w_mlp_out,
        vectors[1],
        vectors[2],
        vectors[3],
        vectors[4],
        vectors[5],
        stream_rms,
    )


def solution(mesh):
    in_specs = (
        P(("tok", "feat"), None),
        P("tok"),
        P(("tok", "feat"), None),
        P("feat", None),
        P("feat", None),
        P("feat", None),
        P("feat"),
        P("feat"),
        P("feat", None),
        P(),
        P(None, "feat"),
        P("feat"),
        P("feat", None),
        P(),
        P(),
        P(),
        P(),
        P(),
    )
    out_specs = (
        P(("tok", "feat"), None),
        P(("tok", "feat"), None),
        P("feat", None),
        P("feat", None),
        P("feat", None),
        P("feat"),
        P("feat"),
        P("feat", None),
        P(),
        P(None, "feat"),
        P("feat"),
        P("feat", None),
        P(),
        P(),
        P(),
        P(),
        P(),
        P(),
    )
    return jax.shard_map(
        on_device, mesh=mesh, in_specs=in_specs, out_specs=out_specs, check_vma=False
    )
```

```python
import functools

import jax
import jax.numpy as jnp
from jax import lax
from jax.experimental import pallas as pl
from jax.experimental.pallas import tpu as pltpu
from jax.sharding import PartitionSpec as P

D = 1024
DH = 64
SEQ = 577


EPSILON = 1e-05
SLOPE = 1.702


def gelu_slope(values):
    sigmoid = jax.nn.sigmoid(SLOPE * values)
    return sigmoid + SLOPE * values * sigmoid * (1.0 - sigmoid)


def column_sums(values):
    return jnp.sum(values.astype(jnp.float32), axis=0)


def split_heads(values):
    return values.reshape(values.shape[0], values.shape[1] // DH, DH)


def apply_layer_norm(values):
    center = jnp.mean(values, axis=1, keepdims=True)
    spread = jnp.mean(values * values, axis=1, keepdims=True) - center * center
    inverse_deviation = lax.rsqrt(spread + EPSILON)
    return ((values - center) * inverse_deviation, inverse_deviation)


def layer_norm_backward(normalized_gradient, centered_scaled, inverse_deviation, norm_gain):
    scaled_output = normalized_gradient * norm_gain.astype(jnp.float32)
    plain_output = jnp.mean(scaled_output, axis=1, keepdims=True)
    cross_term = jnp.mean(scaled_output * centered_scaled, axis=1, keepdims=True)
    return inverse_deviation * (scaled_output - plain_output - centered_scaled * cross_term)


def image_forward(blocks):
    query_img, key_img, value_img = blocks
    scale = DH ** (-0.5)
    query_heads = split_heads(query_img)
    key_heads = split_heads(key_img)
    value_heads = split_heads(value_img)
    scores = (
        jnp.einsum("qhd,khd->hqk", query_heads, key_heads, preferred_element_type=jnp.float32)
        * scale
    )
    top_score = jnp.max(scores, axis=-1, keepdims=True)
    weights = jnp.exp(scores - top_score)
    total = jnp.sum(weights, axis=-1, keepdims=True)
    probs = (weights / total).astype(jnp.bfloat16)
    mixed = jnp.einsum("hqk,khd->qhd", probs, value_heads, preferred_element_type=jnp.float32)
    log_total = top_score[..., 0] + jnp.log(total[..., 0])
    return (mixed.reshape(query_img.shape).astype(jnp.bfloat16), log_total)


def image_backward(blocks):
    query_img, key_img, value_img, grad_img, log_total = blocks
    scale = DH ** (-0.5)
    query_heads = split_heads(query_img)
    key_heads = split_heads(key_img)
    value_heads = split_heads(value_img)
    grad_heads = split_heads(grad_img)
    scores = (
        jnp.einsum("qhd,khd->hqk", query_heads, key_heads, preferred_element_type=jnp.float32)
        * scale
    )
    probs = jnp.exp(scores - log_total[..., None])
    probs_low = probs.astype(jnp.bfloat16)
    grad_probs = jnp.einsum(
        "qhd,khd->hqk", grad_heads, value_heads, preferred_element_type=jnp.float32
    )
    grad_value = jnp.einsum(
        "hqk,qhd->khd", probs_low, grad_heads, preferred_element_type=jnp.float32
    )
    inner = jnp.sum(probs * grad_probs, axis=-1, keepdims=True)
    grad_scores = (probs * (grad_probs - inner)).astype(jnp.bfloat16)
    grad_query = (
        jnp.einsum("hqk,khd->qhd", grad_scores, key_heads, preferred_element_type=jnp.float32)
        * scale
    )
    grad_key = (
        jnp.einsum("hqk,qhd->khd", grad_scores, query_heads, preferred_element_type=jnp.float32)
        * scale
    )
    shape_img = query_img.shape
    return (
        grad_query.reshape(shape_img).astype(jnp.bfloat16),
        grad_key.reshape(shape_img).astype(jnp.bfloat16),
        grad_value.reshape(shape_img).astype(jnp.bfloat16),
    )


def by_image(values, images):
    return values.reshape(images, values.shape[0] // images, values.shape[1])


def on_device_general(
    inputs,
    valid,
    cotangent,
    w_query,
    w_key,
    w_value,
    b_query,
    b_value,
    w_attn_out,
    b_attn_out,
    w_mlp_in,
    b_mlp_in,
    w_mlp_out,
    b_mlp_out,
    attention_norm_gain,
    attention_norm_shift,
    feedforward_norm_gain,
    feedforward_norm_shift,
):
    row_count, width = inputs.shape
    images = valid.shape[0]
    group_rows = images * SEQ
    parts = lax.axis_size("feat")
    extra = row_count * parts - group_rows
    width_local = w_query.shape[0]
    hidden_local = w_mlp_out.shape[0]
    global_rows = lax.axis_index("feat") * row_count + jnp.arange(row_count, dtype=jnp.int32)
    owner = global_rows // SEQ
    matches = (owner[:, None] == jnp.arange(images, dtype=jnp.int32)[None, :]).astype(jnp.float32)
    row_mask = jnp.sum(matches * valid.astype(jnp.float32)[None, :], axis=1)
    live = (global_rows < group_rows).astype(jnp.float32)[:, None]

    def padded(values):
        return jnp.pad(values, ((0, extra), (0, 0)))

    local_input_rows = inputs.astype(jnp.float32)
    first_centered_scaled, first_inverse_deviation = apply_layer_norm(local_input_rows)
    normalized_first = (
        first_centered_scaled * attention_norm_gain.astype(jnp.float32)
        + attention_norm_shift.astype(jnp.float32)
    ).astype(jnp.bfloat16)
    normed_full = lax.all_gather(normalized_first, "feat", axis=0, tiled=True)[:group_rows]
    w_qkv = jnp.concatenate([w_query, w_key, w_value], axis=0)
    projected = jnp.einsum("rd,cd->rc", normed_full, w_qkv, preferred_element_type=jnp.float32)
    queries = (projected[:, :width_local] + b_query.astype(jnp.float32)).astype(jnp.bfloat16)
    key_rows = projected[:, width_local : 2 * width_local].astype(jnp.bfloat16)
    value_rows = (projected[:, 2 * width_local :] + b_value.astype(jnp.float32)).astype(
        jnp.bfloat16
    )
    mixed, log_totals = lax.map(
        image_forward,
        (by_image(queries, images), by_image(key_rows, images), by_image(value_rows, images)),
    )
    mixed = mixed.reshape(group_rows, width_local)
    partial_out = jnp.dot(mixed, w_attn_out, preferred_element_type=jnp.float32)
    attn = lax.psum_scatter(
        padded(partial_out), "feat", scatter_dimension=0, tiled=True
    ) + b_attn_out.astype(jnp.float32)
    middle_state = local_input_rows + attn
    second_centered_scaled, second_inverse_deviation = apply_layer_norm(middle_state)
    normalized_middle = (
        second_centered_scaled * feedforward_norm_gain.astype(jnp.float32)
        + feedforward_norm_shift.astype(jnp.float32)
    ).astype(jnp.bfloat16)
    mid_full = lax.all_gather(normalized_middle, "feat", axis=0, tiled=True)[:group_rows]
    hidden = jnp.dot(mid_full, w_mlp_in, preferred_element_type=jnp.float32) + b_mlp_in.astype(
        jnp.float32
    )
    active = (hidden * jax.nn.sigmoid(SLOPE * hidden)).astype(jnp.bfloat16)
    partial_mlp = jnp.dot(active, w_mlp_out, preferred_element_type=jnp.float32)
    branch = lax.psum_scatter(
        padded(partial_mlp).astype(jnp.bfloat16), "feat", scatter_dimension=0, tiled=True
    ).astype(jnp.float32) + b_mlp_out.astype(jnp.float32)
    output = (middle_state + branch) * live
    output_gradient = cotangent.astype(jnp.float32) * row_mask[:, None]
    grad_branch = output_gradient.astype(jnp.bfloat16)
    grad_b_mlp_out = column_sums(grad_branch)
    branch_full = lax.all_gather(grad_branch, "feat", axis=0, tiled=True)[:group_rows]
    grad_w_mlp_out = jnp.einsum(
        "rf,rd->fd", active, branch_full, preferred_element_type=jnp.float32
    )
    grad_active = jnp.einsum(
        "rd,fd->rf", branch_full, w_mlp_out, preferred_element_type=jnp.float32
    )
    grad_hidden = (grad_active * gelu_slope(hidden)).astype(jnp.bfloat16)
    grad_b_mlp_in = column_sums(grad_hidden)
    grad_mlp_in_rows = jnp.einsum(
        "rf,rd->fd", grad_hidden, mid_full, preferred_element_type=jnp.float32
    )
    partial_mid = jnp.einsum("rf,df->rd", grad_hidden, w_mlp_in, preferred_element_type=jnp.float32)
    midpoint_gradient = lax.psum_scatter(
        padded(partial_mid), "feat", scatter_dimension=0, tiled=True
    )
    feedforward_gain_gradient = jnp.sum(midpoint_gradient * second_centered_scaled, axis=0)
    grad_s_mlp = jnp.sum(midpoint_gradient, axis=0)
    middle_state_gradient = output_gradient + layer_norm_backward(
        midpoint_gradient, second_centered_scaled, second_inverse_deviation, feedforward_norm_gain
    )
    grad_attn = middle_state_gradient.astype(jnp.bfloat16)
    grad_b_attn_out = column_sums(grad_attn)
    attn_full = lax.all_gather(grad_attn, "feat", axis=0, tiled=True)[:group_rows]
    grad_w_attn_out = jnp.einsum("rh,rd->hd", mixed, attn_full, preferred_element_type=jnp.float32)
    grad_mixed = jnp.einsum(
        "rd,hd->rh", attn_full, w_attn_out, preferred_element_type=jnp.float32
    ).astype(jnp.bfloat16)
    grad_query, grad_key, grad_value = lax.map(
        image_backward,
        (
            by_image(queries, images),
            by_image(key_rows, images),
            by_image(value_rows, images),
            by_image(grad_mixed, images),
            log_totals,
        ),
    )
    grad_query = grad_query.reshape(group_rows, width_local)
    grad_key = grad_key.reshape(group_rows, width_local)
    grad_value = grad_value.reshape(group_rows, width_local)
    grad_b_query = column_sums(grad_query)
    grad_b_value = column_sums(grad_value)
    grad_qkv = jnp.concatenate([grad_query, grad_key, grad_value], axis=1)
    grad_w_qkv = jnp.einsum("rc,rd->cd", grad_qkv, normed_full, preferred_element_type=jnp.float32)
    partial_in = jnp.einsum("rc,cd->rd", grad_qkv, w_qkv, preferred_element_type=jnp.float32)
    normalized_gradient = lax.psum_scatter(
        padded(partial_in).astype(jnp.bfloat16), "feat", scatter_dimension=0, tiled=True
    ).astype(jnp.float32)
    attention_gain_gradient = jnp.sum(normalized_gradient * first_centered_scaled, axis=0)
    grad_s_attn = jnp.sum(normalized_gradient, axis=0)
    layer_input_gradient = middle_state_gradient + layer_norm_backward(
        normalized_gradient, first_centered_scaled, first_inverse_deviation, attention_norm_gain
    )
    local_powers = jnp.stack(
        [
            jnp.sum(row_mask[:, None] * local_input_rows * local_input_rows),
            jnp.sum(row_mask[:, None] * attn * attn),
            jnp.sum(row_mask[:, None] * branch * branch),
            jnp.sum(row_mask[:, None] * output * output),
        ]
    )
    local_count = jnp.sum(row_mask)
    bias_entries = jnp.concatenate([grad_b_query, grad_b_value, grad_b_mlp_in])
    bias_row = jnp.pad(bias_entries, (0, width - bias_entries.shape[0]))[None, :]
    packed = jnp.concatenate(
        [grad_w_qkv, grad_w_attn_out, grad_mlp_in_rows, grad_w_mlp_out, bias_row], axis=0
    )
    packed_rows = packed.shape[0]
    tok_parts = lax.axis_size("tok")
    fill_rows = (tok_parts - packed_rows % tok_parts) % tok_parts
    packed = jnp.pad(packed, ((0, fill_rows), (0, 0)))
    shares = lax.psum_scatter(
        packed.astype(jnp.bfloat16), "tok", scatter_dimension=0, tiled=True
    ).astype(jnp.float32)
    summed = lax.all_gather(shares.astype(jnp.bfloat16), "tok", axis=0, tiled=True).astype(
        shares.dtype
    )[:packed_rows]
    offset = 0
    grad_w_query = summed[offset : offset + width_local]
    offset += width_local
    grad_w_key = summed[offset : offset + width_local]
    offset += width_local
    grad_w_value = summed[offset : offset + width_local]
    offset += width_local
    grad_w_attn_out = summed[offset : offset + width_local]
    offset += width_local
    grad_w_mlp_in = summed[offset : offset + hidden_local].T
    offset += hidden_local
    grad_w_mlp_out = summed[offset : offset + hidden_local]
    offset += hidden_local
    bias_sums = summed[offset]
    grad_b_query = bias_sums[:width_local]
    grad_b_value = bias_sums[width_local : 2 * width_local]
    grad_b_mlp_in = bias_sums[2 * width_local : 2 * width_local + hidden_local]
    (
        grad_b_attn_out,
        grad_b_mlp_out,
        attention_gain_gradient,
        grad_s_attn,
        feedforward_gain_gradient,
        grad_s_mlp,
        powers,
        counted,
    ) = lax.psum(
        (
            grad_b_attn_out,
            grad_b_mlp_out,
            attention_gain_gradient,
            grad_s_attn,
            feedforward_gain_gradient,
            grad_s_mlp,
            local_powers,
            local_count,
        ),
        ("tok", "feat"),
    )
    stream_rms = jnp.sqrt(powers / (jnp.maximum(counted, 1.0) * D))
    return (
        output,
        layer_input_gradient,
        grad_w_query,
        grad_w_key,
        grad_w_value,
        grad_b_query,
        grad_b_value,
        grad_w_attn_out,
        grad_b_attn_out,
        grad_w_mlp_in,
        grad_b_mlp_in,
        grad_w_mlp_out,
        grad_b_mlp_out,
        attention_gain_gradient,
        grad_s_attn,
        feedforward_gain_gradient,
        grad_s_mlp,
        stream_rms,
    )


BF16 = jnp.bfloat16
F32 = jnp.float32
AXES = ("tok", "feat")
SLOTS = (0, 1, 3, 2)
PAIRS = ((0, 1), (3, 2))
CHUNK = 16
PART = DH // 2


SPANS = {
    0: 6,
    1: 1,
    2: 0.01,
    3: 30,
    4: 1,
    6: 60,
    7: 6,
    8: 0.01,
    11: 6,
    15: 0.01,
    18: 10,
    19: 0.01,
    23: 0.01,
    24: 6,
    25: 0.01,
    27: 60,
    28: 3,
    29: 3,
    30: 3,
    33: 1,
    34: 3,
    35: 0.01,
    36: 0.01,
    37: 10,
    39: 0.01,
    40: 10,
    44: 1,
    45: 0.01,
    46: 0.01,
}
EARLY = {
    4: (6,),
    7: (2,),
    8: (6,),
    10: (11,),
    13: (15,),
    14: (21,),
    18: (25,),
    20: (26,),
    25: (33,),
    27: (36,),
    31: (39,),
    36: (45,),
    37: (46,),
    38: (52,),
    39: (51,),
    42: (52,),
    43: (58,),
    44: (55,),
    46: (52,),
}
LATE = {
    4: (1, 0),
    13: (1,),
    14: (0,),
    29: (0,),
    32: (0,),
    37: (1, 0),
}


def route(move):
    found = []
    for tok in range(4):
        for feat in range(8):
            target = move(tok // 2, tok % 2, feat // 2, feat % 2)
            if target is not None:
                x, c, z, y = target
                found.append((tok * 8 + feat, (2 * x + c) * 8 + 2 * z + y))
    return found


SWAP_X = route(lambda x, c, z, y: (1 - x, c, z, y))
SWAP_C = route(lambda x, c, z, y: (x, 1 - c, z, y))
SWAP_Y = route(lambda x, c, z, y: (x, c, z, 1 - y))
UP_Z = route(lambda x, c, z, y: (x, c, (z + 1) % 4, y))
DOWN_Z = route(lambda x, c, z, y: (x, c, (z + 3) % 4, y))
FLIP_Z = [route(lambda x, c, z, y, s=s: (x, c, z ^ s, y)) for s in range(4)]
NEXT = [(t * 8 + f, t * 8 + f + 1) for t in range(4) for f in range(7)]
PREVIOUS = [(t * 8 + f + 1, t * 8 + f) for t in range(4) for f in range(7)]


def nt(left, right):
    return lax.dot_general(left, right, (((1,), (1,)), ((), ())), preferred_element_type=F32)


def nn(left, right):
    return lax.dot_general(left, right, (((1,), (0,)), ((), ())), preferred_element_type=F32)


def tn(left, right):
    return lax.dot_general(left, right, (((0,), (0,)), ((), ())), preferred_element_type=F32)


SMEM = pl.BlockSpec(memory_space=pltpu.SMEM)
HBM = pl.BlockSpec(memory_space=pltpu.HBM)
VMEM = pl.BlockSpec(memory_space=pltpu.VMEM)


def kernel_call(body, operands, specs, outs, scratch=(), after=(), span=0.01, vmem=12):
    count, extra = len(operands), len(after)

    def kernel(*refs):
        body(*refs[:count], *refs[count + extra :])

    return pl.pallas_call(
        kernel,
        in_specs=list(specs) + [VMEM] * extra,
        out_specs=[VMEM] * len(outs),
        out_shape=[jax.ShapeDtypeStruct(shape, dtype) for shape, dtype in outs],
        scratch_shapes=list(scratch),
        compiler_params=pltpu.CompilerParams(
            vmem_limit_bytes=vmem * 2**20, fuse_transposed_lhs_in_matmul=True
        ),
        cost_estimate=pl.CostEstimate(
            flops=int(span * 1e9), bytes_accessed=2**16, transcendentals=0
        ),
    )(*operands, *after)


def coordinates():
    tok, feat = lax.axis_index("tok"), lax.axis_index("feat")
    return tok // 2, tok % 2, feat // 2, feat % 2


def chunks(half):
    return [slice(at, at + CHUNK) for at in range(0, half, CHUNK)]


def row_of(vector):
    return vector[...].astype(F32).reshape(1, vector.shape[0])


def folded(values):
    return values[:8] + values[8:]


def moment_norm(values):
    center = jnp.mean(values, axis=1, keepdims=True)
    spread = jnp.mean(values * values, axis=1, keepdims=True) - center * center
    inverse = lax.rsqrt(spread + EPSILON)
    return (values - center) * inverse, inverse


def attention_weights_kernel(wq, wk, wv, wo, b_query, b_value, b_hidden, *refs):
    own, other, both, query, value, hidden, sems = refs
    piece = own.shape[0]
    x, c, _, _ = coordinates()
    width = own.shape[1]
    copies = []
    for source, target in ((b_query, query), (b_value, value), (b_hidden, hidden)):
        copies.append(pltpu.make_async_copy(source, target, sems.at[len(copies)]))
    targets = ((own, 0, x), (other, 0, 1 - x), (both, 0, x), (both, piece, 1 - x))
    for out, first, side in targets:
        at = pl.multiple_of(c * DH + side * PART, PART)
        for m, w in enumerate((wq, wk, wv, wo)):
            copies.append(
                pltpu.make_async_copy(
                    w.at[pl.ds(at, PART)], out.at[pl.ds(first + m * PART, PART)], sems.at[len(copies)]
                )
            )
    for copy in copies:
        copy.start()
    for copy in copies[:3]:
        copy.wait()
    parts = [row_of(vector) for vector in (query, value, hidden)]
    taken = sum(part.shape[1] for part in parts)
    bias = jnp.concatenate(parts + [jnp.zeros((1, width - taken), F32)], axis=1)
    bias = jnp.broadcast_to(bias, (16, width)).astype(BF16)
    for out, first, _ in targets:
        out[first + 4 * PART : first + piece, :] = bias
    for copy in copies[3:]:
        copy.wait()


def edge_kernel(inputs, cotangent, edge):
    rows = inputs.shape[0]
    at = (rows - 8) // 16 * 16
    for i, values in enumerate((inputs, cotangent)):
        edge[8 * i : 8 * i + 8, :] = values[at:, :].astype(F32)[rows - 8 - at :].astype(BF16)


def mlp_weights_kernel(w_in, w_out, own, other, both):
    x, c, _, _ = coordinates()
    quarter = own.shape[0] // 2
    for out, first, side in ((own, 0, x), (other, 2 * quarter, 1 - x)):
        at = pl.multiple_of((2 * c + side) * quarter, quarter)
        found = w_in[:, pl.ds(at, quarter)].T
        rest = w_out[pl.ds(at, quarter), :]
        out[:quarter, :] = found
        out[quarter:, :] = rest
        both[first : first + quarter, :] = found
        both[first + quarter : first + 2 * quarter, :] = rest


def halves_of(refs, count):
    own_zero, other_zero, own_one, other_one, both, own_two, other_two = refs
    own = [own_zero, own_one, both.at[pl.ds(0, count)], own_two]
    return own, [other_zero, other_one, both.at[pl.ds(count, count)], other_two]


def entry_kernel(
    valid, inputs, cotangent, edge, gain_vector, shift_vector, stream, normed, branch, again, ext
):
    _, _, z, y = coordinates()
    rows = inputs.shape[0]
    half = stream.shape[0]
    gain, shift = row_of(gain_vector), row_of(shift_vector)
    flag = valid[z].astype(F32)

    def aligned(at):
        found = pltpu.roll(ext[at.start : at.stop + 8, :], CHUNK + z, 0)[:CHUNK]
        index = at.start + lax.broadcasted_iota(jnp.int32, (CHUNK, 1), 0)
        return jnp.where(index < rows - y, found, 0.0)

    def fill(values, first):
        ext[0:8, :] = edge[...].astype(F32)[first : first + 8]
        ext[8 : 8 + rows, :] = values[...].astype(F32)

    fill(inputs, 0)
    for at in chunks(half):
        found = aligned(at)
        stream[at, :] = found.astype(BF16)
        hat, _ = moment_norm(found)
        normed[at, :] = (hat * gain + shift).astype(BF16)
    fill(cotangent, 8)
    for at in chunks(half):
        branch[at, :] = (aligned(at) * flag).astype(BF16)
        again[at, :] = branch[at, :]


def softmax_columns(scores):
    top = jnp.max(scores, axis=0, keepdims=True)
    weights = jnp.exp(scores - top)
    return weights * (1.0 / jnp.sum(weights, axis=0, keepdims=True))


def pair_forward(rows, halves, w_in, bias, qkv, probs, mixed):
    half = halves[0].shape[0]
    _, _, _, y = coordinates()
    lanes = 2 * DH
    entry = jnp.concatenate([halves[0][...], halves[1][...]], axis=0)
    qkv[...] = (nt(entry, w_in) + bias).astype(BF16)
    key_index = lax.broadcasted_iota(jnp.int32, (2 * half, 1), 0)
    first = rows - y
    second = half + rows - 1 + y
    real = (key_index < first) | ((key_index >= half) & (key_index < second))
    penalty = jnp.where(real, 0.0, -1e30)
    outs = []
    for h in range(2):
        q = qkv[:, h * DH : (h + 1) * DH] * jnp.asarray(DH ** (-0.5), BF16)
        k = qkv[:, lanes + h * DH : lanes + (h + 1) * DH]
        v = qkv[:, 2 * lanes + h * DH : 2 * lanes + (h + 1) * DH]
        found = softmax_columns(nt(k, q) + penalty).astype(BF16)
        probs[h] = found
        outs.append(tn(v, found))
    mixed[...] = jnp.concatenate(outs, axis=0).T.astype(BF16)


def pair_weights(own, other, w_in, w_out):
    for m in range(4):
        target = w_out if m == 3 else w_in
        for i in range(2):
            at = (0 if m == 3 else m * 2 * DH) + i * DH
            target[at : at + PART, :] = own[i][m * PART : (m + 1) * PART, :]
            target[at + PART : at + DH, :] = other[i][m * PART : (m + 1) * PART, :]
    rows_of = [own[i][4 * PART : 4 * PART + 16, :].astype(F32)[0:1] for i in range(2)]
    query = jnp.concatenate([ordered_bias(r, 0) for r in rows_of], axis=1)
    value = jnp.concatenate([ordered_bias(r, 2 * DH) for r in rows_of], axis=1)
    return jnp.concatenate([query, jnp.zeros_like(query), value], axis=1)


def projected(first_mixed, second_mixed, first_out, second_out, outs):
    mixed = jnp.concatenate([first_mixed[...], second_mixed[...]], axis=1)
    weights = jnp.concatenate([first_out[...], second_out[...]], axis=0)
    found = nn(mixed, weights).astype(BF16)
    at = 0
    for out in outs:
        out[...] = found[at : at + out.shape[0]]
        at += out.shape[0]


def ordered_bias(row, first):
    x, c, _, _ = coordinates()
    block = jnp.where(c == 0, row[:, first : first + DH], row[:, first + DH : first + 2 * DH])
    swapped = jnp.concatenate([block[:, PART:], block[:, :PART]], axis=1)
    return jnp.where(x == 0, block, swapped)


def first_pair_kernel(rows, near, far, near_other, far_other, *refs):
    own_zero, other_zero, own_one, other_one, *refs = refs
    qkv_own, qkv_other, probs_own, probs_other, mixed_own, mixed_other, w_in, w_out = refs
    bias = pair_weights((own_zero, own_one), (other_zero, other_one), w_in, w_out)
    weights = w_in[...]
    pair_forward(rows, (near_other, far_other), weights, bias, qkv_other, probs_other, mixed_other)
    pair_forward(rows, (near, far), weights, bias, qkv_own, probs_own, mixed_own)


def second_pair_other_kernel(rows, near, far, both, own_two, other_two, *refs):
    first_mixed, first_out, qkv, probs, mixed, partial, w_in, w_out, bias = refs
    piece = own_two.shape[0]
    own = (both.at[pl.ds(0, piece)], own_two)
    other = (both.at[pl.ds(piece, piece)], other_two)
    found = pair_weights(own, other, w_in, w_out)
    bias[...] = jnp.broadcast_to(found, bias.shape)
    pair_forward(rows, (near, far), w_in[...], found, qkv, probs, mixed)
    projected(first_mixed, mixed, first_out, w_out, (partial,))


def second_pair_own_kernel(rows, near, far, w_in, w_out, bias, first_mixed, first_out, *refs):
    qkv, probs, mixed, *partials = refs
    pair_forward(rows, (near, far), w_in[...], bias[0:1, :], qkv, probs, mixed)
    projected(first_mixed, mixed, first_out, w_out, partials)


def joined_rows(refs, at):
    size = refs[0].shape[0]
    if at.start < size:
        return refs[0][at, :]
    return refs[1][at.start - size : at.stop - size, :]


def real_rows(at, rows, y):
    return at.start + lax.broadcasted_iota(jnp.int32, (CHUNK, 1), 0) < rows - y


def middle_kernel(
    rows,
    valid,
    partial,
    from_core,
    from_y_first,
    from_y_second,
    stream,
    bias_vector,
    gain_vector,
    shift_vector,
    middle,
    normed,
    powers,
):
    _, _, z, y = coordinates()
    bias, gain, shift = row_of(bias_vector), row_of(gain_vector), row_of(shift_vector)
    total = jnp.zeros((8, middle.shape[1]), F32)
    for at in chunks(middle.shape[0]):
        from_y = joined_rows((from_y_first, from_y_second), at)
        attn = partial[at, :].astype(F32) + from_core[at, :].astype(F32)
        attn = attn + from_y.astype(F32) + bias
        found = stream[at, :].astype(F32) + attn
        middle[at, :] = found
        hat, _ = moment_norm(found)
        normed[at, :] = (hat * gain + shift).astype(BF16)
        total = total + folded(jnp.where(real_rows(at, rows, y), attn * attn, 0.0))
    powers[...] = total * valid[z].astype(F32)


def mlp_kernel(near, far, grad_near, grad_far, *refs):
    own, other = halves_of(refs[:7], refs[0].shape[0])
    bias_of, refs = refs[7:11], refs[11:]
    active, grad_hidden, mid_near, mid_far, out_near, out_far, sums = refs
    x, c, _, _ = coordinates()
    half = near.shape[0]
    quarter = own[0].shape[0] // 2
    w_in = [ref[:quarter, :] for side in (own, other) for ref in side]
    w_out = [ref[quarter:, :] for side in (own, other) for ref in side]
    bias = []
    for side in (x, 1 - x):
        at = pl.multiple_of(4 * DH + (2 * c + side) * quarter, quarter)
        for k in range(4):
            bias.append(bias_of[k][4 * PART :, pl.ds(at, quarter)].astype(F32)[0:1])
    bias = jnp.concatenate(bias, axis=1)
    rows = jnp.concatenate([near[...], far[...]], axis=0)
    grads = jnp.concatenate([grad_near[...], grad_far[...]], axis=0)
    size = 2 * quarter
    for n in range(4):
        at = slice(n * size, (n + 1) * size)
        pair = slice(2 * n, 2 * n + 2)
        u = nt(rows, jnp.concatenate(w_in[pair], axis=0)) + bias[:, at]
        gate = jax.nn.sigmoid(SLOPE * u)
        act = u * gate
        active[:, at] = act.astype(BF16)
        slope = gate + SLOPE * act * (1.0 - gate)
        found = (nt(grads, jnp.concatenate(w_out[pair], axis=0)) * slope).astype(BF16)
        grad_hidden[:, at] = found
        sums[:, at] = jnp.broadcast_to(
            jnp.sum(found.astype(F32), axis=0, keepdims=True), (8, size)
        )
    found = nn(grad_hidden[...], jnp.concatenate(w_in, axis=0)).astype(BF16)
    mid_near[...] = found[:half]
    mid_far[...] = found[half:]
    found = nn(active[...], jnp.concatenate(w_out, axis=0)).astype(BF16)
    out_near[...] = found[:half]
    out_far[...] = found[half:]


def products_kernel(split, left_first, left_second, *refs):
    pieces, outs = refs[:4], refs[4:]
    right = jnp.concatenate([piece[...] for piece in pieces], axis=0)
    hidden = left_first.shape[1] // 2
    quarter = hidden // 4
    for side in (1, 0):
        at = slice(side * hidden, (side + 1) * hidden)
        left = jnp.concatenate([left_first[:, at], left_second[:, at]], axis=0)
        found = tn(left, right).astype(BF16)
        if split:
            for k in range(4):
                outs[k][side * quarter : (side + 1) * quarter, :] = found[
                    k * quarter : (k + 1) * quarter
                ]
        else:
            outs[side][...] = found


def far_sum_kernel(values, received, *outs):
    first = received.shape[0] - values.shape[0]
    done = 0
    for out in outs:
        for at in chunks(out.shape[0]):
            source = slice(done + at.start, done + at.stop)
            moved = slice(first + source.start, first + source.stop)
            found = values[source, :].astype(F32) + received[moved, :].astype(F32)
            out[at, :] = found.astype(BF16)
        done += out.shape[0]


def add_split_kernel(keep, received, *outs):
    at = 0
    for out in outs:
        size = out.shape[0]
        out[...] = (
            keep[at : at + size, :].astype(F32) + received[at : at + size, :].astype(F32)
        ).astype(BF16)
        at += size


def output_kernel(
    rows,
    valid,
    partial,
    from_core,
    from_y,
    middle,
    stream,
    bias_vector,
    attn_power,
    sums,
    output,
    heads,
    small,
):
    _, _, z, y = coordinates()
    bias = row_of(bias_vector)
    width = middle.shape[1]
    totals = [jnp.zeros((8, width), F32) for _ in range(3)]
    for at in chunks(middle.shape[0]):
        branch = partial[at, :].astype(F32) + from_core[at, :].astype(F32)
        branch = branch + from_y[at, :].astype(F32) + bias
        found = middle[at, :] + branch
        output[at, :] = found
        entry = stream[at, :].astype(F32)
        real = real_rows(at, rows, y)
        for i, v in enumerate((entry, branch, found)):
            totals[i] = totals[i] + folded(jnp.where(real, v * v, 0.0))
    heads[...] = output[0:8, :]
    flag = valid[z]
    lane = lax.broadcasted_iota(jnp.int32, (1, width), 1)
    entry = jnp.where(lane == 4, (flag * (rows - y)).astype(F32), 0.0)
    powers = [totals[0] * flag.astype(F32), attn_power[...]]
    powers += [total * flag.astype(F32) for total in totals[1:]]
    for i, power in enumerate(powers):
        whole = jnp.sum(jnp.sum(power, axis=0, keepdims=True), axis=1, keepdims=True)
        entry = entry + jnp.where(lane == i, whole, 0.0)
    row = lax.broadcasted_iota(jnp.int32, (8, 1), 0)
    small[...] = jnp.where(row == 6, entry, sums[...])


def norm_back(grad, hat, inverse, gain):
    scaled = grad * gain
    plain = jnp.mean(scaled, axis=1, keepdims=True)
    cross = jnp.mean(scaled * hat, axis=1, keepdims=True)
    return inverse * (scaled - plain - hat * cross)


def middle_back_kernel(
    partial, from_core, from_y, middle, branch, gain_vector, grad, low, sums
):
    width = middle.shape[1]
    gain = row_of(gain_vector)
    totals = [jnp.zeros((8, width), F32) for _ in range(4)]
    for at in chunks(middle.shape[0]):
        found = partial[at, :].astype(F32) + from_core[at, :].astype(F32)
        found = found + from_y[at, :].astype(F32)
        hat, inverse = moment_norm(middle[at, :])
        gy = branch[at, :].astype(F32)
        total = gy + norm_back(found, hat, inverse, gain)
        grad[at, :] = total
        rounded = total.astype(BF16)
        low[at, :] = rounded
        for i, v in enumerate((rounded.astype(F32), gy, found * hat, found)):
            totals[i] = totals[i] + folded(v)
    sums[...] = jnp.concatenate(
        [jnp.sum(v, axis=0, keepdims=True) for v in totals] + [jnp.zeros((4, width), F32)], axis=0
    )


def backward_kernel(pair, *refs):
    grads, normed, refs = refs[:4], refs[4:8], refs[8:]
    w_out, qkv_own, qkv_other, probs_own, probs_other = refs[:5]
    mixed_own, mixed_other, sums_chip, sums_distant = refs[5:9]
    out_own, out_other, give, keep = refs[9:]
    half = grads[0].shape[0]
    rows = 2 * half
    lanes = 2 * DH
    scale = jnp.asarray(DH ** (-0.5), BF16)
    grad_rows = jnp.concatenate([ref[...] for ref in grads], axis=0)
    wide = nt(grad_rows, w_out[...]).astype(BF16)
    hidden_sums = sums_chip[0:1, :] + sums_distant[0:1, :]
    totals = []
    images = ((qkv_own, probs_own, out_own), (qkv_other, probs_other, out_other))
    for image, (qkv, probs, out) in enumerate(images):
        dq, dk, dv = [], [], []
        for h in range(2):
            at = h * DH
            q = qkv[:, at : at + DH] * scale
            k = qkv[:, lanes + at : lanes + at + DH] * scale
            v = qkv[:, 2 * lanes + at : 2 * lanes + at + DH]
            g = wide[image * rows : (image + 1) * rows, h * DH : (h + 1) * DH]
            found = probs[h]
            grad_probs = nt(v, g)
            scores = found.astype(F32)
            product = scores * grad_probs
            inner = jnp.sum(product, axis=0, keepdims=True)
            grad_scores = (product - scores * inner).astype(BF16)
            dv.append(nn(found, g))
            dk.append(nn(grad_scores, q))
            dq.append(tn(k, grad_scores))
        query = jnp.concatenate(dq, axis=0).T.astype(BF16)
        value = jnp.concatenate(dv, axis=1).astype(BF16)
        out[:, :lanes] = query
        out[:, lanes : 2 * lanes] = jnp.concatenate(dk, axis=1).astype(BF16)
        out[:, 2 * lanes :] = value
        totals.append(
            [jnp.sum(v.astype(F32), axis=0, keepdims=True) for v in (query, value)]
        )
    query_sum, value_sum = (totals[0][i] + totals[1][i] for i in range(2))
    stacked = jnp.concatenate([out_own[...], out_other[...]], axis=0)
    grad_w = tn(stacked, jnp.concatenate([ref[...] for ref in normed], axis=0)).astype(BF16)
    mixed = jnp.concatenate([mixed_own[...], mixed_other[...]], axis=0)
    grad_o = tn(mixed, grad_rows).astype(BF16)
    size = 4 * PART + 16
    quarter = hidden_sums.shape[1] // 8
    width = give.shape[1]
    for side, out in enumerate((keep, give)):
        for i in range(2):
            for m in range(4):
                source = grad_o if m == 3 else grad_w
                at = (0 if m == 3 else m * lanes) + i * DH + side * PART
                out[i * size + m * PART : i * size + (m + 1) * PART, :] = source[at : at + PART]
            at = i * DH + side * PART
            block = (side * 4 + 2 * pair + i) * quarter
            row = jnp.concatenate(
                [
                    query_sum[:, at : at + PART],
                    value_sum[:, at : at + PART],
                    jnp.zeros((1, DH), F32),
                    hidden_sums[:, block : block + quarter],
                    jnp.zeros((1, width - lanes - quarter), F32),
                ],
                axis=1,
            )
            out[i * size + 4 * PART : (i + 1) * size, :] = jnp.broadcast_to(row, (16, width)).astype(
                BF16
            )


def entry_product_kernel(first_pair, second_pair, first_weights, second_weights, *outs):
    joined = jnp.concatenate([first_pair[...], second_pair[...]], axis=1)
    weights = jnp.concatenate([first_weights[...], second_weights[...]], axis=0)
    found = nn(joined, weights).astype(BF16)
    at = 0
    for out in outs:
        out[...] = found[at : at + out.shape[0]]
        at += out.shape[0]


def entry_back_kernel(
    rows,
    valid,
    partial,
    from_core,
    from_y,
    stream,
    grad_middle,
    gain_vector,
    middle_sums,
    grad,
    heads,
    small,
):
    width = stream.shape[1]
    gain = row_of(gain_vector)
    totals = [jnp.zeros((8, width), F32) for _ in range(2)]
    for at in chunks(stream.shape[0]):
        found = partial[at, :].astype(F32) + from_core[at, :].astype(F32)
        found = found + from_y[at, :].astype(F32)
        hat, inverse = moment_norm(stream[at, :].astype(F32))
        grad[at, :] = grad_middle[at, :] + norm_back(found, hat, inverse, gain)
        for i, v in enumerate((found * hat, found)):
            totals[i] = totals[i] + folded(v)
    heads[...] = grad[0:8, :]
    small[...] = jnp.concatenate(
        [middle_sums[0:2, :]]
        + [jnp.sum(v, axis=0, keepdims=True) for v in totals]
        + [middle_sums[2:4, :], middle_sums[6:8, :]],
        axis=0,
    )


def exit_kernel(output, grad, after, output_rows, grad_rows, ext):
    _, _, z, y = coordinates()
    half = output.shape[0]
    rows = output_rows.shape[0]
    count = rows - y
    index = lax.broadcasted_iota(jnp.int32, (half, 1), 0)
    ext[8:, :] = jnp.zeros((half - 8, ext.shape[1]), F32)
    for values, at, out in ((output, 0, output_rows), (grad, 8, grad_rows)):
        ext[0:8, :] = after[at : at + 8, :]
        moved = pltpu.roll(values[...], half - z, 0)
        beyond = pltpu.roll(ext[...], count - z, 0)
        out[...] = jnp.where(index < count - z, moved, beyond)[:rows]


def attention_gradients_kernel(own, across, core, core_across, *outs):
    x, c, _, _ = coordinates()
    query, value, hidden = outs[4:]
    pieces = ((own, c, x), (across, c, 1 - x), (core, 1 - c, x), (core_across, 1 - c, 1 - x))
    for ref, c_of, x_of in pieces:
        at = pl.multiple_of(c_of * DH + x_of * PART, PART)
        for m in range(4):
            outs[m][pl.ds(at, PART), :] = ref[m * PART : (m + 1) * PART, :].astype(F32)
    rows = [ref[4 * PART :, :].astype(F32)[0:1] for ref, _, _ in pieces]
    natural = []
    for c_of in range(2):
        for x_of in range(2):
            same = jnp.where(x == x_of, rows[0], rows[1])
            changed = jnp.where(x == x_of, rows[2], rows[3])
            natural.append(jnp.where(c == c_of, same, changed))
    quarter = hidden.shape[0] // 4
    for out, at, size in ((query, 0, PART), (value, PART, PART), (hidden, 2 * DH, quarter)):
        found = jnp.concatenate([row[:, at : at + size] for row in natural], axis=1)
        out[...] = found.reshape(out.shape)


def mlp_in_gradient_kernel(own, across, core, core_across, out):
    x, c, _, _ = coordinates()
    pieces = ((own, c, x), (across, c, 1 - x), (core, 1 - c, x), (core_across, 1 - c, 1 - x))
    for ref, c_of, x_of in pieces:
        quarter = ref.shape[0]
        at = pl.multiple_of((2 * c_of + x_of) * quarter, quarter)
        out[:, pl.ds(at, quarter)] = ref[...].astype(F32).T


def swapped_sum_kernel(own, received, out):
    size = own.shape[0] // 2
    out[:size, :] = (own[:size, :].astype(F32) + received[size:, :].astype(F32)).astype(BF16)
    out[size:, :] = (own[size:, :].astype(F32) + received[:size, :].astype(F32)).astype(BF16)


def mlp_out_gradient_kernel(own, core, out):
    x, c, _, _ = coordinates()
    for ref, c_of in ((own, c), (core, 1 - c)):
        quarter = ref.shape[0] // 2
        for i, side in enumerate((x, 1 - x)):
            at = pl.multiple_of((2 * c_of + side) * quarter, quarter)
            out[pl.ds(at, quarter), :] = ref[i * quarter : (i + 1) * quarter, :].astype(F32)


def sums_kernel(small, received, *outs):
    found = small[...] + received[...]
    for i, out in enumerate(outs[:-1]):
        out[...] = found[i : i + 1].reshape(out.shape)
    outs[-1][...] = found[6:7, : outs[-1].shape[0]].reshape(outs[-1].shape)


def copy_kernel(source, target):
    target[...] = source[...]


def add_wide_kernel(first, second, out):
    out[...] = first[...] + second[...]


def add_split_last_kernel(keep, received, last, zero, one):
    size = zero.shape[0]
    zero[...] = (keep[:size, :].astype(F32) + received[:size, :].astype(F32)).astype(BF16)
    found = keep[size:, :].astype(F32) + received[size:, :].astype(F32)
    one[...] = (found + last[...].astype(F32)).astype(BF16)


def add_three_kernel(first, second, third, out):
    out[...] = (
        first[...].astype(F32) + second[...].astype(F32) + third[...].astype(F32)
    ).astype(BF16)


def on_device(
    inputs,
    valid,
    cotangent,
    w_query,
    w_key,
    w_value,
    b_query,
    b_value,
    w_attn_out,
    b_attn_out,
    w_mlp_in,
    b_mlp_in,
    w_mlp_out,
    b_mlp_out,
    attention_norm_gain,
    attention_norm_shift,
    feedforward_norm_gain,
    feedforward_norm_shift,
):
    rows, width = inputs.shape
    images = valid.shape[0]
    heads_local = w_query.shape[0] // DH
    hidden_local = w_mlp_out.shape[0]
    shape = (lax.axis_size("tok"), lax.axis_size("feat"), images, heads_local, hidden_local, width)
    if shape != (4, 8, 4, 2, 512, 1024) or 2 * rows != SEQ + 1:
        return on_device_general(
            inputs,
            valid,
            cotangent,
            w_query,
            w_key,
            w_value,
            b_query,
            b_value,
            w_attn_out,
            b_attn_out,
            w_mlp_in,
            b_mlp_in,
            w_mlp_out,
            b_mlp_out,
            attention_norm_gain,
            attention_norm_shift,
            feedforward_norm_gain,
            feedforward_norm_shift,
        )
    half = (rows + 15) // 16 * 16
    image = 2 * half
    quarter = hidden_local // 4
    piece = 4 * PART + 16
    row_block = (half, width)
    low_rows, wide_rows = (row_block, BF16), (row_block, F32)
    last, usual = (), 0.01
    calls, sent = [], []

    def send(values, pairs):
        found = lax.ppermute(values, AXES, pairs)
        sent.append(found)
        return found


    def call(body, operands, outs, scratch=(), gate=(), specs=None, span=None, final=False):
        nonlocal last
        specs = [VMEM] * len(operands) if specs is None else specs
        number = len(calls)
        calls.append(number)
        span = SPANS.get(number, usual if span is None else span)
        gate = [g for i, g in enumerate(gate) if i not in LATE.get(number, ())]
        gate += [sent[i] for i in EARLY.get(number, ()) if i < len(sent)]
        found = kernel_call(body, operands, specs, outs, scratch, last + tuple(gate), span)
        if not final:
            last = (min(found, key=lambda v: v.size * v.dtype.itemsize),)
        return found

    def pin(values, gate=()):
        return call(copy_kernel, (values,), [(values.shape, values.dtype)], gate=gate)[0]

    def far_sum(values, received, gate=(), sizes=(half,)):
        outs = [((size, width), BF16) for size in sizes]
        found = call(far_sum_kernel, (values, received), outs, gate=gate)
        return found if len(sizes) > 1 else found[0]

    def split(values, received, sizes, gate=()):
        outs = [((size, width), BF16) for size in sizes]
        return call(add_split_kernel, (values, received), outs, gate=gate)

    def add_last(values, one, three, gate=()):
        return call(add_three_kernel, (values, one, three), [(values.shape, BF16)], gate=gate)[0]

    in_hbm = [
        pltpu.with_memory_space_constraint(w, pltpu.HBM)
        for w in (w_query, w_key, w_value, w_attn_out, b_query, b_value, b_mlp_in)
    ]
    attn_own, attn_other, attn_both = call(
        attention_weights_kernel,
        in_hbm,
        [((piece, width), BF16)] * 2 + [((2 * piece, width), BF16)],
        scratch=[
            pltpu.VMEM((2 * DH,), BF16),
            pltpu.VMEM((2 * DH,), BF16),
            pltpu.VMEM((hidden_local,), BF16),
            pltpu.SemaphoreType.DMA((19,)),
        ],
        specs=[HBM] * 7,
    )
    own_one = send(attn_own, UP_Z)
    attn_three = send(attn_both, DOWN_Z)
    (edge,) = call(edge_kernel, (inputs, cotangent), [((16, width), BF16)])
    edge = send(edge, NEXT)
    mlp_own, mlp_other, mlp_both = call(
        mlp_weights_kernel,
        (w_mlp_in, w_mlp_out),
        [((2 * quarter, width), BF16)] * 2 + [((4 * quarter, width), BF16)],
    )
    stream, normed, branch_grad, branch_again = call(
        entry_kernel,
        (valid, inputs, cotangent, edge, attention_norm_gain, attention_norm_shift),
        [low_rows] * 4,
        scratch=[pltpu.VMEM((half + 8, width), F32)],
        gate=(own_one,),
        specs=[SMEM] + [VMEM] * 5, span=30)
    own_two = send(own_one, UP_Z)
    other_one = send(own_one, SWAP_X)
    normed_y, normed_c = send(normed, SWAP_Y), send(normed, SWAP_C)
    mlp_first = pin(mlp_own, (attn_three, normed_c))
    mlp_one = send(mlp_first, UP_Z)
    pin(edge, (own_two, other_one))
    other_two = send(own_two, SWAP_X)
    branch_again = pin(branch_again, (normed_y,))
    normed_yc = send(normed_y, SWAP_C)
    branch_y, branch_c = send(branch_again, SWAP_Y), send(branch_again, SWAP_C)

    lanes = 2 * DH
    pair_out = [((image, 3 * lanes), BF16)], [((2, image, image), BF16)], [((image, lanes), BF16)]
    weight_out = [((3 * lanes, width), BF16), ((lanes, width), BF16)]
    first_pair = call(
        functools.partial(first_pair_kernel, rows),
        (normed, normed_y, normed_c, normed_yc, attn_own, attn_other, own_one, other_one),
        pair_out[0] * 2 + pair_out[1] * 2 + pair_out[2] * 2 + weight_out,
        span=30,
    )
    w_first, out_first = first_pair[6:]
    qkv_other, probs_other, mixed_other, partial_other, w_second, out_second, second_bias = call(
        functools.partial(second_pair_other_kernel, rows),
        (normed_c, normed_yc, attn_three, own_two, other_two, first_pair[5], out_first),
        pair_out[0]
        + pair_out[1]
        + pair_out[2]
        + [((image, width), BF16)]
        + weight_out
        + [((8, 3 * lanes), F32)],
        gate=(branch_c,),
        span=30,
    )
    from_core = send(partial_other, SWAP_C)
    mlp_two = send(mlp_one, UP_Z)
    mlp_other_one = send(mlp_one, SWAP_X)
    qkv_own, probs_own, mixed_own, partial_near, partial_far = call(
        functools.partial(second_pair_own_kernel, rows),
        (normed, normed_y, w_second, out_second, second_bias, first_pair[4], out_first),
        pair_out[0] + pair_out[1] + pair_out[2] + [low_rows] * 2,
        gate=(mlp_one,),
        span=30,
    )
    saved = (
        (out_first,) + tuple(first_pair[:6]),
        (out_second, qkv_own, qkv_other, probs_own, probs_other, mixed_own, mixed_other),
    )
    parts_of_half = (half // 2 + 8, half - half // 2 - 8)
    attn_far = far_sum(partial_far, from_core, (branch_y,), parts_of_half)
    from_y = tuple(send(part, SWAP_Y) for part in attn_far)
    mlp_three = send(pin(mlp_both), DOWN_Z)
    branch_yc = send(branch_y, SWAP_C)
    middle, normed_middle, attn_power = call(
        functools.partial(middle_kernel, rows),
        (valid, partial_near, from_core) + from_y + (stream,)
        + (b_attn_out, feedforward_norm_gain, feedforward_norm_shift),
        [wide_rows, low_rows, ((8, width), F32)],
        gate=(mlp_other_one, branch_yc),
        specs=[SMEM] + [VMEM] * 8, span=30)
    middle_y, middle_c = send(normed_middle, SWAP_Y), send(normed_middle, SWAP_C)
    pin(attn_power, (mlp_two, middle_c))
    mlp_other_two = send(mlp_two, SWAP_X)

    usual = 10
    middle_yc = send(middle_y, SWAP_C)
    pieces = (mlp_own, mlp_other, mlp_one, mlp_other_one, mlp_three, mlp_two, mlp_other_two)
    pieces += (attn_own, own_one, attn_three, own_two)
    mlp_out = (
        [((image, 8 * quarter), BF16)] * 2 + [low_rows] * 4 + [((8, 8 * quarter), F32)]
    )
    chip = call(
        mlp_kernel,
        (normed_middle, middle_c, branch_grad, branch_c) + pieces,
        mlp_out,
        gate=(middle_y,),
    )
    mid_core, out_core = send(chip[3], SWAP_C), send(chip[5], SWAP_C)
    distant = call(mlp_kernel, (middle_y, middle_yc, branch_y, branch_yc) + pieces, mlp_out)
    out_distant = send(distant[5], SWAP_C)
    mid_far = far_sum(distant[2], send(distant[3], SWAP_C), (mid_core, out_core))
    mid_y = send(mid_far, SWAP_Y)

    grad_out = call(
        functools.partial(products_kernel, True),
        (chip[0], distant[0], branch_grad, branch_c, branch_y, branch_yc),
        [((2 * quarter, width), BF16)] * 4,
        gate=(out_distant,),
    )
    grad_out = dict(zip(SLOTS, grad_out))
    out_two = send(grad_out[2], DOWN_Z)
    out_three = send(grad_out[3], UP_Z)
    grad_in_keep, grad_in_give = call(
        functools.partial(products_kernel, False),
        (chip[1], distant[1], normed_middle, middle_c, middle_y, middle_yc),
        [((4 * quarter, width), BF16)] * 2,
    )
    in_received = send(grad_in_give, SWAP_X)
    grad_middle, grad_attn, middle_sums = call(
        middle_back_kernel,
        (chip[2], mid_core, mid_y, middle, branch_grad, feedforward_norm_gain),
        [wide_rows, low_rows, ((8, width), F32)],
    )
    grad_y, grad_c = send(grad_attn, SWAP_Y), send(grad_attn, SWAP_C)
    out_far = far_sum(distant[4], out_distant)
    (one,) = split(grad_out[1], out_two, (2 * quarter,), (grad_c,))
    out_one = send(one, DOWN_Z)
    grad_yc = send(grad_y, SWAP_C)

    def backward(p, gate=()):
        return call(
            functools.partial(backward_kernel, p),
            (grad_attn, grad_y, grad_c, grad_yc, normed, normed_y, normed_c, normed_yc)
            + saved[p]
            + (chip[6], distant[6]),
            [((image, 6 * DH), BF16)] * 2 + [((2 * piece, width), BF16)] * 2,
            gate=gate,
        )

    second_own, second_other, give, keep = backward(1)
    received = send(give, SWAP_X)
    out_y = send(pin(out_far), SWAP_Y)
    first_own, first_other, give_first, keep_first = backward(0, (out_one, out_three))
    received_first = send(give_first, SWAP_X)
    in_pieces = split(grad_in_keep, in_received, (quarter,) * 4)
    in_pieces = dict(zip(SLOTS, in_pieces))
    in_two = send(in_pieces[2], DOWN_Z)
    in_three = send(in_pieces[3], UP_Z)
    (entry_other,) = call(
        entry_product_kernel, (first_other, second_other, w_first, w_second), [((image, width), BF16)]
    )
    entry_core = send(entry_other, SWAP_C)
    entry_near, entry_far = call(
        entry_product_kernel, (first_own, second_own, w_first, w_second), [low_rows] * 2
    )
    entry_far = far_sum(entry_far, entry_core)
    entry_y = send(entry_far, SWAP_Y)
    three, two = split(keep, received, (piece,) * 2, (in_three,))
    attn_two = send(two, DOWN_Z)
    attn_three = send(three, UP_Z)
    (one,) = split(in_pieces[1], in_two, (quarter,))
    in_one = send(one, DOWN_Z)
    output, output_heads, power_sums = call(
        functools.partial(output_kernel, rows),
        (valid, chip[4], out_core, out_y, middle, stream, b_mlp_out, attn_power, middle_sums),
        [wide_rows, ((8, width), F32), ((8, width), F32)],
        specs=[SMEM] + [VMEM] * 8,
    )
    out_total = call(
        add_three_kernel,
        (grad_out[0], out_one, out_three),
        [((2 * quarter, width), BF16)],
        gate=(received_first,),
    )[0]
    out_across = send(out_total, SWAP_X)
    zero, one = call(
        add_split_last_kernel,
        (keep_first, received_first, attn_two),
        [((piece, width), BF16)] * 2,
    )
    attn_one = send(one, DOWN_Z)
    gradient, heads, small = call(
        functools.partial(entry_back_kernel, rows),
        (valid, entry_near, entry_core, entry_y, stream, grad_middle)
        + (attention_norm_gain, power_sums),
        [wide_rows, ((8, width), F32), ((8, width), F32)],
        gate=(attn_three,),
        specs=[SMEM] + [VMEM] * 7,
    )

    def add_small(received, gate=()):
        return call(add_wide_kernel, (small, received), [(small.shape, F32)], gate=gate)[0]

    heads_after = send(jnp.concatenate([output_heads, heads]), PREVIOUS)
    small = add_small(send(small, SWAP_C))
    small_y = send(small, SWAP_Y)
    attn_total = add_last(zero, attn_one, attn_three, (out_across,))
    attn_across, attn_core = send(attn_total, SWAP_X), send(attn_total, SWAP_C)
    small = add_small(small_y, (attn_core, heads_after))
    small_z = send(small, FLIP_Z[1])
    output_rows, gradient_rows = call(
        exit_kernel,
        (output, gradient, heads_after),
        [((rows, width), F32)] * 2,
        scratch=[pltpu.VMEM((half, width), F32)], final=True)
    small = add_small(small_z)
    small_z = send(small, FLIP_Z[2])
    in_total = add_last(in_pieces[0], in_one, in_three)
    in_across, in_core = send(in_total, SWAP_X), send(in_total, SWAP_C)
    (out_whole,) = call(
        swapped_sum_kernel,
        (out_total, out_across),
        [((2 * quarter, width), BF16)],
        gate=(attn_across,),
    )
    out_core = send(out_whole, SWAP_C)
    attn_last = send(attn_across, SWAP_C)
    small = add_small(small_z, (in_core,))
    small_x = send(small, SWAP_X)
    attn_grads = call(
        attention_gradients_kernel,
        (attn_total, attn_across, attn_core, attn_last),
        [((2 * DH, width), F32)] * 4
        + [((2 * DH,), F32), ((2 * DH,), F32), ((hidden_local,), F32)], final=True)
    in_last = send(in_across, SWAP_C)
    (grad_w_mlp_out,) = call(
        mlp_out_gradient_kernel, (out_whole, out_core), [((hidden_local, width), F32)], final=True)
    (grad_w_mlp_in,) = call(
        mlp_in_gradient_kernel,
        (in_total, in_across, in_core, in_last),
        [((width, hidden_local), F32)], final=True)
    *vectors, powers = call(
        sums_kernel, (small, small_x), [((width,), F32)] * 6 + [((2 * DH,), F32)], final=True)
    stream_rms = jnp.sqrt(powers[:4] / (jnp.maximum(powers[4], 1.0) * D))
    return (
        output_rows,
        gradient_rows,
        attn_grads[0],
        attn_grads[1],
        attn_grads[2],
        attn_grads[4],
        attn_grads[5],
        attn_grads[3],
        vectors[0],
        grad_w_mlp_in,
        attn_grads[6],
        grad_w_mlp_out,
        vectors[1],
        vectors[2],
        vectors[3],
        vectors[4],
        vectors[5],
        stream_rms,
    )


def solution(mesh):
    in_specs = (
        P(("tok", "feat"), None),
        P("tok"),
        P(("tok", "feat"), None),
        P("feat", None),
        P("feat", None),
        P("feat", None),
        P("feat"),
        P("feat"),
        P("feat", None),
        P(),
        P(None, "feat"),
        P("feat"),
        P("feat", None),
        P(),
        P(),
        P(),
        P(),
        P(),
    )
    out_specs = (
        P(("tok", "feat"), None),
        P(("tok", "feat"), None),
        P("feat", None),
        P("feat", None),
        P("feat", None),
        P("feat"),
        P("feat"),
        P("feat", None),
        P(),
        P(None, "feat"),
        P("feat"),
        P("feat", None),
        P(),
        P(),
        P(),
        P(),
        P(),
        P(),
    )
    return jax.shard_map(
        on_device, mesh=mesh, in_specs=in_specs, out_specs=out_specs, check_vma=False
    )
```

```python
import functools

import jax
import jax.numpy as jnp
from jax import lax
from jax.experimental import pallas as pl
from jax.experimental.pallas import tpu as pltpu
from jax.sharding import PartitionSpec as P

D = 1024
DH = 64
SEQ = 577


EPSILON = 1e-05
SLOPE = 1.702


def gelu_slope(values):
    sigmoid = jax.nn.sigmoid(SLOPE * values)
    return sigmoid + SLOPE * values * sigmoid * (1.0 - sigmoid)


def column_sums(values):
    return jnp.sum(values.astype(jnp.float32), axis=0)


def split_heads(values):
    return values.reshape(values.shape[0], values.shape[1] // DH, DH)


def apply_layer_norm(values):
    center = jnp.mean(values, axis=1, keepdims=True)
    spread = jnp.mean(values * values, axis=1, keepdims=True) - center * center
    inverse_deviation = lax.rsqrt(spread + EPSILON)
    return ((values - center) * inverse_deviation, inverse_deviation)


def layer_norm_backward(normalized_gradient, centered_scaled, inverse_deviation, norm_gain):
    scaled_output = normalized_gradient * norm_gain.astype(jnp.float32)
    plain_output = jnp.mean(scaled_output, axis=1, keepdims=True)
    cross_term = jnp.mean(scaled_output * centered_scaled, axis=1, keepdims=True)
    return inverse_deviation * (scaled_output - plain_output - centered_scaled * cross_term)


def image_forward(blocks):
    query_img, key_img, value_img = blocks
    scale = DH ** (-0.5)
    query_heads = split_heads(query_img)
    key_heads = split_heads(key_img)
    value_heads = split_heads(value_img)
    scores = (
        jnp.einsum("qhd,khd->hqk", query_heads, key_heads, preferred_element_type=jnp.float32)
        * scale
    )
    top_score = jnp.max(scores, axis=-1, keepdims=True)
    weights = jnp.exp(scores - top_score)
    total = jnp.sum(weights, axis=-1, keepdims=True)
    probs = (weights / total).astype(jnp.bfloat16)
    mixed = jnp.einsum("hqk,khd->qhd", probs, value_heads, preferred_element_type=jnp.float32)
    log_total = top_score[..., 0] + jnp.log(total[..., 0])
    return (mixed.reshape(query_img.shape).astype(jnp.bfloat16), log_total)


def image_backward(blocks):
    query_img, key_img, value_img, grad_img, log_total = blocks
    scale = DH ** (-0.5)
    query_heads = split_heads(query_img)
    key_heads = split_heads(key_img)
    value_heads = split_heads(value_img)
    grad_heads = split_heads(grad_img)
    scores = (
        jnp.einsum("qhd,khd->hqk", query_heads, key_heads, preferred_element_type=jnp.float32)
        * scale
    )
    probs = jnp.exp(scores - log_total[..., None])
    probs_low = probs.astype(jnp.bfloat16)
    grad_probs = jnp.einsum(
        "qhd,khd->hqk", grad_heads, value_heads, preferred_element_type=jnp.float32
    )
    grad_value = jnp.einsum(
        "hqk,qhd->khd", probs_low, grad_heads, preferred_element_type=jnp.float32
    )
    inner = jnp.sum(probs * grad_probs, axis=-1, keepdims=True)
    grad_scores = (probs * (grad_probs - inner)).astype(jnp.bfloat16)
    grad_query = (
        jnp.einsum("hqk,khd->qhd", grad_scores, key_heads, preferred_element_type=jnp.float32)
        * scale
    )
    grad_key = (
        jnp.einsum("hqk,qhd->khd", grad_scores, query_heads, preferred_element_type=jnp.float32)
        * scale
    )
    shape_img = query_img.shape
    return (
        grad_query.reshape(shape_img).astype(jnp.bfloat16),
        grad_key.reshape(shape_img).astype(jnp.bfloat16),
        grad_value.reshape(shape_img).astype(jnp.bfloat16),
    )


def by_image(values, images):
    return values.reshape(images, values.shape[0] // images, values.shape[1])


def on_device_general(
    inputs,
    valid,
    cotangent,
    w_query,
    w_key,
    w_value,
    b_query,
    b_value,
    w_attn_out,
    b_attn_out,
    w_mlp_in,
    b_mlp_in,
    w_mlp_out,
    b_mlp_out,
    attention_norm_gain,
    attention_norm_shift,
    feedforward_norm_gain,
    feedforward_norm_shift,
):
    row_count, width = inputs.shape
    images = valid.shape[0]
    group_rows = images * SEQ
    parts = lax.axis_size("feat")
    extra = row_count * parts - group_rows
    width_local = w_query.shape[0]
    hidden_local = w_mlp_out.shape[0]
    global_rows = lax.axis_index("feat") * row_count + jnp.arange(row_count, dtype=jnp.int32)
    owner = global_rows // SEQ
    matches = (owner[:, None] == jnp.arange(images, dtype=jnp.int32)[None, :]).astype(jnp.float32)
    row_mask = jnp.sum(matches * valid.astype(jnp.float32)[None, :], axis=1)
    live = (global_rows < group_rows).astype(jnp.float32)[:, None]

    def padded(values):
        return jnp.pad(values, ((0, extra), (0, 0)))

    local_input_rows = inputs.astype(jnp.float32)
    first_centered_scaled, first_inverse_deviation = apply_layer_norm(local_input_rows)
    normalized_first = (
        first_centered_scaled * attention_norm_gain.astype(jnp.float32)
        + attention_norm_shift.astype(jnp.float32)
    ).astype(jnp.bfloat16)
    normed_full = lax.all_gather(normalized_first, "feat", axis=0, tiled=True)[:group_rows]
    w_qkv = jnp.concatenate([w_query, w_key, w_value], axis=0)
    projected = jnp.einsum("rd,cd->rc", normed_full, w_qkv, preferred_element_type=jnp.float32)
    queries = (projected[:, :width_local] + b_query.astype(jnp.float32)).astype(jnp.bfloat16)
    key_rows = projected[:, width_local : 2 * width_local].astype(jnp.bfloat16)
    value_rows = (projected[:, 2 * width_local :] + b_value.astype(jnp.float32)).astype(
        jnp.bfloat16
    )
    mixed, log_totals = lax.map(
        image_forward,
        (by_image(queries, images), by_image(key_rows, images), by_image(value_rows, images)),
    )
    mixed = mixed.reshape(group_rows, width_local)
    partial_out = jnp.dot(mixed, w_attn_out, preferred_element_type=jnp.float32)
    attn = lax.psum_scatter(
        padded(partial_out), "feat", scatter_dimension=0, tiled=True
    ) + b_attn_out.astype(jnp.float32)
    middle_state = local_input_rows + attn
    second_centered_scaled, second_inverse_deviation = apply_layer_norm(middle_state)
    normalized_middle = (
        second_centered_scaled * feedforward_norm_gain.astype(jnp.float32)
        + feedforward_norm_shift.astype(jnp.float32)
    ).astype(jnp.bfloat16)
    mid_full = lax.all_gather(normalized_middle, "feat", axis=0, tiled=True)[:group_rows]
    hidden = jnp.dot(mid_full, w_mlp_in, preferred_element_type=jnp.float32) + b_mlp_in.astype(
        jnp.float32
    )
    active = (hidden * jax.nn.sigmoid(SLOPE * hidden)).astype(jnp.bfloat16)
    partial_mlp = jnp.dot(active, w_mlp_out, preferred_element_type=jnp.float32)
    branch = lax.psum_scatter(
        padded(partial_mlp).astype(jnp.bfloat16), "feat", scatter_dimension=0, tiled=True
    ).astype(jnp.float32) + b_mlp_out.astype(jnp.float32)
    output = (middle_state + branch) * live
    output_gradient = cotangent.astype(jnp.float32) * row_mask[:, None]
    grad_branch = output_gradient.astype(jnp.bfloat16)
    grad_b_mlp_out = column_sums(grad_branch)
    branch_full = lax.all_gather(grad_branch, "feat", axis=0, tiled=True)[:group_rows]
    grad_w_mlp_out = jnp.einsum(
        "rf,rd->fd", active, branch_full, preferred_element_type=jnp.float32
    )
    grad_active = jnp.einsum(
        "rd,fd->rf", branch_full, w_mlp_out, preferred_element_type=jnp.float32
    )
    grad_hidden = (grad_active * gelu_slope(hidden)).astype(jnp.bfloat16)
    grad_b_mlp_in = column_sums(grad_hidden)
    grad_mlp_in_rows = jnp.einsum(
        "rf,rd->fd", grad_hidden, mid_full, preferred_element_type=jnp.float32
    )
    partial_mid = jnp.einsum("rf,df->rd", grad_hidden, w_mlp_in, preferred_element_type=jnp.float32)
    midpoint_gradient = lax.psum_scatter(
        padded(partial_mid), "feat", scatter_dimension=0, tiled=True
    )
    feedforward_gain_gradient = jnp.sum(midpoint_gradient * second_centered_scaled, axis=0)
    grad_s_mlp = jnp.sum(midpoint_gradient, axis=0)
    middle_state_gradient = output_gradient + layer_norm_backward(
        midpoint_gradient, second_centered_scaled, second_inverse_deviation, feedforward_norm_gain
    )
    grad_attn = middle_state_gradient.astype(jnp.bfloat16)
    grad_b_attn_out = column_sums(grad_attn)
    attn_full = lax.all_gather(grad_attn, "feat", axis=0, tiled=True)[:group_rows]
    grad_w_attn_out = jnp.einsum("rh,rd->hd", mixed, attn_full, preferred_element_type=jnp.float32)
    grad_mixed = jnp.einsum(
        "rd,hd->rh", attn_full, w_attn_out, preferred_element_type=jnp.float32
    ).astype(jnp.bfloat16)
    grad_query, grad_key, grad_value = lax.map(
        image_backward,
        (
            by_image(queries, images),
            by_image(key_rows, images),
            by_image(value_rows, images),
            by_image(grad_mixed, images),
            log_totals,
        ),
    )
    grad_query = grad_query.reshape(group_rows, width_local)
    grad_key = grad_key.reshape(group_rows, width_local)
    grad_value = grad_value.reshape(group_rows, width_local)
    grad_b_query = column_sums(grad_query)
    grad_b_value = column_sums(grad_value)
    grad_qkv = jnp.concatenate([grad_query, grad_key, grad_value], axis=1)
    grad_w_qkv = jnp.einsum("rc,rd->cd", grad_qkv, normed_full, preferred_element_type=jnp.float32)
    partial_in = jnp.einsum("rc,cd->rd", grad_qkv, w_qkv, preferred_element_type=jnp.float32)
    normalized_gradient = lax.psum_scatter(
        padded(partial_in).astype(jnp.bfloat16), "feat", scatter_dimension=0, tiled=True
    ).astype(jnp.float32)
    attention_gain_gradient = jnp.sum(normalized_gradient * first_centered_scaled, axis=0)
    grad_s_attn = jnp.sum(normalized_gradient, axis=0)
    layer_input_gradient = middle_state_gradient + layer_norm_backward(
        normalized_gradient, first_centered_scaled, first_inverse_deviation, attention_norm_gain
    )
    local_powers = jnp.stack(
        [
            jnp.sum(row_mask[:, None] * local_input_rows * local_input_rows),
            jnp.sum(row_mask[:, None] * attn * attn),
            jnp.sum(row_mask[:, None] * branch * branch),
            jnp.sum(row_mask[:, None] * output * output),
        ]
    )
    local_count = jnp.sum(row_mask)
    bias_entries = jnp.concatenate([grad_b_query, grad_b_value, grad_b_mlp_in])
    bias_row = jnp.pad(bias_entries, (0, width - bias_entries.shape[0]))[None, :]
    packed = jnp.concatenate(
        [grad_w_qkv, grad_w_attn_out, grad_mlp_in_rows, grad_w_mlp_out, bias_row], axis=0
    )
    packed_rows = packed.shape[0]
    tok_parts = lax.axis_size("tok")
    fill_rows = (tok_parts - packed_rows % tok_parts) % tok_parts
    packed = jnp.pad(packed, ((0, fill_rows), (0, 0)))
    shares = lax.psum_scatter(
        packed.astype(jnp.bfloat16), "tok", scatter_dimension=0, tiled=True
    ).astype(jnp.float32)
    summed = lax.all_gather(shares.astype(jnp.bfloat16), "tok", axis=0, tiled=True).astype(
        shares.dtype
    )[:packed_rows]
    offset = 0
    grad_w_query = summed[offset : offset + width_local]
    offset += width_local
    grad_w_key = summed[offset : offset + width_local]
    offset += width_local
    grad_w_value = summed[offset : offset + width_local]
    offset += width_local
    grad_w_attn_out = summed[offset : offset + width_local]
    offset += width_local
    grad_w_mlp_in = summed[offset : offset + hidden_local].T
    offset += hidden_local
    grad_w_mlp_out = summed[offset : offset + hidden_local]
    offset += hidden_local
    bias_sums = summed[offset]
    grad_b_query = bias_sums[:width_local]
    grad_b_value = bias_sums[width_local : 2 * width_local]
    grad_b_mlp_in = bias_sums[2 * width_local : 2 * width_local + hidden_local]
    (
        grad_b_attn_out,
        grad_b_mlp_out,
        attention_gain_gradient,
        grad_s_attn,
        feedforward_gain_gradient,
        grad_s_mlp,
        powers,
        counted,
    ) = lax.psum(
        (
            grad_b_attn_out,
            grad_b_mlp_out,
            attention_gain_gradient,
            grad_s_attn,
            feedforward_gain_gradient,
            grad_s_mlp,
            local_powers,
            local_count,
        ),
        ("tok", "feat"),
    )
    stream_rms = jnp.sqrt(powers / (jnp.maximum(counted, 1.0) * D))
    return (
        output,
        layer_input_gradient,
        grad_w_query,
        grad_w_key,
        grad_w_value,
        grad_b_query,
        grad_b_value,
        grad_w_attn_out,
        grad_b_attn_out,
        grad_w_mlp_in,
        grad_b_mlp_in,
        grad_w_mlp_out,
        grad_b_mlp_out,
        attention_gain_gradient,
        grad_s_attn,
        feedforward_gain_gradient,
        grad_s_mlp,
        stream_rms,
    )


BF16 = jnp.bfloat16
F32 = jnp.float32
AXES = ("tok", "feat")
SLOTS = (0, 1, 3, 2)
PAIRS = ((0, 1), (3, 2))
CHUNK = 16
PART = DH // 2


SPANS = {
    0: 6,
    1: 1,
    2: 0.01,
    3: 1,
    4: 0.01,
    6: 60,
    7: 6,
    8: 0.01,
    11: 6,
    12: 10,
    13: 1,
    14: 10,
    15: 0.01,
    16: 30,
    17: 6,
    18: 10,
    19: 0.01,
    23: 0.01,
    24: 6,
    25: 0.01,
    26: 1,
    27: 30,
    28: 3,
    29: 0.01,
    30: 3,
    31: 3,
    33: 6,
    34: 3,
    35: 0.01,
    36: 1,
    37: 10,
    39: 0.01,
    40: 1,
    44: 1,
    45: 0.01,
    46: 0.01,
}
EARLY = {
    2: (2,),
    4: (6,),
    5: (0, 7),
    6: (8,),
    7: (2,),
    8: (6,),
    10: (11,),
    12: (11,),
    13: (15,),
    14: (21,),
    15: (14,),
    17: (26,),
    18: (25,),
    20: (26,),
    27: (36,),
    31: (39,),
    37: (46,),
    38: (52,),
    39: (51,),
    42: (52,),
    43: (58,),
    44: (55, 57),
    45: (44, 58),
    46: (52,),
}
LATE = {
    4: (1, 0),
    5: (0, 1),
    8: (0,),
    12: (1,),
    13: (1,),
    14: (0,),
    21: (0,),
    29: (0,),
    32: (0,),
    37: (1, 0),
}


def route(move):
    found = []
    for tok in range(4):
        for feat in range(8):
            target = move(tok // 2, tok % 2, feat // 2, feat % 2)
            if target is not None:
                x, c, z, y = target
                found.append((tok * 8 + feat, (2 * x + c) * 8 + 2 * z + y))
    return found


SWAP_X = route(lambda x, c, z, y: (1 - x, c, z, y))
SWAP_C = route(lambda x, c, z, y: (x, 1 - c, z, y))
SWAP_Y = route(lambda x, c, z, y: (x, c, z, 1 - y))
UP_Z = route(lambda x, c, z, y: (x, c, (z + 1) % 4, y))
DOWN_Z = route(lambda x, c, z, y: (x, c, (z + 3) % 4, y))
FLIP_Z = [route(lambda x, c, z, y, s=s: (x, c, z ^ s, y)) for s in range(4)]
NEXT = [(t * 8 + f, t * 8 + f + 1) for t in range(4) for f in range(7)]
PREVIOUS = [(t * 8 + f + 1, t * 8 + f) for t in range(4) for f in range(7)]


def nt(left, right):
    return lax.dot_general(left, right, (((1,), (1,)), ((), ())), preferred_element_type=F32)


def nn(left, right):
    return lax.dot_general(left, right, (((1,), (0,)), ((), ())), preferred_element_type=F32)


def tn(left, right):
    return lax.dot_general(left, right, (((0,), (0,)), ((), ())), preferred_element_type=F32)


SMEM = pl.BlockSpec(memory_space=pltpu.SMEM)
HBM = pl.BlockSpec(memory_space=pltpu.HBM)
VMEM = pl.BlockSpec(memory_space=pltpu.VMEM)


def kernel_call(body, operands, specs, outs, scratch=(), after=(), span=0.01, vmem=12):
    count, extra = len(operands), len(after)

    def kernel(*refs):
        body(*refs[:count], *refs[count + extra :])

    return pl.pallas_call(
        kernel,
        in_specs=list(specs) + [VMEM] * extra,
        out_specs=[VMEM] * len(outs),
        out_shape=[jax.ShapeDtypeStruct(shape, dtype) for shape, dtype in outs],
        scratch_shapes=list(scratch),
        compiler_params=pltpu.CompilerParams(
            vmem_limit_bytes=vmem * 2**20, fuse_transposed_lhs_in_matmul=True
        ),
        cost_estimate=pl.CostEstimate(
            flops=int(span * 1e9), bytes_accessed=2**16, transcendentals=0
        ),
    )(*operands, *after)


def coordinates():
    tok, feat = lax.axis_index("tok"), lax.axis_index("feat")
    return tok // 2, tok % 2, feat // 2, feat % 2


def chunks(half):
    return [slice(at, at + CHUNK) for at in range(0, half, CHUNK)]


def row_of(vector):
    return vector[...].astype(F32).reshape(1, vector.shape[0])


def folded(values):
    return values[:8] + values[8:]


def moment_norm(values):
    center = jnp.mean(values, axis=1, keepdims=True)
    spread = jnp.mean(values * values, axis=1, keepdims=True) - center * center
    inverse = lax.rsqrt(spread + EPSILON)
    return (values - center) * inverse, inverse


def attention_weights_kernel(wq, wk, wv, wo, b_query, b_value, b_hidden, *refs):
    own, other, both, query, value, hidden, sems = refs
    piece = own.shape[0]
    x, c, _, _ = coordinates()
    width = own.shape[1]
    copies = []
    for source, target in ((b_query, query), (b_value, value), (b_hidden, hidden)):
        copies.append(pltpu.make_async_copy(source, target, sems.at[len(copies)]))
    targets = ((own, 0, x), (other, 0, 1 - x), (both, 0, x), (both, piece, 1 - x))
    for out, first, side in targets:
        at = pl.multiple_of(c * DH + side * PART, PART)
        for m, w in enumerate((wq, wk, wv, wo)):
            copies.append(
                pltpu.make_async_copy(
                    w.at[pl.ds(at, PART)], out.at[pl.ds(first + m * PART, PART)], sems.at[len(copies)]
                )
            )
    for copy in copies:
        copy.start()
    for copy in copies[:3]:
        copy.wait()
    parts = [row_of(vector) for vector in (query, value, hidden)]
    taken = sum(part.shape[1] for part in parts)
    bias = jnp.concatenate(parts + [jnp.zeros((1, width - taken), F32)], axis=1)
    bias = jnp.broadcast_to(bias, (16, width)).astype(BF16)
    for out, first, _ in targets:
        out[first + 4 * PART : first + piece, :] = bias
    for copy in copies[3:]:
        copy.wait()


def edge_kernel(inputs, cotangent, edge):
    rows = inputs.shape[0]
    at = (rows - 8) // 16 * 16
    for i, values in enumerate((inputs, cotangent)):
        edge[8 * i : 8 * i + 8, :] = values[at:, :].astype(F32)[rows - 8 - at :].astype(BF16)


def mlp_weights_kernel(w_in, w_out, own, other, both):
    x, c, _, _ = coordinates()
    quarter = own.shape[0] // 2
    for out, first, side in ((own, 0, x), (other, 2 * quarter, 1 - x)):
        at = pl.multiple_of((2 * c + side) * quarter, quarter)
        found = w_in[:, pl.ds(at, quarter)].T
        rest = w_out[pl.ds(at, quarter), :]
        out[:quarter, :] = found
        out[quarter:, :] = rest
        both[first : first + quarter, :] = found
        both[first + quarter : first + 2 * quarter, :] = rest


def halves_of(refs, count):
    own_zero, other_zero, own_one, other_one, both, own_two, other_two = refs
    own = [own_zero, own_one, both.at[pl.ds(0, count)], own_two]
    return own, [other_zero, other_one, both.at[pl.ds(count, count)], other_two]


def entry_kernel(
    valid, inputs, cotangent, edge, gain_vector, shift_vector, stream, normed, branch, again, ext
):
    _, _, z, y = coordinates()
    rows = inputs.shape[0]
    half = stream.shape[0]
    gain, shift = row_of(gain_vector), row_of(shift_vector)
    flag = valid[z].astype(F32)

    def aligned(at):
        found = pltpu.roll(ext[at.start : at.stop + 8, :], CHUNK + z, 0)[:CHUNK]
        index = at.start + lax.broadcasted_iota(jnp.int32, (CHUNK, 1), 0)
        return jnp.where(index < rows - y, found, 0.0)

    def fill(values, first):
        ext[0:8, :] = edge[...].astype(F32)[first : first + 8]
        ext[8 : 8 + rows, :] = values[...].astype(F32)

    fill(inputs, 0)
    for at in chunks(half):
        found = aligned(at)
        stream[at, :] = found.astype(BF16)
        hat, _ = moment_norm(found)
        normed[at, :] = (hat * gain + shift).astype(BF16)
    fill(cotangent, 8)
    for at in chunks(half):
        branch[at, :] = (aligned(at) * flag).astype(BF16)
        again[at, :] = branch[at, :]


def softmax_columns(scores):
    top = jnp.max(scores, axis=0, keepdims=True)
    weights = jnp.exp(scores - top)
    return weights * (1.0 / jnp.sum(weights, axis=0, keepdims=True))


def pair_forward(rows, halves, w_in, bias, qkv, probs, mixed):
    half = halves[0].shape[0]
    _, _, _, y = coordinates()
    lanes = 2 * DH
    entry = jnp.concatenate([halves[0][...], halves[1][...]], axis=0)
    qkv[...] = (nt(entry, w_in) + bias).astype(BF16)
    key_index = lax.broadcasted_iota(jnp.int32, (2 * half, 1), 0)
    first = rows - y
    second = half + rows - 1 + y
    real = (key_index < first) | ((key_index >= half) & (key_index < second))
    penalty = jnp.where(real, 0.0, -1e30)
    outs = []
    for h in range(2):
        q = qkv[:, h * DH : (h + 1) * DH] * jnp.asarray(DH ** (-0.5), BF16)
        k = qkv[:, lanes + h * DH : lanes + (h + 1) * DH]
        v = qkv[:, 2 * lanes + h * DH : 2 * lanes + (h + 1) * DH]
        found = softmax_columns(nt(k, q) + penalty).astype(BF16)
        probs[h] = found
        outs.append(tn(v, found))
    mixed[...] = jnp.concatenate(outs, axis=0).T.astype(BF16)


def pair_weights(own, other, w_in, w_out):
    for m in range(4):
        target = w_out if m == 3 else w_in
        for i in range(2):
            at = (0 if m == 3 else m * 2 * DH) + i * DH
            target[at : at + PART, :] = own[i][m * PART : (m + 1) * PART, :]
            target[at + PART : at + DH, :] = other[i][m * PART : (m + 1) * PART, :]
    rows_of = [own[i][4 * PART : 4 * PART + 16, :].astype(F32)[0:1] for i in range(2)]
    query = jnp.concatenate([ordered_bias(r, 0) for r in rows_of], axis=1)
    value = jnp.concatenate([ordered_bias(r, 2 * DH) for r in rows_of], axis=1)
    return jnp.concatenate([query, jnp.zeros_like(query), value], axis=1)


def projected(first_mixed, second_mixed, first_out, second_out, outs):
    mixed = jnp.concatenate([first_mixed[...], second_mixed[...]], axis=1)
    weights = jnp.concatenate([first_out[...], second_out[...]], axis=0)
    found = nn(mixed, weights).astype(BF16)
    at = 0
    for out in outs:
        out[...] = found[at : at + out.shape[0]]
        at += out.shape[0]


def ordered_bias(row, first):
    x, c, _, _ = coordinates()
    block = jnp.where(c == 0, row[:, first : first + DH], row[:, first + DH : first + 2 * DH])
    swapped = jnp.concatenate([block[:, PART:], block[:, :PART]], axis=1)
    return jnp.where(x == 0, block, swapped)


def first_pair_kernel(rows, near, far, near_other, far_other, *refs):
    own_zero, other_zero, own_one, other_one, *refs = refs
    qkv_own, qkv_other, probs_own, probs_other, mixed_own, mixed_other, w_in, w_out = refs
    bias = pair_weights((own_zero, own_one), (other_zero, other_one), w_in, w_out)
    weights = w_in[...]
    pair_forward(rows, (near_other, far_other), weights, bias, qkv_other, probs_other, mixed_other)
    pair_forward(rows, (near, far), weights, bias, qkv_own, probs_own, mixed_own)


def second_pair_other_kernel(rows, near, far, both, own_two, other_two, *refs):
    first_mixed, first_out, qkv, probs, mixed, partial, w_in, w_out, bias = refs
    piece = own_two.shape[0]
    own = (both.at[pl.ds(0, piece)], own_two)
    other = (both.at[pl.ds(piece, piece)], other_two)
    found = pair_weights(own, other, w_in, w_out)
    bias[...] = jnp.broadcast_to(found, bias.shape)
    pair_forward(rows, (near, far), w_in[...], found, qkv, probs, mixed)
    projected(first_mixed, mixed, first_out, w_out, (partial,))


def second_pair_own_kernel(rows, near, far, w_in, w_out, bias, first_mixed, first_out, *refs):
    qkv, probs, mixed, *partials = refs
    pair_forward(rows, (near, far), w_in[...], bias[0:1, :], qkv, probs, mixed)
    projected(first_mixed, mixed, first_out, w_out, partials)


def joined_rows(refs, at):
    size = refs[0].shape[0]
    if at.start < size:
        return refs[0][at, :]
    return refs[1][at.start - size : at.stop - size, :]


def real_rows(at, rows, y):
    return at.start + lax.broadcasted_iota(jnp.int32, (CHUNK, 1), 0) < rows - y


def middle_kernel(
    rows,
    valid,
    partial,
    from_core,
    from_y_first,
    from_y_second,
    stream,
    bias_vector,
    gain_vector,
    shift_vector,
    middle,
    normed,
    powers,
):
    _, _, z, y = coordinates()
    bias, gain, shift = row_of(bias_vector), row_of(gain_vector), row_of(shift_vector)
    total = jnp.zeros((8, middle.shape[1]), F32)
    for at in chunks(middle.shape[0]):
        from_y = joined_rows((from_y_first, from_y_second), at)
        attn = partial[at, :].astype(F32) + from_core[at, :].astype(F32)
        attn = attn + from_y.astype(F32) + bias
        found = stream[at, :].astype(F32) + attn
        middle[at, :] = found
        hat, _ = moment_norm(found)
        normed[at, :] = (hat * gain + shift).astype(BF16)
        total = total + folded(jnp.where(real_rows(at, rows, y), attn * attn, 0.0))
    powers[...] = total * valid[z].astype(F32)


def mlp_kernel(near, far, grad_near, grad_far, *refs):
    own, other = halves_of(refs[:7], refs[0].shape[0])
    bias_of, refs = refs[7:11], refs[11:]
    active, grad_hidden, mid_near, mid_far, out_near, out_far, sums = refs
    x, c, _, _ = coordinates()
    half = near.shape[0]
    quarter = own[0].shape[0] // 2
    w_in = [ref[:quarter, :] for side in (own, other) for ref in side]
    w_out = [ref[quarter:, :] for side in (own, other) for ref in side]
    bias = []
    for side in (x, 1 - x):
        at = pl.multiple_of(4 * DH + (2 * c + side) * quarter, quarter)
        for k in range(4):
            bias.append(bias_of[k][4 * PART :, pl.ds(at, quarter)].astype(F32)[0:1])
    bias = jnp.concatenate(bias, axis=1)
    rows = jnp.concatenate([near[...], far[...]], axis=0)
    grads = jnp.concatenate([grad_near[...], grad_far[...]], axis=0)
    size = 2 * quarter
    for n in range(4):
        at = slice(n * size, (n + 1) * size)
        pair = slice(2 * n, 2 * n + 2)
        u = nt(rows, jnp.concatenate(w_in[pair], axis=0)) + bias[:, at]
        gate = jax.nn.sigmoid(SLOPE * u)
        act = u * gate
        active[:, at] = act.astype(BF16)
        slope = gate + SLOPE * act * (1.0 - gate)
        found = (nt(grads, jnp.concatenate(w_out[pair], axis=0)) * slope).astype(BF16)
        grad_hidden[:, at] = found
        sums[:, at] = jnp.broadcast_to(
            jnp.sum(found.astype(F32), axis=0, keepdims=True), (8, size)
        )
    found = nn(grad_hidden[...], jnp.concatenate(w_in, axis=0)).astype(BF16)
    mid_near[...] = found[:half]
    mid_far[...] = found[half:]
    found = nn(active[...], jnp.concatenate(w_out, axis=0)).astype(BF16)
    out_near[...] = found[:half]
    out_far[...] = found[half:]


def products_kernel(split, left_first, left_second, *refs):
    pieces, outs = refs[:4], refs[4:]
    right = jnp.concatenate([piece[...] for piece in pieces], axis=0)
    hidden = left_first.shape[1] // 2
    quarter = hidden // 4
    for side in (1, 0):
        at = slice(side * hidden, (side + 1) * hidden)
        left = jnp.concatenate([left_first[:, at], left_second[:, at]], axis=0)
        found = tn(left, right).astype(BF16)
        if split:
            for k in range(4):
                outs[k][side * quarter : (side + 1) * quarter, :] = found[
                    k * quarter : (k + 1) * quarter
                ]
        else:
            outs[side][...] = found


def far_sum_kernel(values, received, *outs):
    first = received.shape[0] - values.shape[0]
    done = 0
    for out in outs:
        for at in chunks(out.shape[0]):
            source = slice(done + at.start, done + at.stop)
            moved = slice(first + source.start, first + source.stop)
            found = values[source, :].astype(F32) + received[moved, :].astype(F32)
            out[at, :] = found.astype(BF16)
        done += out.shape[0]


def add_split_kernel(keep, received, *outs):
    at = 0
    for out in outs:
        size = out.shape[0]
        out[...] = (
            keep[at : at + size, :].astype(F32) + received[at : at + size, :].astype(F32)
        ).astype(BF16)
        at += size


def output_kernel(
    rows,
    valid,
    partial,
    from_core,
    from_y,
    middle,
    stream,
    bias_vector,
    attn_power,
    sums,
    output,
    heads,
    small,
):
    _, _, z, y = coordinates()
    bias = row_of(bias_vector)
    width = middle.shape[1]
    totals = [jnp.zeros((8, width), F32) for _ in range(3)]
    for at in chunks(middle.shape[0]):
        branch = partial[at, :].astype(F32) + from_core[at, :].astype(F32)
        branch = branch + from_y[at, :].astype(F32) + bias
        found = middle[at, :] + branch
        output[at, :] = found
        entry = stream[at, :].astype(F32)
        real = real_rows(at, rows, y)
        for i, v in enumerate((entry, branch, found)):
            totals[i] = totals[i] + folded(jnp.where(real, v * v, 0.0))
    heads[...] = output[0:8, :]
    flag = valid[z]
    lane = lax.broadcasted_iota(jnp.int32, (1, width), 1)
    entry = jnp.where(lane == 4, (flag * (rows - y)).astype(F32), 0.0)
    powers = [totals[0] * flag.astype(F32), attn_power[...]]
    powers += [total * flag.astype(F32) for total in totals[1:]]
    for i, power in enumerate(powers):
        whole = jnp.sum(jnp.sum(power, axis=0, keepdims=True), axis=1, keepdims=True)
        entry = entry + jnp.where(lane == i, whole, 0.0)
    row = lax.broadcasted_iota(jnp.int32, (8, 1), 0)
    small[...] = jnp.where(row == 6, entry, sums[...])


def norm_back(grad, hat, inverse, gain):
    scaled = grad * gain
    plain = jnp.mean(scaled, axis=1, keepdims=True)
    cross = jnp.mean(scaled * hat, axis=1, keepdims=True)
    return inverse * (scaled - plain - hat * cross)


def middle_back_kernel(
    partial, from_core, from_y, middle, branch, gain_vector, grad, low, sums
):
    width = middle.shape[1]
    gain = row_of(gain_vector)
    totals = [jnp.zeros((8, width), F32) for _ in range(4)]
    for at in chunks(middle.shape[0]):
        found = partial[at, :].astype(F32) + from_core[at, :].astype(F32)
        found = found + from_y[at, :].astype(F32)
        hat, inverse = moment_norm(middle[at, :])
        gy = branch[at, :].astype(F32)
        total = gy + norm_back(found, hat, inverse, gain)
        grad[at, :] = total
        rounded = total.astype(BF16)
        low[at, :] = rounded
        for i, v in enumerate((rounded.astype(F32), gy, found * hat, found)):
            totals[i] = totals[i] + folded(v)
    sums[...] = jnp.concatenate(
        [jnp.sum(v, axis=0, keepdims=True) for v in totals] + [jnp.zeros((4, width), F32)], axis=0
    )


def backward_kernel(pair, *refs):
    grads, normed, refs = refs[:4], refs[4:8], refs[8:]
    w_out, qkv_own, qkv_other, probs_own, probs_other = refs[:5]
    mixed_own, mixed_other, sums_chip, sums_distant = refs[5:9]
    out_own, out_other, give, keep = refs[9:]
    half = grads[0].shape[0]
    rows = 2 * half
    lanes = 2 * DH
    scale = jnp.asarray(DH ** (-0.5), BF16)
    grad_rows = jnp.concatenate([ref[...] for ref in grads], axis=0)
    wide = nt(grad_rows, w_out[...]).astype(BF16)
    hidden_sums = sums_chip[0:1, :] + sums_distant[0:1, :]
    totals = []
    images = ((qkv_own, probs_own, out_own), (qkv_other, probs_other, out_other))
    for image, (qkv, probs, out) in enumerate(images):
        dq, dk, dv = [], [], []
        for h in range(2):
            at = h * DH
            q = qkv[:, at : at + DH] * scale
            k = qkv[:, lanes + at : lanes + at + DH] * scale
            v = qkv[:, 2 * lanes + at : 2 * lanes + at + DH]
            g = wide[image * rows : (image + 1) * rows, h * DH : (h + 1) * DH]
            found = probs[h]
            grad_probs = nt(v, g)
            scores = found.astype(F32)
            product = scores * grad_probs
            inner = jnp.sum(product, axis=0, keepdims=True)
            grad_scores = (product - scores * inner).astype(BF16)
            dv.append(nn(found, g))
            dk.append(nn(grad_scores, q))
            dq.append(tn(k, grad_scores))
        query = jnp.concatenate(dq, axis=0).T.astype(BF16)
        value = jnp.concatenate(dv, axis=1).astype(BF16)
        out[:, :lanes] = query
        out[:, lanes : 2 * lanes] = jnp.concatenate(dk, axis=1).astype(BF16)
        out[:, 2 * lanes :] = value
        totals.append(
            [jnp.sum(v.astype(F32), axis=0, keepdims=True) for v in (query, value)]
        )
    query_sum, value_sum = (totals[0][i] + totals[1][i] for i in range(2))
    stacked = jnp.concatenate([out_own[...], out_other[...]], axis=0)
    grad_w = tn(stacked, jnp.concatenate([ref[...] for ref in normed], axis=0)).astype(BF16)
    mixed = jnp.concatenate([mixed_own[...], mixed_other[...]], axis=0)
    grad_o = tn(mixed, grad_rows).astype(BF16)
    size = 4 * PART + 16
    quarter = hidden_sums.shape[1] // 8
    width = give.shape[1]
    for side, out in enumerate((keep, give)):
        for i in range(2):
            for m in range(4):
                source = grad_o if m == 3 else grad_w
                at = (0 if m == 3 else m * lanes) + i * DH + side * PART
                out[i * size + m * PART : i * size + (m + 1) * PART, :] = source[at : at + PART]
            at = i * DH + side * PART
            block = (side * 4 + 2 * pair + i) * quarter
            row = jnp.concatenate(
                [
                    query_sum[:, at : at + PART],
                    value_sum[:, at : at + PART],
                    jnp.zeros((1, DH), F32),
                    hidden_sums[:, block : block + quarter],
                    jnp.zeros((1, width - lanes - quarter), F32),
                ],
                axis=1,
            )
            out[i * size + 4 * PART : (i + 1) * size, :] = jnp.broadcast_to(row, (16, width)).astype(
                BF16
            )


def entry_product_kernel(first_pair, second_pair, first_weights, second_weights, *outs):
    joined = jnp.concatenate([first_pair[...], second_pair[...]], axis=1)
    weights = jnp.concatenate([first_weights[...], second_weights[...]], axis=0)
    found = nn(joined, weights).astype(BF16)
    at = 0
    for out in outs:
        out[...] = found[at : at + out.shape[0]]
        at += out.shape[0]


def entry_back_kernel(
    rows,
    valid,
    partial,
    from_core,
    from_y,
    stream,
    grad_middle,
    gain_vector,
    middle_sums,
    grad,
    heads,
    small,
):
    width = stream.shape[1]
    gain = row_of(gain_vector)
    totals = [jnp.zeros((8, width), F32) for _ in range(2)]
    for at in chunks(stream.shape[0]):
        found = partial[at, :].astype(F32) + from_core[at, :].astype(F32)
        found = found + from_y[at, :].astype(F32)
        hat, inverse = moment_norm(stream[at, :].astype(F32))
        grad[at, :] = grad_middle[at, :] + norm_back(found, hat, inverse, gain)
        for i, v in enumerate((found * hat, found)):
            totals[i] = totals[i] + folded(v)
    heads[...] = grad[0:8, :]
    small[...] = jnp.concatenate(
        [middle_sums[0:2, :]]
        + [jnp.sum(v, axis=0, keepdims=True) for v in totals]
        + [middle_sums[2:4, :], middle_sums[6:8, :]],
        axis=0,
    )


def exit_kernel(output, grad, after, output_rows, grad_rows, ext):
    _, _, z, y = coordinates()
    half = output.shape[0]
    rows = output_rows.shape[0]
    count = rows - y
    index = lax.broadcasted_iota(jnp.int32, (half, 1), 0)
    ext[8:, :] = jnp.zeros((half - 8, ext.shape[1]), F32)
    for values, at, out in ((output, 0, output_rows), (grad, 8, grad_rows)):
        ext[0:8, :] = after[at : at + 8, :]
        moved = pltpu.roll(values[...], half - z, 0)
        beyond = pltpu.roll(ext[...], count - z, 0)
        out[...] = jnp.where(index < count - z, moved, beyond)[:rows]


def attention_gradients_kernel(own, across, core, core_across, *outs):
    x, c, _, _ = coordinates()
    query, value, hidden = outs[4:]
    pieces = ((own, c, x), (across, c, 1 - x), (core, 1 - c, x), (core_across, 1 - c, 1 - x))
    for ref, c_of, x_of in pieces:
        at = pl.multiple_of(c_of * DH + x_of * PART, PART)
        for m in range(4):
            outs[m][pl.ds(at, PART), :] = ref[m * PART : (m + 1) * PART, :].astype(F32)
    rows = [ref[4 * PART :, :].astype(F32)[0:1] for ref, _, _ in pieces]
    natural = []
    for c_of in range(2):
        for x_of in range(2):
            same = jnp.where(x == x_of, rows[0], rows[1])
            changed = jnp.where(x == x_of, rows[2], rows[3])
            natural.append(jnp.where(c == c_of, same, changed))
    quarter = hidden.shape[0] // 4
    for out, at, size in ((query, 0, PART), (value, PART, PART), (hidden, 2 * DH, quarter)):
        found = jnp.concatenate([row[:, at : at + size] for row in natural], axis=1)
        out[...] = found.reshape(out.shape)


def mlp_in_gradient_kernel(own, across, core, core_across, out):
    x, c, _, _ = coordinates()
    pieces = ((own, c, x), (across, c, 1 - x), (core, 1 - c, x), (core_across, 1 - c, 1 - x))
    for ref, c_of, x_of in pieces:
        quarter = ref.shape[0]
        at = pl.multiple_of((2 * c_of + x_of) * quarter, quarter)
        out[:, pl.ds(at, quarter)] = ref[...].astype(F32).T


def swapped_sum_kernel(own, received, out):
    size = own.shape[0] // 2
    out[:size, :] = (own[:size, :].astype(F32) + received[size:, :].astype(F32)).astype(BF16)
    out[size:, :] = (own[size:, :].astype(F32) + received[:size, :].astype(F32)).astype(BF16)


def mlp_out_gradient_kernel(own, core, out):
    x, c, _, _ = coordinates()
    for ref, c_of in ((own, c), (core, 1 - c)):
        quarter = ref.shape[0] // 2
        for i, side in enumerate((x, 1 - x)):
            at = pl.multiple_of((2 * c_of + side) * quarter, quarter)
            out[pl.ds(at, quarter), :] = ref[i * quarter : (i + 1) * quarter, :].astype(F32)


def sums_kernel(small, received, *outs):
    found = small[...] + received[...]
    for i, out in enumerate(outs[:-1]):
        out[...] = found[i : i + 1].reshape(out.shape)
    outs[-1][...] = found[6:7, : outs[-1].shape[0]].reshape(outs[-1].shape)


def copy_kernel(source, target):
    target[...] = source[...]


def add_wide_kernel(first, second, out):
    out[...] = first[...] + second[...]


def add_split_last_kernel(keep, received, last, zero, one):
    size = zero.shape[0]
    zero[...] = (keep[:size, :].astype(F32) + received[:size, :].astype(F32)).astype(BF16)
    found = keep[size:, :].astype(F32) + received[size:, :].astype(F32)
    one[...] = (found + last[...].astype(F32)).astype(BF16)


def add_three_kernel(first, second, third, out):
    out[...] = (
        first[...].astype(F32) + second[...].astype(F32) + third[...].astype(F32)
    ).astype(BF16)


def on_device(
    inputs,
    valid,
    cotangent,
    w_query,
    w_key,
    w_value,
    b_query,
    b_value,
    w_attn_out,
    b_attn_out,
    w_mlp_in,
    b_mlp_in,
    w_mlp_out,
    b_mlp_out,
    attention_norm_gain,
    attention_norm_shift,
    feedforward_norm_gain,
    feedforward_norm_shift,
):
    rows, width = inputs.shape
    images = valid.shape[0]
    heads_local = w_query.shape[0] // DH
    hidden_local = w_mlp_out.shape[0]
    shape = (lax.axis_size("tok"), lax.axis_size("feat"), images, heads_local, hidden_local, width)
    if shape != (4, 8, 4, 2, 512, 1024) or 2 * rows != SEQ + 1:
        return on_device_general(
            inputs,
            valid,
            cotangent,
            w_query,
            w_key,
            w_value,
            b_query,
            b_value,
            w_attn_out,
            b_attn_out,
            w_mlp_in,
            b_mlp_in,
            w_mlp_out,
            b_mlp_out,
            attention_norm_gain,
            attention_norm_shift,
            feedforward_norm_gain,
            feedforward_norm_shift,
        )
    half = (rows + 15) // 16 * 16
    image = 2 * half
    quarter = hidden_local // 4
    piece = 4 * PART + 16
    row_block = (half, width)
    low_rows, wide_rows = (row_block, BF16), (row_block, F32)
    last, usual = (), 0.01
    calls, sent = [], []

    def send(values, pairs):
        found = lax.ppermute(values, AXES, pairs)
        sent.append(found)
        return found


    def call(body, operands, outs, scratch=(), gate=(), specs=None, span=None, final=False):
        nonlocal last
        specs = [VMEM] * len(operands) if specs is None else specs
        number = len(calls)
        calls.append(number)
        span = SPANS.get(number, usual if span is None else span)
        gate = [g for i, g in enumerate(gate) if i not in LATE.get(number, ())]
        gate += [sent[i] for i in EARLY.get(number, ()) if i < len(sent)]
        found = kernel_call(body, operands, specs, outs, scratch, last + tuple(gate), span)
        if not final:
            last = (min(found, key=lambda v: v.size * v.dtype.itemsize),)
        return found

    def pin(values, gate=()):
        return call(copy_kernel, (values,), [(values.shape, values.dtype)], gate=gate)[0]

    def far_sum(values, received, gate=(), sizes=(half,)):
        outs = [((size, width), BF16) for size in sizes]
        found = call(far_sum_kernel, (values, received), outs, gate=gate)
        return found if len(sizes) > 1 else found[0]

    def split(values, received, sizes, gate=()):
        outs = [((size, width), BF16) for size in sizes]
        return call(add_split_kernel, (values, received), outs, gate=gate)

    def add_last(values, one, three, gate=()):
        return call(add_three_kernel, (values, one, three), [(values.shape, BF16)], gate=gate)[0]

    in_hbm = [
        pltpu.with_memory_space_constraint(w, pltpu.HBM)
        for w in (w_query, w_key, w_value, w_attn_out, b_query, b_value, b_mlp_in)
    ]
    attn_own, attn_other, attn_both = call(
        attention_weights_kernel,
        in_hbm,
        [((piece, width), BF16)] * 2 + [((2 * piece, width), BF16)],
        scratch=[
            pltpu.VMEM((2 * DH,), BF16),
            pltpu.VMEM((2 * DH,), BF16),
            pltpu.VMEM((hidden_local,), BF16),
            pltpu.SemaphoreType.DMA((19,)),
        ],
        specs=[HBM] * 7,
    )
    own_one = send(attn_own, UP_Z)
    attn_three = send(attn_both, DOWN_Z)
    (edge,) = call(edge_kernel, (inputs, cotangent), [((16, width), BF16)])
    edge = send(edge, NEXT)
    mlp_own, mlp_other, mlp_both = call(
        mlp_weights_kernel,
        (w_mlp_in, w_mlp_out),
        [((2 * quarter, width), BF16)] * 2 + [((4 * quarter, width), BF16)],
    )
    stream, normed, branch_grad, branch_again = call(
        entry_kernel,
        (valid, inputs, cotangent, edge, attention_norm_gain, attention_norm_shift),
        [low_rows] * 4,
        scratch=[pltpu.VMEM((half + 8, width), F32)],
        gate=(own_one,),
        specs=[SMEM] + [VMEM] * 5, span=30)
    own_two = send(own_one, UP_Z)
    other_one = send(own_one, SWAP_X)
    normed_y, normed_c = send(normed, SWAP_Y), send(normed, SWAP_C)
    mlp_first = pin(mlp_own, (attn_three, normed_c))
    mlp_one = send(mlp_first, UP_Z)
    pin(edge, (own_two, other_one))
    other_two = send(own_two, SWAP_X)
    branch_again = pin(branch_again, (normed_y,))
    normed_yc = send(normed_y, SWAP_C)
    branch_y, branch_c = send(branch_again, SWAP_Y), send(branch_again, SWAP_C)

    lanes = 2 * DH
    pair_out = [((image, 3 * lanes), BF16)], [((2, image, image), BF16)], [((image, lanes), BF16)]
    weight_out = [((3 * lanes, width), BF16), ((lanes, width), BF16)]
    first_pair = call(
        functools.partial(first_pair_kernel, rows),
        (normed, normed_y, normed_c, normed_yc, attn_own, attn_other, own_one, other_one),
        pair_out[0] * 2 + pair_out[1] * 2 + pair_out[2] * 2 + weight_out,
        span=30,
    )
    w_first, out_first = first_pair[6:]
    qkv_other, probs_other, mixed_other, partial_other, w_second, out_second, second_bias = call(
        functools.partial(second_pair_other_kernel, rows),
        (normed_c, normed_yc, attn_three, own_two, other_two, first_pair[5], out_first),
        pair_out[0]
        + pair_out[1]
        + pair_out[2]
        + [((image, width), BF16)]
        + weight_out
        + [((8, 3 * lanes), F32)],
        gate=(branch_c,),
        span=30,
    )
    from_core = send(partial_other, SWAP_C)
    mlp_two = send(mlp_one, UP_Z)
    mlp_other_one = send(mlp_one, SWAP_X)
    qkv_own, probs_own, mixed_own, partial_near, partial_far = call(
        functools.partial(second_pair_own_kernel, rows),
        (normed, normed_y, w_second, out_second, second_bias, first_pair[4], out_first),
        pair_out[0] + pair_out[1] + pair_out[2] + [low_rows] * 2,
        gate=(mlp_one,),
        span=30,
    )
    saved = (
        (out_first,) + tuple(first_pair[:6]),
        (out_second, qkv_own, qkv_other, probs_own, probs_other, mixed_own, mixed_other),
    )
    parts_of_half = (half // 2 + 8, half - half // 2 - 8)
    attn_far = far_sum(partial_far, from_core, (branch_y,), parts_of_half)
    from_y = tuple(send(part, SWAP_Y) for part in attn_far)
    mlp_three = send(pin(mlp_both), DOWN_Z)
    branch_yc = send(branch_y, SWAP_C)
    middle, normed_middle, attn_power = call(
        functools.partial(middle_kernel, rows),
        (valid, partial_near, from_core) + from_y + (stream,)
        + (b_attn_out, feedforward_norm_gain, feedforward_norm_shift),
        [wide_rows, low_rows, ((8, width), F32)],
        gate=(mlp_other_one, branch_yc),
        specs=[SMEM] + [VMEM] * 8, span=30)
    middle_y, middle_c = send(normed_middle, SWAP_Y), send(normed_middle, SWAP_C)
    pin(attn_power, (mlp_two, middle_c))
    mlp_other_two = send(mlp_two, SWAP_X)

    usual = 10
    middle_yc = send(middle_y, SWAP_C)
    pieces = (mlp_own, mlp_other, mlp_one, mlp_other_one, mlp_three, mlp_two, mlp_other_two)
    pieces += (attn_own, own_one, attn_three, own_two)
    mlp_out = (
        [((image, 8 * quarter), BF16)] * 2 + [low_rows] * 4 + [((8, 8 * quarter), F32)]
    )
    chip = call(
        mlp_kernel,
        (normed_middle, middle_c, branch_grad, branch_c) + pieces,
        mlp_out,
        gate=(middle_y,),
    )
    mid_core, out_core = send(chip[3], SWAP_C), send(chip[5], SWAP_C)
    distant = call(mlp_kernel, (middle_y, middle_yc, branch_y, branch_yc) + pieces, mlp_out)
    out_distant = send(distant[5], SWAP_C)
    mid_far = far_sum(distant[2], send(distant[3], SWAP_C), (mid_core, out_core))
    mid_y = send(mid_far, SWAP_Y)

    grad_out = call(
        functools.partial(products_kernel, True),
        (chip[0], distant[0], branch_grad, branch_c, branch_y, branch_yc),
        [((2 * quarter, width), BF16)] * 4,
        gate=(out_distant,),
    )
    grad_out = dict(zip(SLOTS, grad_out))
    out_two = send(grad_out[2], DOWN_Z)
    out_three = send(grad_out[3], UP_Z)
    grad_in_keep, grad_in_give = call(
        functools.partial(products_kernel, False),
        (chip[1], distant[1], normed_middle, middle_c, middle_y, middle_yc),
        [((4 * quarter, width), BF16)] * 2,
    )
    in_received = send(grad_in_give, SWAP_X)
    grad_middle, grad_attn, middle_sums = call(
        middle_back_kernel,
        (chip[2], mid_core, mid_y, middle, branch_grad, feedforward_norm_gain),
        [wide_rows, low_rows, ((8, width), F32)],
    )
    grad_y, grad_c = send(grad_attn, SWAP_Y), send(grad_attn, SWAP_C)
    out_far = far_sum(distant[4], out_distant)
    (one,) = split(grad_out[1], out_two, (2 * quarter,), (grad_c,))
    out_one = send(one, DOWN_Z)
    grad_yc = send(grad_y, SWAP_C)

    def backward(p, gate=()):
        return call(
            functools.partial(backward_kernel, p),
            (grad_attn, grad_y, grad_c, grad_yc, normed, normed_y, normed_c, normed_yc)
            + saved[p]
            + (chip[6], distant[6]),
            [((image, 6 * DH), BF16)] * 2 + [((2 * piece, width), BF16)] * 2,
            gate=gate,
        )

    second_own, second_other, give, keep = backward(1)
    received = send(give, SWAP_X)
    out_y = send(pin(out_far), SWAP_Y)
    first_own, first_other, give_first, keep_first = backward(0, (out_one, out_three))
    received_first = send(give_first, SWAP_X)
    in_pieces = split(grad_in_keep, in_received, (quarter,) * 4)
    in_pieces = dict(zip(SLOTS, in_pieces))
    in_two = send(in_pieces[2], DOWN_Z)
    in_three = send(in_pieces[3], UP_Z)
    (entry_other,) = call(
        entry_product_kernel, (first_other, second_other, w_first, w_second), [((image, width), BF16)]
    )
    entry_core = send(entry_other, SWAP_C)
    entry_near, entry_far = call(
        entry_product_kernel, (first_own, second_own, w_first, w_second), [low_rows] * 2
    )
    entry_far = far_sum(entry_far, entry_core)
    entry_y = send(entry_far, SWAP_Y)
    three, two = split(keep, received, (piece,) * 2, (in_three,))
    attn_two = send(two, DOWN_Z)
    attn_three = send(three, UP_Z)
    (one,) = split(in_pieces[1], in_two, (quarter,))
    in_one = send(one, DOWN_Z)
    output, output_heads, power_sums = call(
        functools.partial(output_kernel, rows),
        (valid, chip[4], out_core, out_y, middle, stream, b_mlp_out, attn_power, middle_sums),
        [wide_rows, ((8, width), F32), ((8, width), F32)],
        specs=[SMEM] + [VMEM] * 8,
    )
    out_total = call(
        add_three_kernel,
        (grad_out[0], out_one, out_three),
        [((2 * quarter, width), BF16)],
        gate=(received_first,),
    )[0]
    out_across = send(out_total, SWAP_X)
    zero, one = call(
        add_split_last_kernel,
        (keep_first, received_first, attn_two),
        [((piece, width), BF16)] * 2,
    )
    attn_one = send(one, DOWN_Z)
    gradient, heads, small = call(
        functools.partial(entry_back_kernel, rows),
        (valid, entry_near, entry_core, entry_y, stream, grad_middle)
        + (attention_norm_gain, power_sums),
        [wide_rows, ((8, width), F32), ((8, width), F32)],
        gate=(attn_three,),
        specs=[SMEM] + [VMEM] * 7,
    )

    def add_small(received, gate=()):
        return call(add_wide_kernel, (small, received), [(small.shape, F32)], gate=gate)[0]

    heads_after = send(jnp.concatenate([output_heads, heads]), PREVIOUS)
    small = add_small(send(small, SWAP_C))
    small_y = send(small, SWAP_Y)
    attn_total = add_last(zero, attn_one, attn_three, (out_across,))
    attn_across, attn_core = send(attn_total, SWAP_X), send(attn_total, SWAP_C)
    small = add_small(small_y, (attn_core, heads_after))
    small_z = send(small, FLIP_Z[1])
    output_rows, gradient_rows = call(
        exit_kernel,
        (output, gradient, heads_after),
        [((rows, width), F32)] * 2,
        scratch=[pltpu.VMEM((half, width), F32)], final=True)
    small = add_small(small_z)
    small_z = send(small, FLIP_Z[2])
    in_total = add_last(in_pieces[0], in_one, in_three)
    in_across, in_core = send(in_total, SWAP_X), send(in_total, SWAP_C)
    (out_whole,) = call(
        swapped_sum_kernel,
        (out_total, out_across),
        [((2 * quarter, width), BF16)],
        gate=(attn_across,),
    )
    out_core = send(out_whole, SWAP_C)
    attn_last = send(attn_across, SWAP_C)
    small = add_small(small_z, (in_core,))
    small_x = send(small, SWAP_X)
    attn_grads = call(
        attention_gradients_kernel,
        (attn_total, attn_across, attn_core, attn_last),
        [((2 * DH, width), F32)] * 4
        + [((2 * DH,), F32), ((2 * DH,), F32), ((hidden_local,), F32)], final=True)
    in_last = send(in_across, SWAP_C)
    (grad_w_mlp_out,) = call(
        mlp_out_gradient_kernel, (out_whole, out_core), [((hidden_local, width), F32)], final=True)
    (grad_w_mlp_in,) = call(
        mlp_in_gradient_kernel,
        (in_total, in_across, in_core, in_last),
        [((width, hidden_local), F32)], final=True)
    *vectors, powers = call(
        sums_kernel, (small, small_x), [((width,), F32)] * 6 + [((2 * DH,), F32)], final=True)
    stream_rms = jnp.sqrt(powers[:4] / (jnp.maximum(powers[4], 1.0) * D))
    return (
        output_rows,
        gradient_rows,
        attn_grads[0],
        attn_grads[1],
        attn_grads[2],
        attn_grads[4],
        attn_grads[5],
        attn_grads[3],
        vectors[0],
        grad_w_mlp_in,
        attn_grads[6],
        grad_w_mlp_out,
        vectors[1],
        vectors[2],
        vectors[3],
        vectors[4],
        vectors[5],
        stream_rms,
    )


def solution(mesh):
    in_specs = (
        P(("tok", "feat"), None),
        P("tok"),
        P(("tok", "feat"), None),
        P("feat", None),
        P("feat", None),
        P("feat", None),
        P("feat"),
        P("feat"),
        P("feat", None),
        P(),
        P(None, "feat"),
        P("feat"),
        P("feat", None),
        P(),
        P(),
        P(),
        P(),
        P(),
    )
    out_specs = (
        P(("tok", "feat"), None),
        P(("tok", "feat"), None),
        P("feat", None),
        P("feat", None),
        P("feat", None),
        P("feat"),
        P("feat"),
        P("feat", None),
        P(),
        P(None, "feat"),
        P("feat"),
        P("feat", None),
        P(),
        P(),
        P(),
        P(),
        P(),
        P(),
    )
    return jax.shard_map(
        on_device, mesh=mesh, in_specs=in_specs, out_specs=out_specs, check_vma=False
    )
```

```python
import functools

import jax
import jax.numpy as jnp
from jax import lax
from jax.experimental import pallas as pl
from jax.experimental.pallas import tpu as pltpu
from jax.sharding import PartitionSpec as P

D = 1024
DH = 64
SEQ = 577


EPSILON = 1e-05
SLOPE = 1.702


def gelu_slope(values):
    sigmoid = jax.nn.sigmoid(SLOPE * values)
    return sigmoid + SLOPE * values * sigmoid * (1.0 - sigmoid)


def column_sums(values):
    return jnp.sum(values.astype(jnp.float32), axis=0)


def split_heads(values):
    return values.reshape(values.shape[0], values.shape[1] // DH, DH)


def apply_layer_norm(values):
    center = jnp.mean(values, axis=1, keepdims=True)
    spread = jnp.mean(values * values, axis=1, keepdims=True) - center * center
    inverse_deviation = lax.rsqrt(spread + EPSILON)
    return ((values - center) * inverse_deviation, inverse_deviation)


def layer_norm_backward(normalized_gradient, centered_scaled, inverse_deviation, norm_gain):
    scaled_output = normalized_gradient * norm_gain.astype(jnp.float32)
    plain_output = jnp.mean(scaled_output, axis=1, keepdims=True)
    cross_term = jnp.mean(scaled_output * centered_scaled, axis=1, keepdims=True)
    return inverse_deviation * (scaled_output - plain_output - centered_scaled * cross_term)


def image_forward(blocks):
    query_img, key_img, value_img = blocks
    scale = DH ** (-0.5)
    query_heads = split_heads(query_img)
    key_heads = split_heads(key_img)
    value_heads = split_heads(value_img)
    scores = (
        jnp.einsum("qhd,khd->hqk", query_heads, key_heads, preferred_element_type=jnp.float32)
        * scale
    )
    top_score = jnp.max(scores, axis=-1, keepdims=True)
    weights = jnp.exp(scores - top_score)
    total = jnp.sum(weights, axis=-1, keepdims=True)
    probs = (weights / total).astype(jnp.bfloat16)
    mixed = jnp.einsum("hqk,khd->qhd", probs, value_heads, preferred_element_type=jnp.float32)
    log_total = top_score[..., 0] + jnp.log(total[..., 0])
    return (mixed.reshape(query_img.shape).astype(jnp.bfloat16), log_total)


def image_backward(blocks):
    query_img, key_img, value_img, grad_img, log_total = blocks
    scale = DH ** (-0.5)
    query_heads = split_heads(query_img)
    key_heads = split_heads(key_img)
    value_heads = split_heads(value_img)
    grad_heads = split_heads(grad_img)
    scores = (
        jnp.einsum("qhd,khd->hqk", query_heads, key_heads, preferred_element_type=jnp.float32)
        * scale
    )
    probs = jnp.exp(scores - log_total[..., None])
    probs_low = probs.astype(jnp.bfloat16)
    grad_probs = jnp.einsum(
        "qhd,khd->hqk", grad_heads, value_heads, preferred_element_type=jnp.float32
    )
    grad_value = jnp.einsum(
        "hqk,qhd->khd", probs_low, grad_heads, preferred_element_type=jnp.float32
    )
    inner = jnp.sum(probs * grad_probs, axis=-1, keepdims=True)
    grad_scores = (probs * (grad_probs - inner)).astype(jnp.bfloat16)
    grad_query = (
        jnp.einsum("hqk,khd->qhd", grad_scores, key_heads, preferred_element_type=jnp.float32)
        * scale
    )
    grad_key = (
        jnp.einsum("hqk,qhd->khd", grad_scores, query_heads, preferred_element_type=jnp.float32)
        * scale
    )
    shape_img = query_img.shape
    return (
        grad_query.reshape(shape_img).astype(jnp.bfloat16),
        grad_key.reshape(shape_img).astype(jnp.bfloat16),
        grad_value.reshape(shape_img).astype(jnp.bfloat16),
    )


def by_image(values, images):
    return values.reshape(images, values.shape[0] // images, values.shape[1])


def on_device_general(
    inputs,
    valid,
    cotangent,
    w_query,
    w_key,
    w_value,
    b_query,
    b_value,
    w_attn_out,
    b_attn_out,
    w_mlp_in,
    b_mlp_in,
    w_mlp_out,
    b_mlp_out,
    attention_norm_gain,
    attention_norm_shift,
    feedforward_norm_gain,
    feedforward_norm_shift,
):
    row_count, width = inputs.shape
    images = valid.shape[0]
    group_rows = images * SEQ
    parts = lax.axis_size("feat")
    extra = row_count * parts - group_rows
    width_local = w_query.shape[0]
    hidden_local = w_mlp_out.shape[0]
    global_rows = lax.axis_index("feat") * row_count + jnp.arange(row_count, dtype=jnp.int32)
    owner = global_rows // SEQ
    matches = (owner[:, None] == jnp.arange(images, dtype=jnp.int32)[None, :]).astype(jnp.float32)
    row_mask = jnp.sum(matches * valid.astype(jnp.float32)[None, :], axis=1)
    live = (global_rows < group_rows).astype(jnp.float32)[:, None]

    def padded(values):
        return jnp.pad(values, ((0, extra), (0, 0)))

    local_input_rows = inputs.astype(jnp.float32)
    first_centered_scaled, first_inverse_deviation = apply_layer_norm(local_input_rows)
    normalized_first = (
        first_centered_scaled * attention_norm_gain.astype(jnp.float32)
        + attention_norm_shift.astype(jnp.float32)
    ).astype(jnp.bfloat16)
    normed_full = lax.all_gather(normalized_first, "feat", axis=0, tiled=True)[:group_rows]
    w_qkv = jnp.concatenate([w_query, w_key, w_value], axis=0)
    projected = jnp.einsum("rd,cd->rc", normed_full, w_qkv, preferred_element_type=jnp.float32)
    queries = (projected[:, :width_local] + b_query.astype(jnp.float32)).astype(jnp.bfloat16)
    key_rows = projected[:, width_local : 2 * width_local].astype(jnp.bfloat16)
    value_rows = (projected[:, 2 * width_local :] + b_value.astype(jnp.float32)).astype(
        jnp.bfloat16
    )
    mixed, log_totals = lax.map(
        image_forward,
        (by_image(queries, images), by_image(key_rows, images), by_image(value_rows, images)),
    )
    mixed = mixed.reshape(group_rows, width_local)
    partial_out = jnp.dot(mixed, w_attn_out, preferred_element_type=jnp.float32)
    attn = lax.psum_scatter(
        padded(partial_out), "feat", scatter_dimension=0, tiled=True
    ) + b_attn_out.astype(jnp.float32)
    middle_state = local_input_rows + attn
    second_centered_scaled, second_inverse_deviation = apply_layer_norm(middle_state)
    normalized_middle = (
        second_centered_scaled * feedforward_norm_gain.astype(jnp.float32)
        + feedforward_norm_shift.astype(jnp.float32)
    ).astype(jnp.bfloat16)
    mid_full = lax.all_gather(normalized_middle, "feat", axis=0, tiled=True)[:group_rows]
    hidden = jnp.dot(mid_full, w_mlp_in, preferred_element_type=jnp.float32) + b_mlp_in.astype(
        jnp.float32
    )
    active = (hidden * jax.nn.sigmoid(SLOPE * hidden)).astype(jnp.bfloat16)
    partial_mlp = jnp.dot(active, w_mlp_out, preferred_element_type=jnp.float32)
    branch = lax.psum_scatter(
        padded(partial_mlp).astype(jnp.bfloat16), "feat", scatter_dimension=0, tiled=True
    ).astype(jnp.float32) + b_mlp_out.astype(jnp.float32)
    output = (middle_state + branch) * live
    output_gradient = cotangent.astype(jnp.float32) * row_mask[:, None]
    grad_branch = output_gradient.astype(jnp.bfloat16)
    grad_b_mlp_out = column_sums(grad_branch)
    branch_full = lax.all_gather(grad_branch, "feat", axis=0, tiled=True)[:group_rows]
    grad_w_mlp_out = jnp.einsum(
        "rf,rd->fd", active, branch_full, preferred_element_type=jnp.float32
    )
    grad_active = jnp.einsum(
        "rd,fd->rf", branch_full, w_mlp_out, preferred_element_type=jnp.float32
    )
    grad_hidden = (grad_active * gelu_slope(hidden)).astype(jnp.bfloat16)
    grad_b_mlp_in = column_sums(grad_hidden)
    grad_mlp_in_rows = jnp.einsum(
        "rf,rd->fd", grad_hidden, mid_full, preferred_element_type=jnp.float32
    )
    partial_mid = jnp.einsum("rf,df->rd", grad_hidden, w_mlp_in, preferred_element_type=jnp.float32)
    midpoint_gradient = lax.psum_scatter(
        padded(partial_mid), "feat", scatter_dimension=0, tiled=True
    )
    feedforward_gain_gradient = jnp.sum(midpoint_gradient * second_centered_scaled, axis=0)
    grad_s_mlp = jnp.sum(midpoint_gradient, axis=0)
    middle_state_gradient = output_gradient + layer_norm_backward(
        midpoint_gradient, second_centered_scaled, second_inverse_deviation, feedforward_norm_gain
    )
    grad_attn = middle_state_gradient.astype(jnp.bfloat16)
    grad_b_attn_out = column_sums(grad_attn)
    attn_full = lax.all_gather(grad_attn, "feat", axis=0, tiled=True)[:group_rows]
    grad_w_attn_out = jnp.einsum("rh,rd->hd", mixed, attn_full, preferred_element_type=jnp.float32)
    grad_mixed = jnp.einsum(
        "rd,hd->rh", attn_full, w_attn_out, preferred_element_type=jnp.float32
    ).astype(jnp.bfloat16)
    grad_query, grad_key, grad_value = lax.map(
        image_backward,
        (
            by_image(queries, images),
            by_image(key_rows, images),
            by_image(value_rows, images),
            by_image(grad_mixed, images),
            log_totals,
        ),
    )
    grad_query = grad_query.reshape(group_rows, width_local)
    grad_key = grad_key.reshape(group_rows, width_local)
    grad_value = grad_value.reshape(group_rows, width_local)
    grad_b_query = column_sums(grad_query)
    grad_b_value = column_sums(grad_value)
    grad_qkv = jnp.concatenate([grad_query, grad_key, grad_value], axis=1)
    grad_w_qkv = jnp.einsum("rc,rd->cd", grad_qkv, normed_full, preferred_element_type=jnp.float32)
    partial_in = jnp.einsum("rc,cd->rd", grad_qkv, w_qkv, preferred_element_type=jnp.float32)
    normalized_gradient = lax.psum_scatter(
        padded(partial_in).astype(jnp.bfloat16), "feat", scatter_dimension=0, tiled=True
    ).astype(jnp.float32)
    attention_gain_gradient = jnp.sum(normalized_gradient * first_centered_scaled, axis=0)
    grad_s_attn = jnp.sum(normalized_gradient, axis=0)
    layer_input_gradient = middle_state_gradient + layer_norm_backward(
        normalized_gradient, first_centered_scaled, first_inverse_deviation, attention_norm_gain
    )
    local_powers = jnp.stack(
        [
            jnp.sum(row_mask[:, None] * local_input_rows * local_input_rows),
            jnp.sum(row_mask[:, None] * attn * attn),
            jnp.sum(row_mask[:, None] * branch * branch),
            jnp.sum(row_mask[:, None] * output * output),
        ]
    )
    local_count = jnp.sum(row_mask)
    bias_entries = jnp.concatenate([grad_b_query, grad_b_value, grad_b_mlp_in])
    bias_row = jnp.pad(bias_entries, (0, width - bias_entries.shape[0]))[None, :]
    packed = jnp.concatenate(
        [grad_w_qkv, grad_w_attn_out, grad_mlp_in_rows, grad_w_mlp_out, bias_row], axis=0
    )
    packed_rows = packed.shape[0]
    tok_parts = lax.axis_size("tok")
    fill_rows = (tok_parts - packed_rows % tok_parts) % tok_parts
    packed = jnp.pad(packed, ((0, fill_rows), (0, 0)))
    shares = lax.psum_scatter(
        packed.astype(jnp.bfloat16), "tok", scatter_dimension=0, tiled=True
    ).astype(jnp.float32)
    summed = lax.all_gather(shares.astype(jnp.bfloat16), "tok", axis=0, tiled=True).astype(
        shares.dtype
    )[:packed_rows]
    offset = 0
    grad_w_query = summed[offset : offset + width_local]
    offset += width_local
    grad_w_key = summed[offset : offset + width_local]
    offset += width_local
    grad_w_value = summed[offset : offset + width_local]
    offset += width_local
    grad_w_attn_out = summed[offset : offset + width_local]
    offset += width_local
    grad_w_mlp_in = summed[offset : offset + hidden_local].T
    offset += hidden_local
    grad_w_mlp_out = summed[offset : offset + hidden_local]
    offset += hidden_local
    bias_sums = summed[offset]
    grad_b_query = bias_sums[:width_local]
    grad_b_value = bias_sums[width_local : 2 * width_local]
    grad_b_mlp_in = bias_sums[2 * width_local : 2 * width_local + hidden_local]
    (
        grad_b_attn_out,
        grad_b_mlp_out,
        attention_gain_gradient,
        grad_s_attn,
        feedforward_gain_gradient,
        grad_s_mlp,
        powers,
        counted,
    ) = lax.psum(
        (
            grad_b_attn_out,
            grad_b_mlp_out,
            attention_gain_gradient,
            grad_s_attn,
            feedforward_gain_gradient,
            grad_s_mlp,
            local_powers,
            local_count,
        ),
        ("tok", "feat"),
    )
    stream_rms = jnp.sqrt(powers / (jnp.maximum(counted, 1.0) * D))
    return (
        output,
        layer_input_gradient,
        grad_w_query,
        grad_w_key,
        grad_w_value,
        grad_b_query,
        grad_b_value,
        grad_w_attn_out,
        grad_b_attn_out,
        grad_w_mlp_in,
        grad_b_mlp_in,
        grad_w_mlp_out,
        grad_b_mlp_out,
        attention_gain_gradient,
        grad_s_attn,
        feedforward_gain_gradient,
        grad_s_mlp,
        stream_rms,
    )


BF16 = jnp.bfloat16
F32 = jnp.float32
AXES = ("tok", "feat")
SLOTS = (0, 1, 3, 2)
PAIRS = ((0, 1), (3, 2))
CHUNK = 16
PART = DH // 2


SPANS = {
    0: 6,
    1: 1,
    2: 0.01,
    4: 10,
    5: 6,
    6: 60,
    7: 6,
    8: 0.01,
    9: 30,
    10: 6,
    11: 6,
    12: 6,
    13: 1,
    14: 1,
    15: 3,
    16: 3,
    17: 10,
    18: 6,
    19: 1,
    20: 3,
    22: 10,
    24: 3,
    25: 3,
    26: 10,
    27: 1,
    28: 60,
    29: 0.01,
    30: 0.01,
    31: 3,
    32: 3,
    33: 3,
    34: 6,
    35: 60,
    36: 1,
    37: 0.01,
    38: 60,
    39: 0.01,
    41: 60,
    42: 0.01,
    43: 6,
    45: 10,
    46: 0.01,
    47: 0.01,
    48: 0.01,
}
EARLY = {
    2: (2,),
    3: (0,),
    10: (2,),
    15: (21,),
    17: (26, 22, 24),
    18: (24,),
    19: (25,),
    20: (17,),
    21: (26,),
    24: (31, 30),
    25: (17,),
    27: (32,),
    28: (36,),
    30: (29,),
    32: (39,),
    33: (37,),
    35: (43,),
    36: (42,),
    38: (47,),
    40: (53,),
    41: (53,),
    42: (45, 49),
    44: (59, 56, 34),
    45: (56, 58, 42),
}
LATE = {
    7: (0,),
    13: (1,),
    15: (0,),
    17: (1,),
    22: (0,),
    30: (0,),
    42: (0,),
    45: (0,),
}


def route(move):
    found = []
    for tok in range(4):
        for feat in range(8):
            target = move(tok // 2, tok % 2, feat // 2, feat % 2)
            if target is not None:
                x, c, z, y = target
                found.append((tok * 8 + feat, (2 * x + c) * 8 + 2 * z + y))
    return found


SWAP_X = route(lambda x, c, z, y: (1 - x, c, z, y))
SWAP_C = route(lambda x, c, z, y: (x, 1 - c, z, y))
SWAP_Y = route(lambda x, c, z, y: (x, c, z, 1 - y))
UP_Z = route(lambda x, c, z, y: (x, c, (z + 1) % 4, y))
DOWN_Z = route(lambda x, c, z, y: (x, c, (z + 3) % 4, y))
FLIP_Z = [route(lambda x, c, z, y, s=s: (x, c, z ^ s, y)) for s in range(4)]
NEXT = [(t * 8 + f, t * 8 + f + 1) for t in range(4) for f in range(7)]
PREVIOUS = [(t * 8 + f + 1, t * 8 + f) for t in range(4) for f in range(7)]


def nt(left, right):
    return lax.dot_general(left, right, (((1,), (1,)), ((), ())), preferred_element_type=F32)


def nn(left, right):
    return lax.dot_general(left, right, (((1,), (0,)), ((), ())), preferred_element_type=F32)


def tn(left, right):
    return lax.dot_general(left, right, (((0,), (0,)), ((), ())), preferred_element_type=F32)


SMEM = pl.BlockSpec(memory_space=pltpu.SMEM)
HBM = pl.BlockSpec(memory_space=pltpu.HBM)
VMEM = pl.BlockSpec(memory_space=pltpu.VMEM)


def kernel_call(body, operands, specs, outs, scratch=(), after=(), span=0.01, vmem=12):
    count, extra = len(operands), len(after)

    def kernel(*refs):
        body(*refs[:count], *refs[count + extra :])

    return pl.pallas_call(
        kernel,
        in_specs=list(specs) + [VMEM] * extra,
        out_specs=[VMEM] * len(outs),
        out_shape=[jax.ShapeDtypeStruct(shape, dtype) for shape, dtype in outs],
        scratch_shapes=list(scratch),
        compiler_params=pltpu.CompilerParams(
            vmem_limit_bytes=vmem * 2**20, fuse_transposed_lhs_in_matmul=True
        ),
        cost_estimate=pl.CostEstimate(
            flops=int(span * 1e9), bytes_accessed=2**16, transcendentals=0
        ),
    )(*operands, *after)


def coordinates():
    tok, feat = lax.axis_index("tok"), lax.axis_index("feat")
    return tok // 2, tok % 2, feat // 2, feat % 2


def chunks(half):
    return [slice(at, at + CHUNK) for at in range(0, half, CHUNK)]


def row_of(vector):
    return vector[...].astype(F32).reshape(1, vector.shape[0])


def folded(values):
    return values[:8] + values[8:]


def moment_norm(values):
    center = jnp.mean(values, axis=1, keepdims=True)
    spread = jnp.mean(values * values, axis=1, keepdims=True) - center * center
    inverse = lax.rsqrt(spread + EPSILON)
    return (values - center) * inverse, inverse


def attention_weights_kernel(wq, wk, wv, wo, b_query, b_value, b_hidden, *refs):
    own, other, both, query, value, hidden, sems = refs
    piece = own.shape[0]
    x, c, _, _ = coordinates()
    width = own.shape[1]
    copies = []
    for source, target in ((b_query, query), (b_value, value), (b_hidden, hidden)):
        copies.append(pltpu.make_async_copy(source, target, sems.at[len(copies)]))
    targets = ((own, 0, x), (other, 0, 1 - x), (both, 0, x), (both, piece, 1 - x))
    for out, first, side in targets:
        at = pl.multiple_of(c * DH + side * PART, PART)
        for m, w in enumerate((wq, wk, wv, wo)):
            copies.append(
                pltpu.make_async_copy(
                    w.at[pl.ds(at, PART)], out.at[pl.ds(first + m * PART, PART)], sems.at[len(copies)]
                )
            )
    for copy in copies:
        copy.start()
    for copy in copies[:3]:
        copy.wait()
    parts = [row_of(vector) for vector in (query, value, hidden)]
    taken = sum(part.shape[1] for part in parts)
    bias = jnp.concatenate(parts + [jnp.zeros((1, width - taken), F32)], axis=1)
    bias = jnp.broadcast_to(bias, (16, width)).astype(BF16)
    for out, first, _ in targets:
        out[first + 4 * PART : first + piece, :] = bias
    for copy in copies[3:]:
        copy.wait()


def edge_kernel(inputs, cotangent, edge):
    rows = inputs.shape[0]
    at = (rows - 8) // 16 * 16
    for i, values in enumerate((inputs, cotangent)):
        edge[8 * i : 8 * i + 8, :] = values[at:, :].astype(F32)[rows - 8 - at :].astype(BF16)


def mlp_weights_kernel(w_in, w_out, own, other, both):
    x, c, _, _ = coordinates()
    quarter = own.shape[0] // 2
    for out, first, side in ((own, 0, x), (other, 2 * quarter, 1 - x)):
        at = pl.multiple_of((2 * c + side) * quarter, quarter)
        found = w_in[:, pl.ds(at, quarter)].T
        rest = w_out[pl.ds(at, quarter), :]
        out[:quarter, :] = found
        out[quarter:, :] = rest
        both[first : first + quarter, :] = found
        both[first + quarter : first + 2 * quarter, :] = rest


def halves_of(refs, count):
    own_zero, other_zero, own_one, other_one, both, own_two, other_two = refs
    own = [own_zero, own_one, both.at[pl.ds(0, count)], own_two]
    return own, [other_zero, other_one, both.at[pl.ds(count, count)], other_two]


def entry_kernel(
    valid, inputs, cotangent, edge, gain_vector, shift_vector, stream, normed, branch, again, ext
):
    _, _, z, y = coordinates()
    rows = inputs.shape[0]
    half = stream.shape[0]
    gain, shift = row_of(gain_vector), row_of(shift_vector)
    flag = valid[z].astype(F32)

    def aligned(at):
        found = pltpu.roll(ext[at.start : at.stop + 8, :], CHUNK + z, 0)[:CHUNK]
        index = at.start + lax.broadcasted_iota(jnp.int32, (CHUNK, 1), 0)
        return jnp.where(index < rows - y, found, 0.0)

    def fill(values, first):
        ext[0:8, :] = edge[...].astype(F32)[first : first + 8]
        ext[8 : 8 + rows, :] = values[...].astype(F32)

    fill(inputs, 0)
    for at in chunks(half):
        found = aligned(at)
        stream[at, :] = found.astype(BF16)
        hat, _ = moment_norm(found)
        normed[at, :] = (hat * gain + shift).astype(BF16)
    fill(cotangent, 8)
    for at in chunks(half):
        branch[at, :] = (aligned(at) * flag).astype(BF16)
        again[at, :] = branch[at, :]


def softmax_columns(scores):
    top = jnp.max(scores, axis=0, keepdims=True)
    weights = jnp.exp(scores - top)
    return weights * (1.0 / jnp.sum(weights, axis=0, keepdims=True))


def pair_forward(rows, halves, w_in, bias, qkv, probs, mixed):
    half = halves[0].shape[0]
    _, _, _, y = coordinates()
    lanes = 2 * DH
    entry = jnp.concatenate([halves[0][...], halves[1][...]], axis=0)
    qkv[...] = (nt(entry, w_in) + bias).astype(BF16)
    key_index = lax.broadcasted_iota(jnp.int32, (2 * half, 1), 0)
    first = rows - y
    second = half + rows - 1 + y
    real = (key_index < first) | ((key_index >= half) & (key_index < second))
    penalty = jnp.where(real, 0.0, -1e30)
    outs = []
    for h in range(2):
        q = qkv[:, h * DH : (h + 1) * DH] * jnp.asarray(DH ** (-0.5), BF16)
        k = qkv[:, lanes + h * DH : lanes + (h + 1) * DH]
        v = qkv[:, 2 * lanes + h * DH : 2 * lanes + (h + 1) * DH]
        found = softmax_columns(nt(k, q) + penalty).astype(BF16)
        probs[h] = found
        outs.append(tn(v, found))
    mixed[...] = jnp.concatenate(outs, axis=0).T.astype(BF16)


def pair_weights(own, other, w_in, w_out):
    for m in range(4):
        target = w_out if m == 3 else w_in
        for i in range(2):
            at = (0 if m == 3 else m * 2 * DH) + i * DH
            target[at : at + PART, :] = own[i][m * PART : (m + 1) * PART, :]
            target[at + PART : at + DH, :] = other[i][m * PART : (m + 1) * PART, :]
    rows_of = [own[i][4 * PART : 4 * PART + 16, :].astype(F32)[0:1] for i in range(2)]
    query = jnp.concatenate([ordered_bias(r, 0) for r in rows_of], axis=1)
    value = jnp.concatenate([ordered_bias(r, 2 * DH) for r in rows_of], axis=1)
    return jnp.concatenate([query, jnp.zeros_like(query), value], axis=1)


def projected(first_mixed, second_mixed, first_out, second_out, outs):
    mixed = jnp.concatenate([first_mixed[...], second_mixed[...]], axis=1)
    weights = jnp.concatenate([first_out[...], second_out[...]], axis=0)
    found = nn(mixed, weights).astype(BF16)
    at = 0
    for out in outs:
        out[...] = found[at : at + out.shape[0]]
        at += out.shape[0]


def ordered_bias(row, first):
    x, c, _, _ = coordinates()
    block = jnp.where(c == 0, row[:, first : first + DH], row[:, first + DH : first + 2 * DH])
    swapped = jnp.concatenate([block[:, PART:], block[:, :PART]], axis=1)
    return jnp.where(x == 0, block, swapped)


def first_pair_kernel(rows, near, far, near_other, far_other, *refs):
    own_zero, other_zero, own_one, other_one, *refs = refs
    qkv_own, qkv_other, probs_own, probs_other, mixed_own, mixed_other, w_in, w_out = refs
    bias = pair_weights((own_zero, own_one), (other_zero, other_one), w_in, w_out)
    weights = w_in[...]
    pair_forward(rows, (near_other, far_other), weights, bias, qkv_other, probs_other, mixed_other)
    pair_forward(rows, (near, far), weights, bias, qkv_own, probs_own, mixed_own)


def second_pair_other_kernel(rows, near, far, both, own_two, other_two, *refs):
    first_mixed, first_out, qkv, probs, mixed, partial, w_in, w_out, bias = refs
    piece = own_two.shape[0]
    own = (both.at[pl.ds(0, piece)], own_two)
    other = (both.at[pl.ds(piece, piece)], other_two)
    found = pair_weights(own, other, w_in, w_out)
    bias[...] = jnp.broadcast_to(found, bias.shape)
    pair_forward(rows, (near, far), w_in[...], found, qkv, probs, mixed)
    projected(first_mixed, mixed, first_out, w_out, (partial,))


def second_pair_own_kernel(rows, near, far, w_in, w_out, bias, first_mixed, first_out, *refs):
    qkv, probs, mixed, *partials = refs
    pair_forward(rows, (near, far), w_in[...], bias[0:1, :], qkv, probs, mixed)
    projected(first_mixed, mixed, first_out, w_out, partials)


def joined_rows(refs, at):
    size = refs[0].shape[0]
    if at.start < size:
        return refs[0][at, :]
    return refs[1][at.start - size : at.stop - size, :]


def real_rows(at, rows, y):
    return at.start + lax.broadcasted_iota(jnp.int32, (CHUNK, 1), 0) < rows - y


def middle_kernel(
    rows,
    valid,
    partial,
    from_core,
    from_y_first,
    from_y_second,
    stream,
    bias_vector,
    gain_vector,
    shift_vector,
    middle,
    normed,
    powers,
):
    _, _, z, y = coordinates()
    bias, gain, shift = row_of(bias_vector), row_of(gain_vector), row_of(shift_vector)
    total = jnp.zeros((8, middle.shape[1]), F32)
    for at in chunks(middle.shape[0]):
        from_y = joined_rows((from_y_first, from_y_second), at)
        attn = partial[at, :].astype(F32) + from_core[at, :].astype(F32)
        attn = attn + from_y.astype(F32) + bias
        found = stream[at, :].astype(F32) + attn
        middle[at, :] = found
        hat, _ = moment_norm(found)
        normed[at, :] = (hat * gain + shift).astype(BF16)
        total = total + folded(jnp.where(real_rows(at, rows, y), attn * attn, 0.0))
    powers[...] = total * valid[z].astype(F32)


def mlp_kernel(near, far, grad_near, grad_far, *refs):
    own, other = halves_of(refs[:7], refs[0].shape[0])
    bias_of, refs = refs[7:11], refs[11:]
    active, grad_hidden, mid_near, mid_far, out_near, out_far, sums = refs
    x, c, _, _ = coordinates()
    half = near.shape[0]
    quarter = own[0].shape[0] // 2
    w_in = [ref[:quarter, :] for side in (own, other) for ref in side]
    w_out = [ref[quarter:, :] for side in (own, other) for ref in side]
    bias = []
    for side in (x, 1 - x):
        at = pl.multiple_of(4 * DH + (2 * c + side) * quarter, quarter)
        for k in range(4):
            bias.append(bias_of[k][4 * PART :, pl.ds(at, quarter)].astype(F32)[0:1])
    bias = jnp.concatenate(bias, axis=1)
    rows = jnp.concatenate([near[...], far[...]], axis=0)
    grads = jnp.concatenate([grad_near[...], grad_far[...]], axis=0)
    size = 2 * quarter
    for n in range(4):
        at = slice(n * size, (n + 1) * size)
        pair = slice(2 * n, 2 * n + 2)
        u = nt(rows, jnp.concatenate(w_in[pair], axis=0)) + bias[:, at]
        gate = jax.nn.sigmoid(SLOPE * u)
        act = u * gate
        active[:, at] = act.astype(BF16)
        slope = gate + SLOPE * act * (1.0 - gate)
        found = (nt(grads, jnp.concatenate(w_out[pair], axis=0)) * slope).astype(BF16)
        grad_hidden[:, at] = found
        sums[:, at] = jnp.broadcast_to(
            jnp.sum(found.astype(F32), axis=0, keepdims=True), (8, size)
        )
    found = nn(grad_hidden[...], jnp.concatenate(w_in, axis=0)).astype(BF16)
    mid_near[...] = found[:half]
    mid_far[...] = found[half:]
    found = nn(active[...], jnp.concatenate(w_out, axis=0)).astype(BF16)
    out_near[...] = found[:half]
    out_far[...] = found[half:]


def products_kernel(split, left_first, left_second, *refs):
    pieces, outs = refs[:4], refs[4:]
    right = jnp.concatenate([piece[...] for piece in pieces], axis=0)
    hidden = left_first.shape[1] // 2
    quarter = hidden // 4
    for side in (1, 0):
        at = slice(side * hidden, (side + 1) * hidden)
        left = jnp.concatenate([left_first[:, at], left_second[:, at]], axis=0)
        found = tn(left, right).astype(BF16)
        if split:
            for k in range(4):
                outs[k][side * quarter : (side + 1) * quarter, :] = found[
                    k * quarter : (k + 1) * quarter
                ]
        else:
            outs[side][...] = found


def far_sum_kernel(values, received, *outs):
    first = received.shape[0] - values.shape[0]
    done = 0
    for out in outs:
        for at in chunks(out.shape[0]):
            source = slice(done + at.start, done + at.stop)
            moved = slice(first + source.start, first + source.stop)
            found = values[source, :].astype(F32) + received[moved, :].astype(F32)
            out[at, :] = found.astype(BF16)
        done += out.shape[0]


def add_split_kernel(keep, received, *outs):
    at = 0
    for out in outs:
        size = out.shape[0]
        out[...] = (
            keep[at : at + size, :].astype(F32) + received[at : at + size, :].astype(F32)
        ).astype(BF16)
        at += size


def output_kernel(
    rows,
    valid,
    partial,
    from_core,
    from_y,
    middle,
    stream,
    bias_vector,
    attn_power,
    sums,
    output,
    heads,
    small,
):
    _, _, z, y = coordinates()
    bias = row_of(bias_vector)
    width = middle.shape[1]
    totals = [jnp.zeros((8, width), F32) for _ in range(3)]
    for at in chunks(middle.shape[0]):
        branch = partial[at, :].astype(F32) + from_core[at, :].astype(F32)
        branch = branch + from_y[at, :].astype(F32) + bias
        found = middle[at, :] + branch
        output[at, :] = found
        entry = stream[at, :].astype(F32)
        real = real_rows(at, rows, y)
        for i, v in enumerate((entry, branch, found)):
            totals[i] = totals[i] + folded(jnp.where(real, v * v, 0.0))
    heads[...] = output[0:8, :]
    flag = valid[z]
    lane = lax.broadcasted_iota(jnp.int32, (1, width), 1)
    entry = jnp.where(lane == 4, (flag * (rows - y)).astype(F32), 0.0)
    powers = [totals[0] * flag.astype(F32), attn_power[...]]
    powers += [total * flag.astype(F32) for total in totals[1:]]
    for i, power in enumerate(powers):
        whole = jnp.sum(jnp.sum(power, axis=0, keepdims=True), axis=1, keepdims=True)
        entry = entry + jnp.where(lane == i, whole, 0.0)
    row = lax.broadcasted_iota(jnp.int32, (8, 1), 0)
    small[...] = jnp.where(row == 6, entry, sums[...])


def norm_back(grad, hat, inverse, gain):
    scaled = grad * gain
    plain = jnp.mean(scaled, axis=1, keepdims=True)
    cross = jnp.mean(scaled * hat, axis=1, keepdims=True)
    return inverse * (scaled - plain - hat * cross)


def middle_back_kernel(
    partial, from_core, from_y, middle, branch, gain_vector, grad, low, sums
):
    width = middle.shape[1]
    gain = row_of(gain_vector)
    totals = [jnp.zeros((8, width), F32) for _ in range(4)]
    for at in chunks(middle.shape[0]):
        found = partial[at, :].astype(F32) + from_core[at, :].astype(F32)
        found = found + from_y[at, :].astype(F32)
        hat, inverse = moment_norm(middle[at, :])
        gy = branch[at, :].astype(F32)
        total = gy + norm_back(found, hat, inverse, gain)
        grad[at, :] = total
        rounded = total.astype(BF16)
        low[at, :] = rounded
        for i, v in enumerate((rounded.astype(F32), gy, found * hat, found)):
            totals[i] = totals[i] + folded(v)
    sums[...] = jnp.concatenate(
        [jnp.sum(v, axis=0, keepdims=True) for v in totals] + [jnp.zeros((4, width), F32)], axis=0
    )


def backward_kernel(pair, *refs):
    grads, normed, refs = refs[:4], refs[4:8], refs[8:]
    w_out, qkv_own, qkv_other, probs_own, probs_other = refs[:5]
    mixed_own, mixed_other, sums_chip, sums_distant = refs[5:9]
    out_own, out_other, give, keep = refs[9:]
    half = grads[0].shape[0]
    rows = 2 * half
    lanes = 2 * DH
    scale = jnp.asarray(DH ** (-0.5), BF16)
    grad_rows = jnp.concatenate([ref[...] for ref in grads], axis=0)
    wide = nt(grad_rows, w_out[...]).astype(BF16)
    hidden_sums = sums_chip[0:1, :] + sums_distant[0:1, :]
    totals = []
    images = ((qkv_own, probs_own, out_own), (qkv_other, probs_other, out_other))
    for image, (qkv, probs, out) in enumerate(images):
        dq, dk, dv = [], [], []
        for h in range(2):
            at = h * DH
            q = qkv[:, at : at + DH] * scale
            k = qkv[:, lanes + at : lanes + at + DH] * scale
            v = qkv[:, 2 * lanes + at : 2 * lanes + at + DH]
            g = wide[image * rows : (image + 1) * rows, h * DH : (h + 1) * DH]
            found = probs[h]
            grad_probs = nt(v, g)
            scores = found.astype(F32)
            product = scores * grad_probs
            inner = jnp.sum(product, axis=0, keepdims=True)
            grad_scores = (product - scores * inner).astype(BF16)
            dv.append(nn(found, g))
            dk.append(nn(grad_scores, q))
            dq.append(tn(k, grad_scores))
        query = jnp.concatenate(dq, axis=0).T.astype(BF16)
        value = jnp.concatenate(dv, axis=1).astype(BF16)
        out[:, :lanes] = query
        out[:, lanes : 2 * lanes] = jnp.concatenate(dk, axis=1).astype(BF16)
        out[:, 2 * lanes :] = value
        totals.append(
            [jnp.sum(v.astype(F32), axis=0, keepdims=True) for v in (query, value)]
        )
    query_sum, value_sum = (totals[0][i] + totals[1][i] for i in range(2))
    stacked = jnp.concatenate([out_own[...], out_other[...]], axis=0)
    grad_w = tn(stacked, jnp.concatenate([ref[...] for ref in normed], axis=0)).astype(BF16)
    mixed = jnp.concatenate([mixed_own[...], mixed_other[...]], axis=0)
    grad_o = tn(mixed, grad_rows).astype(BF16)
    size = 4 * PART + 16
    quarter = hidden_sums.shape[1] // 8
    width = give.shape[1]
    for side, out in enumerate((keep, give)):
        for i in range(2):
            for m in range(4):
                source = grad_o if m == 3 else grad_w
                at = (0 if m == 3 else m * lanes) + i * DH + side * PART
                out[i * size + m * PART : i * size + (m + 1) * PART, :] = source[at : at + PART]
            at = i * DH + side * PART
            block = (side * 4 + 2 * pair + i) * quarter
            row = jnp.concatenate(
                [
                    query_sum[:, at : at + PART],
                    value_sum[:, at : at + PART],
                    jnp.zeros((1, DH), F32),
                    hidden_sums[:, block : block + quarter],
                    jnp.zeros((1, width - lanes - quarter), F32),
                ],
                axis=1,
            )
            out[i * size + 4 * PART : (i + 1) * size, :] = jnp.broadcast_to(row, (16, width)).astype(
                BF16
            )


def entry_product_kernel(first_pair, second_pair, first_weights, second_weights, *outs):
    joined = jnp.concatenate([first_pair[...], second_pair[...]], axis=1)
    weights = jnp.concatenate([first_weights[...], second_weights[...]], axis=0)
    found = nn(joined, weights).astype(BF16)
    at = 0
    for out in outs:
        out[...] = found[at : at + out.shape[0]]
        at += out.shape[0]


def entry_back_kernel(
    rows,
    valid,
    partial,
    from_core,
    from_y,
    stream,
    grad_middle,
    gain_vector,
    middle_sums,
    grad,
    heads,
    small,
):
    width = stream.shape[1]
    gain = row_of(gain_vector)
    totals = [jnp.zeros((8, width), F32) for _ in range(2)]
    for at in chunks(stream.shape[0]):
        found = partial[at, :].astype(F32) + from_core[at, :].astype(F32)
        found = found + from_y[at, :].astype(F32)
        hat, inverse = moment_norm(stream[at, :].astype(F32))
        grad[at, :] = grad_middle[at, :] + norm_back(found, hat, inverse, gain)
        for i, v in enumerate((found * hat, found)):
            totals[i] = totals[i] + folded(v)
    heads[...] = grad[0:8, :]
    small[...] = jnp.concatenate(
        [middle_sums[0:2, :]]
        + [jnp.sum(v, axis=0, keepdims=True) for v in totals]
        + [middle_sums[2:4, :], middle_sums[6:8, :]],
        axis=0,
    )


def exit_kernel(values, after, out, ext):
    _, _, z, y = coordinates()
    half = values.shape[0]
    rows = out.shape[0]
    count = rows - y
    index = lax.broadcasted_iota(jnp.int32, (half, 1), 0)
    ext[8:, :] = jnp.zeros((half - 8, ext.shape[1]), F32)
    ext[0:8, :] = after[...]
    moved = pltpu.roll(values[...], half - z, 0)
    beyond = pltpu.roll(ext[...], count - z, 0)
    out[...] = jnp.where(index < count - z, moved, beyond)[:rows]


def attention_gradients_kernel(own, across, core, core_across, *outs):
    x, c, _, _ = coordinates()
    query, value, hidden = outs[4:]
    pieces = ((own, c, x), (across, c, 1 - x), (core, 1 - c, x), (core_across, 1 - c, 1 - x))
    for ref, c_of, x_of in pieces:
        at = pl.multiple_of(c_of * DH + x_of * PART, PART)
        for m in range(4):
            outs[m][pl.ds(at, PART), :] = ref[m * PART : (m + 1) * PART, :].astype(F32)
    rows = [ref[4 * PART :, :].astype(F32)[0:1] for ref, _, _ in pieces]
    natural = []
    for c_of in range(2):
        for x_of in range(2):
            same = jnp.where(x == x_of, rows[0], rows[1])
            changed = jnp.where(x == x_of, rows[2], rows[3])
            natural.append(jnp.where(c == c_of, same, changed))
    quarter = hidden.shape[0] // 4
    for out, at, size in ((query, 0, PART), (value, PART, PART), (hidden, 2 * DH, quarter)):
        found = jnp.concatenate([row[:, at : at + size] for row in natural], axis=1)
        out[...] = found.reshape(out.shape)


def mlp_in_gradient_kernel(own, across, core, core_across, out):
    x, c, _, _ = coordinates()
    pieces = ((own, c, x), (across, c, 1 - x), (core, 1 - c, x), (core_across, 1 - c, 1 - x))
    for ref, c_of, x_of in pieces:
        quarter = ref.shape[0]
        at = pl.multiple_of((2 * c_of + x_of) * quarter, quarter)
        out[:, pl.ds(at, quarter)] = ref[...].astype(F32).T


def swapped_sum_kernel(own, received, out):
    size = own.shape[0] // 2
    out[:size, :] = (own[:size, :].astype(F32) + received[size:, :].astype(F32)).astype(BF16)
    out[size:, :] = (own[size:, :].astype(F32) + received[:size, :].astype(F32)).astype(BF16)


def mlp_out_gradient_kernel(own, core, out):
    x, c, _, _ = coordinates()
    for ref, c_of in ((own, c), (core, 1 - c)):
        quarter = ref.shape[0] // 2
        for i, side in enumerate((x, 1 - x)):
            at = pl.multiple_of((2 * c_of + side) * quarter, quarter)
            out[pl.ds(at, quarter), :] = ref[i * quarter : (i + 1) * quarter, :].astype(F32)


def sums_kernel(small, received, *outs):
    found = small[...] + received[...]
    for i, out in enumerate(outs[:-1]):
        out[...] = found[i : i + 1].reshape(out.shape)
    outs[-1][...] = found[6:7, : outs[-1].shape[0]].reshape(outs[-1].shape)


def copy_kernel(source, target):
    target[...] = source[...]


def add_wide_kernel(first, second, out):
    out[...] = first[...] + second[...]


def add_split_last_kernel(keep, received, last, zero, one):
    size = zero.shape[0]
    zero[...] = (keep[:size, :].astype(F32) + received[:size, :].astype(F32)).astype(BF16)
    found = keep[size:, :].astype(F32) + received[size:, :].astype(F32)
    one[...] = (found + last[...].astype(F32)).astype(BF16)


def add_three_kernel(first, second, third, out):
    out[...] = (
        first[...].astype(F32) + second[...].astype(F32) + third[...].astype(F32)
    ).astype(BF16)


def on_device(
    inputs,
    valid,
    cotangent,
    w_query,
    w_key,
    w_value,
    b_query,
    b_value,
    w_attn_out,
    b_attn_out,
    w_mlp_in,
    b_mlp_in,
    w_mlp_out,
    b_mlp_out,
    attention_norm_gain,
    attention_norm_shift,
    feedforward_norm_gain,
    feedforward_norm_shift,
):
    rows, width = inputs.shape
    images = valid.shape[0]
    heads_local = w_query.shape[0] // DH
    hidden_local = w_mlp_out.shape[0]
    shape = (lax.axis_size("tok"), lax.axis_size("feat"), images, heads_local, hidden_local, width)
    if shape != (4, 8, 4, 2, 512, 1024) or 2 * rows != SEQ + 1:
        return on_device_general(
            inputs,
            valid,
            cotangent,
            w_query,
            w_key,
            w_value,
            b_query,
            b_value,
            w_attn_out,
            b_attn_out,
            w_mlp_in,
            b_mlp_in,
            w_mlp_out,
            b_mlp_out,
            attention_norm_gain,
            attention_norm_shift,
            feedforward_norm_gain,
            feedforward_norm_shift,
        )
    half = (rows + 15) // 16 * 16
    image = 2 * half
    quarter = hidden_local // 4
    piece = 4 * PART + 16
    row_block = (half, width)
    low_rows, wide_rows = (row_block, BF16), (row_block, F32)
    last, usual = (), 0.01
    calls, sent = [], []

    def send(values, pairs):
        found = lax.ppermute(values, AXES, pairs)
        sent.append(found)
        return found


    def call(body, operands, outs, scratch=(), gate=(), specs=None, span=None, final=False):
        nonlocal last
        specs = [VMEM] * len(operands) if specs is None else specs
        number = len(calls)
        calls.append(number)
        span = SPANS.get(number, usual if span is None else span)
        gate = [g for i, g in enumerate(gate) if i not in LATE.get(number, ())]
        gate += [sent[i] for i in EARLY.get(number, ()) if i < len(sent)]
        found = kernel_call(body, operands, specs, outs, scratch, last + tuple(gate), span)
        if not final:
            last = (min(found, key=lambda v: v.size * v.dtype.itemsize),)
        return found

    def pin(values, gate=()):
        return call(copy_kernel, (values,), [(values.shape, values.dtype)], gate=gate)[0]

    def far_sum(values, received, gate=(), sizes=(half,)):
        outs = [((size, width), BF16) for size in sizes]
        found = call(far_sum_kernel, (values, received), outs, gate=gate)
        return found if len(sizes) > 1 else found[0]

    def split(values, received, sizes, gate=()):
        outs = [((size, width), BF16) for size in sizes]
        return call(add_split_kernel, (values, received), outs, gate=gate)

    def add_last(values, one, three, gate=()):
        return call(add_three_kernel, (values, one, three), [(values.shape, BF16)], gate=gate)[0]

    in_hbm = [
        pltpu.with_memory_space_constraint(w, pltpu.HBM)
        for w in (w_query, w_key, w_value, w_attn_out, b_query, b_value, b_mlp_in)
    ]
    attn_own, attn_other, attn_both = call(
        attention_weights_kernel,
        in_hbm,
        [((piece, width), BF16)] * 2 + [((2 * piece, width), BF16)],
        scratch=[
            pltpu.VMEM((2 * DH,), BF16),
            pltpu.VMEM((2 * DH,), BF16),
            pltpu.VMEM((hidden_local,), BF16),
            pltpu.SemaphoreType.DMA((19,)),
        ],
        specs=[HBM] * 7,
    )
    own_one = send(attn_own, UP_Z)
    attn_three = send(attn_both, DOWN_Z)
    (edge,) = call(edge_kernel, (inputs, cotangent), [((16, width), BF16)])
    edge = send(edge, NEXT)
    mlp_own, mlp_other, mlp_both = call(
        mlp_weights_kernel,
        (w_mlp_in, w_mlp_out),
        [((2 * quarter, width), BF16)] * 2 + [((4 * quarter, width), BF16)],
    )
    stream, normed, branch_grad, branch_again = call(
        entry_kernel,
        (valid, inputs, cotangent, edge, attention_norm_gain, attention_norm_shift),
        [low_rows] * 4,
        scratch=[pltpu.VMEM((half + 8, width), F32)],
        gate=(own_one,),
        specs=[SMEM] + [VMEM] * 5, span=30)
    own_two = send(own_one, UP_Z)
    other_one = send(own_one, SWAP_X)
    normed_y, normed_c = send(normed, SWAP_Y), send(normed, SWAP_C)
    pin(edge, (own_two, other_one))
    other_two = send(own_two, SWAP_X)
    branch_again = pin(branch_again, (normed_y,))
    normed_yc = send(normed_y, SWAP_C)
    branch_y, branch_c = send(branch_again, SWAP_Y), send(branch_again, SWAP_C)

    lanes = 2 * DH
    pair_out = [((image, 3 * lanes), BF16)], [((2, image, image), BF16)], [((image, lanes), BF16)]
    weight_out = [((3 * lanes, width), BF16), ((lanes, width), BF16)]
    first_pair = call(
        functools.partial(first_pair_kernel, rows),
        (normed, normed_y, normed_c, normed_yc, attn_own, attn_other, own_one, other_one),
        pair_out[0] * 2 + pair_out[1] * 2 + pair_out[2] * 2 + weight_out,
        span=30,
    )
    w_first, out_first = first_pair[6:]
    mlp_first = pin(mlp_own, (attn_three, normed_c))
    mlp_one = send(mlp_first, UP_Z)
    qkv_other, probs_other, mixed_other, partial_other, w_second, out_second, second_bias = call(
        functools.partial(second_pair_other_kernel, rows),
        (normed_c, normed_yc, attn_three, own_two, other_two, first_pair[5], out_first),
        pair_out[0]
        + pair_out[1]
        + pair_out[2]
        + [((image, width), BF16)]
        + weight_out
        + [((8, 3 * lanes), F32)],
        gate=(branch_c,),
        span=30,
    )
    from_core = send(partial_other, SWAP_C)
    qkv_own, probs_own, mixed_own, partial_near, partial_far = call(
        functools.partial(second_pair_own_kernel, rows),
        (normed, normed_y, w_second, out_second, second_bias, first_pair[4], out_first),
        pair_out[0] + pair_out[1] + pair_out[2] + [low_rows] * 2,
        span=30,
    )
    saved = (
        (out_first,) + tuple(first_pair[:6]),
        (out_second, qkv_own, qkv_other, probs_own, probs_other, mixed_own, mixed_other),
    )
    parts_of_half = (half // 2 + 8, half - half // 2 - 8)
    attn_far = far_sum(partial_far, from_core, (branch_y,), parts_of_half)
    from_y = tuple(send(part, SWAP_Y) for part in attn_far)
    mlp_one = pin(mlp_one)
    mlp_two = send(mlp_one, UP_Z)
    mlp_other_one = send(mlp_one, SWAP_X)
    mlp_three = send(pin(mlp_both), DOWN_Z)
    branch_yc = send(branch_y, SWAP_C)
    middle, normed_middle, attn_power = call(
        functools.partial(middle_kernel, rows),
        (valid, partial_near, from_core) + from_y + (stream,)
        + (b_attn_out, feedforward_norm_gain, feedforward_norm_shift),
        [wide_rows, low_rows, ((8, width), F32)],
        gate=(mlp_other_one, branch_yc),
        specs=[SMEM] + [VMEM] * 8, span=30)
    middle_y, middle_c = send(normed_middle, SWAP_Y), send(normed_middle, SWAP_C)
    pin(attn_power, (mlp_two, middle_c))
    mlp_other_two = send(mlp_two, SWAP_X)

    usual = 10
    middle_yc = send(middle_y, SWAP_C)
    pieces = (mlp_own, mlp_other, mlp_one, mlp_other_one, mlp_three, mlp_two, mlp_other_two)
    pieces += (attn_own, own_one, attn_three, own_two)
    mlp_out = (
        [((image, 8 * quarter), BF16)] * 2 + [low_rows] * 4 + [((8, 8 * quarter), F32)]
    )
    chip = call(
        mlp_kernel,
        (normed_middle, middle_c, branch_grad, branch_c) + pieces,
        mlp_out,
        gate=(middle_y,),
    )
    mid_core, out_core = send(chip[3], SWAP_C), send(chip[5], SWAP_C)
    distant = call(mlp_kernel, (middle_y, middle_yc, branch_y, branch_yc) + pieces, mlp_out)
    out_distant = send(distant[5], SWAP_C)
    mid_far = far_sum(distant[2], send(distant[3], SWAP_C), (mid_core, out_core))
    mid_y = send(mid_far, SWAP_Y)

    grad_out = call(
        functools.partial(products_kernel, True),
        (chip[0], distant[0], branch_grad, branch_c, branch_y, branch_yc),
        [((2 * quarter, width), BF16)] * 4,
        gate=(out_distant,),
    )
    grad_out = dict(zip(SLOTS, grad_out))
    out_two = send(grad_out[2], DOWN_Z)
    out_three = send(grad_out[3], UP_Z)
    grad_in_keep, grad_in_give = call(
        functools.partial(products_kernel, False),
        (chip[1], distant[1], normed_middle, middle_c, middle_y, middle_yc),
        [((4 * quarter, width), BF16)] * 2,
    )
    in_received = send(grad_in_give, SWAP_X)
    grad_middle, grad_attn, middle_sums = call(
        middle_back_kernel,
        (chip[2], mid_core, mid_y, middle, branch_grad, feedforward_norm_gain),
        [wide_rows, low_rows, ((8, width), F32)],
    )
    grad_y, grad_c = send(grad_attn, SWAP_Y), send(grad_attn, SWAP_C)
    out_far = far_sum(distant[4], out_distant)
    (one,) = split(grad_out[1], out_two, (2 * quarter,), (grad_c,))
    out_one = send(one, DOWN_Z)
    grad_yc = send(grad_y, SWAP_C)

    def backward(p, gate=()):
        return call(
            functools.partial(backward_kernel, p),
            (grad_attn, grad_y, grad_c, grad_yc, normed, normed_y, normed_c, normed_yc)
            + saved[p]
            + (chip[6], distant[6]),
            [((image, 6 * DH), BF16)] * 2 + [((2 * piece, width), BF16)] * 2,
            gate=gate,
        )

    second_own, second_other, give, keep = backward(1)
    received = send(give, SWAP_X)
    out_y = send(pin(out_far), SWAP_Y)
    first_own, first_other, give_first, keep_first = backward(0, (out_one, out_three))
    received_first = send(give_first, SWAP_X)
    in_pieces = split(grad_in_keep, in_received, (quarter,) * 4)
    in_pieces = dict(zip(SLOTS, in_pieces))
    in_two = send(in_pieces[2], DOWN_Z)
    in_three = send(in_pieces[3], UP_Z)
    (entry_other,) = call(
        entry_product_kernel, (first_other, second_other, w_first, w_second), [((image, width), BF16)]
    )
    entry_core = send(entry_other, SWAP_C)
    entry_near, entry_far = call(
        entry_product_kernel, (first_own, second_own, w_first, w_second), [low_rows] * 2
    )
    entry_far = far_sum(entry_far, entry_core)
    entry_y = send(entry_far, SWAP_Y)
    three, two = split(keep, received, (piece,) * 2, (in_three,))
    attn_two = send(two, DOWN_Z)
    attn_three = send(three, UP_Z)
    (one,) = split(in_pieces[1], in_two, (quarter,))
    in_one = send(one, DOWN_Z)
    output, output_heads, power_sums = call(
        functools.partial(output_kernel, rows),
        (valid, chip[4], out_core, out_y, middle, stream, b_mlp_out, attn_power, middle_sums),
        [wide_rows, ((8, width), F32), ((8, width), F32)],
        specs=[SMEM] + [VMEM] * 8,
    )
    output_after = send(output_heads, PREVIOUS)
    out_total = call(
        add_three_kernel,
        (grad_out[0], out_one, out_three),
        [((2 * quarter, width), BF16)],
        gate=(received_first,),
    )[0]
    out_across = send(out_total, SWAP_X)
    zero, one = call(
        add_split_last_kernel,
        (keep_first, received_first, attn_two),
        [((piece, width), BF16)] * 2,
    )
    attn_one = send(one, DOWN_Z)
    gradient, heads, small = call(
        functools.partial(entry_back_kernel, rows),
        (valid, entry_near, entry_core, entry_y, stream, grad_middle)
        + (attention_norm_gain, power_sums),
        [wide_rows, ((8, width), F32), ((8, width), F32)],
        gate=(attn_three,),
        specs=[SMEM] + [VMEM] * 7,
    )

    def add_small(received, gate=()):
        return call(add_wide_kernel, (small, received), [(small.shape, F32)], gate=gate)[0]

    def rows_out(values, after):
        return call(
            exit_kernel,
            (values, after),
            [((rows, width), F32)],
            scratch=[pltpu.VMEM((half, width), F32)],
            final=True,
        )[0]

    small = add_small(send(small, SWAP_C))
    small_y = send(small, SWAP_Y)
    heads_after = send(heads, PREVIOUS)
    attn_total = add_last(zero, attn_one, attn_three, (out_across,))
    attn_across, attn_core = send(attn_total, SWAP_X), send(attn_total, SWAP_C)
    (out_whole,) = call(
        swapped_sum_kernel,
        (out_total, out_across),
        [((2 * quarter, width), BF16)],
    )
    out_core = send(out_whole, SWAP_C)
    small = add_small(small_y, (attn_core,))
    small_z = send(small, FLIP_Z[1])
    output_rows = rows_out(output, output_after)
    gradient_rows = rows_out(gradient, heads_after)
    in_total = add_last(in_pieces[0], in_one, in_three, (out_core,))
    in_across, in_core = send(in_total, SWAP_X), send(in_total, SWAP_C)
    small = add_small(small_z)
    small_z = send(small, FLIP_Z[2])
    (grad_w_mlp_out,) = call(
        mlp_out_gradient_kernel,
        (out_whole, out_core),
        [((hidden_local, width), F32)],
        final=True,
    )
    attn_last = send(attn_across, SWAP_C)
    small = add_small(small_z, (in_core,))
    small_x = send(small, SWAP_X)
    attn_grads = call(
        attention_gradients_kernel,
        (attn_total, attn_across, attn_core, attn_last),
        [((2 * DH, width), F32)] * 4
        + [((2 * DH,), F32), ((2 * DH,), F32), ((hidden_local,), F32)],
        final=True,
    )
    in_last = send(in_across, SWAP_C)
    (grad_w_mlp_in,) = call(
        mlp_in_gradient_kernel,
        (in_total, in_across, in_core, in_last),
        [((width, hidden_local), F32)],
        final=True,
    )
    *vectors, powers = call(
        sums_kernel,
        (small, small_x),
        [((width,), F32)] * 6 + [((2 * DH,), F32)],
        final=True,
    )
    stream_rms = jnp.sqrt(powers[:4] / (jnp.maximum(powers[4], 1.0) * D))
    return (
        output_rows,
        gradient_rows,
        attn_grads[0],
        attn_grads[1],
        attn_grads[2],
        attn_grads[4],
        attn_grads[5],
        attn_grads[3],
        vectors[0],
        grad_w_mlp_in,
        attn_grads[6],
        grad_w_mlp_out,
        vectors[1],
        vectors[2],
        vectors[3],
        vectors[4],
        vectors[5],
        stream_rms,
    )


def solution(mesh):
    in_specs = (
        P(("tok", "feat"), None),
        P("tok"),
        P(("tok", "feat"), None),
        P("feat", None),
        P("feat", None),
        P("feat", None),
        P("feat"),
        P("feat"),
        P("feat", None),
        P(),
        P(None, "feat"),
        P("feat"),
        P("feat", None),
        P(),
        P(),
        P(),
        P(),
        P(),
    )
    out_specs = (
        P(("tok", "feat"), None),
        P(("tok", "feat"), None),
        P("feat", None),
        P("feat", None),
        P("feat", None),
        P("feat"),
        P("feat"),
        P("feat", None),
        P(),
        P(None, "feat"),
        P("feat"),
        P("feat", None),
        P(),
        P(),
        P(),
        P(),
        P(),
        P(),
    )
    return jax.shard_map(
        on_device, mesh=mesh, in_specs=in_specs, out_specs=out_specs, check_vma=False
    )
```

```python
import functools

import jax
import jax.numpy as jnp
from jax import lax
from jax.experimental import pallas as pl
from jax.experimental.pallas import tpu as pltpu
from jax.sharding import PartitionSpec as P

D = 1024
DH = 64
SEQ = 577


EPSILON = 1e-05
SLOPE = 1.702


def gelu_slope(values):
    sigmoid = jax.nn.sigmoid(SLOPE * values)
    return sigmoid + SLOPE * values * sigmoid * (1.0 - sigmoid)


def column_sums(values):
    return jnp.sum(values.astype(jnp.float32), axis=0)


def split_heads(values):
    return values.reshape(values.shape[0], values.shape[1] // DH, DH)


def apply_layer_norm(values):
    center = jnp.mean(values, axis=1, keepdims=True)
    spread = jnp.mean(values * values, axis=1, keepdims=True) - center * center
    inverse_deviation = lax.rsqrt(spread + EPSILON)
    return ((values - center) * inverse_deviation, inverse_deviation)


def layer_norm_backward(normalized_gradient, centered_scaled, inverse_deviation, norm_gain):
    scaled_output = normalized_gradient * norm_gain.astype(jnp.float32)
    plain_output = jnp.mean(scaled_output, axis=1, keepdims=True)
    cross_term = jnp.mean(scaled_output * centered_scaled, axis=1, keepdims=True)
    return inverse_deviation * (scaled_output - plain_output - centered_scaled * cross_term)


def image_forward(blocks):
    query_img, key_img, value_img = blocks
    scale = DH ** (-0.5)
    query_heads = split_heads(query_img)
    key_heads = split_heads(key_img)
    value_heads = split_heads(value_img)
    scores = (
        jnp.einsum("qhd,khd->hqk", query_heads, key_heads, preferred_element_type=jnp.float32)
        * scale
    )
    top_score = jnp.max(scores, axis=-1, keepdims=True)
    weights = jnp.exp(scores - top_score)
    total = jnp.sum(weights, axis=-1, keepdims=True)
    probs = (weights / total).astype(jnp.bfloat16)
    mixed = jnp.einsum("hqk,khd->qhd", probs, value_heads, preferred_element_type=jnp.float32)
    log_total = top_score[..., 0] + jnp.log(total[..., 0])
    return (mixed.reshape(query_img.shape).astype(jnp.bfloat16), log_total)


def image_backward(blocks):
    query_img, key_img, value_img, grad_img, log_total = blocks
    scale = DH ** (-0.5)
    query_heads = split_heads(query_img)
    key_heads = split_heads(key_img)
    value_heads = split_heads(value_img)
    grad_heads = split_heads(grad_img)
    scores = (
        jnp.einsum("qhd,khd->hqk", query_heads, key_heads, preferred_element_type=jnp.float32)
        * scale
    )
    probs = jnp.exp(scores - log_total[..., None])
    probs_low = probs.astype(jnp.bfloat16)
    grad_probs = jnp.einsum(
        "qhd,khd->hqk", grad_heads, value_heads, preferred_element_type=jnp.float32
    )
    grad_value = jnp.einsum(
        "hqk,qhd->khd", probs_low, grad_heads, preferred_element_type=jnp.float32
    )
    inner = jnp.sum(probs * grad_probs, axis=-1, keepdims=True)
    grad_scores = (probs * (grad_probs - inner)).astype(jnp.bfloat16)
    grad_query = (
        jnp.einsum("hqk,khd->qhd", grad_scores, key_heads, preferred_element_type=jnp.float32)
        * scale
    )
    grad_key = (
        jnp.einsum("hqk,qhd->khd", grad_scores, query_heads, preferred_element_type=jnp.float32)
        * scale
    )
    shape_img = query_img.shape
    return (
        grad_query.reshape(shape_img).astype(jnp.bfloat16),
        grad_key.reshape(shape_img).astype(jnp.bfloat16),
        grad_value.reshape(shape_img).astype(jnp.bfloat16),
    )


def by_image(values, images):
    return values.reshape(images, values.shape[0] // images, values.shape[1])


def on_device_general(
    inputs,
    valid,
    cotangent,
    w_query,
    w_key,
    w_value,
    b_query,
    b_value,
    w_attn_out,
    b_attn_out,
    w_mlp_in,
    b_mlp_in,
    w_mlp_out,
    b_mlp_out,
    attention_norm_gain,
    attention_norm_shift,
    feedforward_norm_gain,
    feedforward_norm_shift,
):
    row_count, width = inputs.shape
    images = valid.shape[0]
    group_rows = images * SEQ
    parts = lax.axis_size("feat")
    extra = row_count * parts - group_rows
    width_local = w_query.shape[0]
    hidden_local = w_mlp_out.shape[0]
    global_rows = lax.axis_index("feat") * row_count + jnp.arange(row_count, dtype=jnp.int32)
    owner = global_rows // SEQ
    matches = (owner[:, None] == jnp.arange(images, dtype=jnp.int32)[None, :]).astype(jnp.float32)
    row_mask = jnp.sum(matches * valid.astype(jnp.float32)[None, :], axis=1)
    live = (global_rows < group_rows).astype(jnp.float32)[:, None]

    def padded(values):
        return jnp.pad(values, ((0, extra), (0, 0)))

    local_input_rows = inputs.astype(jnp.float32)
    first_centered_scaled, first_inverse_deviation = apply_layer_norm(local_input_rows)
    normalized_first = (
        first_centered_scaled * attention_norm_gain.astype(jnp.float32)
        + attention_norm_shift.astype(jnp.float32)
    ).astype(jnp.bfloat16)
    normed_full = lax.all_gather(normalized_first, "feat", axis=0, tiled=True)[:group_rows]
    w_qkv = jnp.concatenate([w_query, w_key, w_value], axis=0)
    projected = jnp.einsum("rd,cd->rc", normed_full, w_qkv, preferred_element_type=jnp.float32)
    queries = (projected[:, :width_local] + b_query.astype(jnp.float32)).astype(jnp.bfloat16)
    key_rows = projected[:, width_local : 2 * width_local].astype(jnp.bfloat16)
    value_rows = (projected[:, 2 * width_local :] + b_value.astype(jnp.float32)).astype(
        jnp.bfloat16
    )
    mixed, log_totals = lax.map(
        image_forward,
        (by_image(queries, images), by_image(key_rows, images), by_image(value_rows, images)),
    )
    mixed = mixed.reshape(group_rows, width_local)
    partial_out = jnp.dot(mixed, w_attn_out, preferred_element_type=jnp.float32)
    attn = lax.psum_scatter(
        padded(partial_out), "feat", scatter_dimension=0, tiled=True
    ) + b_attn_out.astype(jnp.float32)
    middle_state = local_input_rows + attn
    second_centered_scaled, second_inverse_deviation = apply_layer_norm(middle_state)
    normalized_middle = (
        second_centered_scaled * feedforward_norm_gain.astype(jnp.float32)
        + feedforward_norm_shift.astype(jnp.float32)
    ).astype(jnp.bfloat16)
    mid_full = lax.all_gather(normalized_middle, "feat", axis=0, tiled=True)[:group_rows]
    hidden = jnp.dot(mid_full, w_mlp_in, preferred_element_type=jnp.float32) + b_mlp_in.astype(
        jnp.float32
    )
    active = (hidden * jax.nn.sigmoid(SLOPE * hidden)).astype(jnp.bfloat16)
    partial_mlp = jnp.dot(active, w_mlp_out, preferred_element_type=jnp.float32)
    branch = lax.psum_scatter(
        padded(partial_mlp).astype(jnp.bfloat16), "feat", scatter_dimension=0, tiled=True
    ).astype(jnp.float32) + b_mlp_out.astype(jnp.float32)
    output = (middle_state + branch) * live
    output_gradient = cotangent.astype(jnp.float32) * row_mask[:, None]
    grad_branch = output_gradient.astype(jnp.bfloat16)
    grad_b_mlp_out = column_sums(grad_branch)
    branch_full = lax.all_gather(grad_branch, "feat", axis=0, tiled=True)[:group_rows]
    grad_w_mlp_out = jnp.einsum(
        "rf,rd->fd", active, branch_full, preferred_element_type=jnp.float32
    )
    grad_active = jnp.einsum(
        "rd,fd->rf", branch_full, w_mlp_out, preferred_element_type=jnp.float32
    )
    grad_hidden = (grad_active * gelu_slope(hidden)).astype(jnp.bfloat16)
    grad_b_mlp_in = column_sums(grad_hidden)
    grad_mlp_in_rows = jnp.einsum(
        "rf,rd->fd", grad_hidden, mid_full, preferred_element_type=jnp.float32
    )
    partial_mid = jnp.einsum("rf,df->rd", grad_hidden, w_mlp_in, preferred_element_type=jnp.float32)
    midpoint_gradient = lax.psum_scatter(
        padded(partial_mid), "feat", scatter_dimension=0, tiled=True
    )
    feedforward_gain_gradient = jnp.sum(midpoint_gradient * second_centered_scaled, axis=0)
    grad_s_mlp = jnp.sum(midpoint_gradient, axis=0)
    middle_state_gradient = output_gradient + layer_norm_backward(
        midpoint_gradient, second_centered_scaled, second_inverse_deviation, feedforward_norm_gain
    )
    grad_attn = middle_state_gradient.astype(jnp.bfloat16)
    grad_b_attn_out = column_sums(grad_attn)
    attn_full = lax.all_gather(grad_attn, "feat", axis=0, tiled=True)[:group_rows]
    grad_w_attn_out = jnp.einsum("rh,rd->hd", mixed, attn_full, preferred_element_type=jnp.float32)
    grad_mixed = jnp.einsum(
        "rd,hd->rh", attn_full, w_attn_out, preferred_element_type=jnp.float32
    ).astype(jnp.bfloat16)
    grad_query, grad_key, grad_value = lax.map(
        image_backward,
        (
            by_image(queries, images),
            by_image(key_rows, images),
            by_image(value_rows, images),
            by_image(grad_mixed, images),
            log_totals,
        ),
    )
    grad_query = grad_query.reshape(group_rows, width_local)
    grad_key = grad_key.reshape(group_rows, width_local)
    grad_value = grad_value.reshape(group_rows, width_local)
    grad_b_query = column_sums(grad_query)
    grad_b_value = column_sums(grad_value)
    grad_qkv = jnp.concatenate([grad_query, grad_key, grad_value], axis=1)
    grad_w_qkv = jnp.einsum("rc,rd->cd", grad_qkv, normed_full, preferred_element_type=jnp.float32)
    partial_in = jnp.einsum("rc,cd->rd", grad_qkv, w_qkv, preferred_element_type=jnp.float32)
    normalized_gradient = lax.psum_scatter(
        padded(partial_in).astype(jnp.bfloat16), "feat", scatter_dimension=0, tiled=True
    ).astype(jnp.float32)
    attention_gain_gradient = jnp.sum(normalized_gradient * first_centered_scaled, axis=0)
    grad_s_attn = jnp.sum(normalized_gradient, axis=0)
    layer_input_gradient = middle_state_gradient + layer_norm_backward(
        normalized_gradient, first_centered_scaled, first_inverse_deviation, attention_norm_gain
    )
    local_powers = jnp.stack(
        [
            jnp.sum(row_mask[:, None] * local_input_rows * local_input_rows),
            jnp.sum(row_mask[:, None] * attn * attn),
            jnp.sum(row_mask[:, None] * branch * branch),
            jnp.sum(row_mask[:, None] * output * output),
        ]
    )
    local_count = jnp.sum(row_mask)
    bias_entries = jnp.concatenate([grad_b_query, grad_b_value, grad_b_mlp_in])
    bias_row = jnp.pad(bias_entries, (0, width - bias_entries.shape[0]))[None, :]
    packed = jnp.concatenate(
        [grad_w_qkv, grad_w_attn_out, grad_mlp_in_rows, grad_w_mlp_out, bias_row], axis=0
    )
    packed_rows = packed.shape[0]
    tok_parts = lax.axis_size("tok")
    fill_rows = (tok_parts - packed_rows % tok_parts) % tok_parts
    packed = jnp.pad(packed, ((0, fill_rows), (0, 0)))
    shares = lax.psum_scatter(
        packed.astype(jnp.bfloat16), "tok", scatter_dimension=0, tiled=True
    ).astype(jnp.float32)
    summed = lax.all_gather(shares.astype(jnp.bfloat16), "tok", axis=0, tiled=True).astype(
        shares.dtype
    )[:packed_rows]
    offset = 0
    grad_w_query = summed[offset : offset + width_local]
    offset += width_local
    grad_w_key = summed[offset : offset + width_local]
    offset += width_local
    grad_w_value = summed[offset : offset + width_local]
    offset += width_local
    grad_w_attn_out = summed[offset : offset + width_local]
    offset += width_local
    grad_w_mlp_in = summed[offset : offset + hidden_local].T
    offset += hidden_local
    grad_w_mlp_out = summed[offset : offset + hidden_local]
    offset += hidden_local
    bias_sums = summed[offset]
    grad_b_query = bias_sums[:width_local]
    grad_b_value = bias_sums[width_local : 2 * width_local]
    grad_b_mlp_in = bias_sums[2 * width_local : 2 * width_local + hidden_local]
    (
        grad_b_attn_out,
        grad_b_mlp_out,
        attention_gain_gradient,
        grad_s_attn,
        feedforward_gain_gradient,
        grad_s_mlp,
        powers,
        counted,
    ) = lax.psum(
        (
            grad_b_attn_out,
            grad_b_mlp_out,
            attention_gain_gradient,
            grad_s_attn,
            feedforward_gain_gradient,
            grad_s_mlp,
            local_powers,
            local_count,
        ),
        ("tok", "feat"),
    )
    stream_rms = jnp.sqrt(powers / (jnp.maximum(counted, 1.0) * D))
    return (
        output,
        layer_input_gradient,
        grad_w_query,
        grad_w_key,
        grad_w_value,
        grad_b_query,
        grad_b_value,
        grad_w_attn_out,
        grad_b_attn_out,
        grad_w_mlp_in,
        grad_b_mlp_in,
        grad_w_mlp_out,
        grad_b_mlp_out,
        attention_gain_gradient,
        grad_s_attn,
        feedforward_gain_gradient,
        grad_s_mlp,
        stream_rms,
    )


BF16 = jnp.bfloat16
F32 = jnp.float32
AXES = ("tok", "feat")
SLOTS = (0, 1, 3, 2)
PAIRS = ((0, 1), (3, 2))
CHUNK = 16
PART = DH // 2


SPANS = {
    0: 6,
    1: 1,
    2: 0.01,
    4: 10,
    5: 6,
    6: 60,
    7: 6,
    8: 0.01,
    9: 30,
    10: 6,
    11: 6,
    12: 6,
    13: 1,
    14: 1,
    15: 3,
    16: 3,
    17: 10,
    18: 6,
    19: 1,
    20: 3,
    22: 10,
    24: 3,
    25: 3,
    26: 10,
    27: 1,
    28: 60,
    29: 0.01,
    30: 0.01,
    31: 3,
    32: 3,
    33: 3,
    34: 6,
    35: 60,
    36: 1,
    37: 0.01,
    38: 60,
    39: 0.01,
    41: 60,
    42: 0.01,
    43: 6,
    45: 10,
    46: 0.01,
    47: 0.01,
    48: 0.01,
}
EARLY = {
    2: (2,),
    3: (0,),
    10: (2,),
    15: (21,),
    17: (26, 22, 24),
    18: (24,),
    19: (25,),
    20: (17,),
    21: (26,),
    24: (31, 30),
    25: (17,),
    27: (32,),
    28: (36,),
    30: (29,),
    32: (39,),
    33: (37,),
    35: (43,),
    36: (42,),
    38: (47,),
    40: (53,),
    41: (53,),
    42: (45, 49),
    44: (59, 56, 34),
    45: (56, 58, 42),
}
LATE = {
    7: (0,),
    13: (1,),
    15: (0,),
    17: (1,),
    22: (0,),
    30: (0,),
    42: (0,),
    45: (0,),
}


def route(move):
    found = []
    for tok in range(4):
        for feat in range(8):
            target = move(tok // 2, tok % 2, feat // 2, feat % 2)
            if target is not None:
                x, c, z, y = target
                found.append((tok * 8 + feat, (2 * x + c) * 8 + 2 * z + y))
    return found


SWAP_X = route(lambda x, c, z, y: (1 - x, c, z, y))
SWAP_C = route(lambda x, c, z, y: (x, 1 - c, z, y))
SWAP_Y = route(lambda x, c, z, y: (x, c, z, 1 - y))
UP_Z = route(lambda x, c, z, y: (x, c, (z + 1) % 4, y))
DOWN_Z = route(lambda x, c, z, y: (x, c, (z + 3) % 4, y))
FLIP_Z = [route(lambda x, c, z, y, s=s: (x, c, z ^ s, y)) for s in range(4)]
NEXT = [(t * 8 + f, t * 8 + f + 1) for t in range(4) for f in range(7)]
PREVIOUS = [(t * 8 + f + 1, t * 8 + f) for t in range(4) for f in range(7)]


def nt(left, right):
    return lax.dot_general(left, right, (((1,), (1,)), ((), ())), preferred_element_type=F32)


def nn(left, right):
    return lax.dot_general(left, right, (((1,), (0,)), ((), ())), preferred_element_type=F32)


def tn(left, right):
    return lax.dot_general(left, right, (((0,), (0,)), ((), ())), preferred_element_type=F32)


SMEM = pl.BlockSpec(memory_space=pltpu.SMEM)
HBM = pl.BlockSpec(memory_space=pltpu.HBM)
VMEM = pl.BlockSpec(memory_space=pltpu.VMEM)


def kernel_call(body, operands, specs, outs, scratch=(), after=(), span=0.01, vmem=12):
    count, extra = len(operands), len(after)

    def kernel(*refs):
        body(*refs[:count], *refs[count + extra :])

    return pl.pallas_call(
        kernel,
        in_specs=list(specs) + [VMEM] * extra,
        out_specs=[VMEM] * len(outs),
        out_shape=[jax.ShapeDtypeStruct(shape, dtype) for shape, dtype in outs],
        scratch_shapes=list(scratch),
        compiler_params=pltpu.CompilerParams(
            vmem_limit_bytes=vmem * 2**20, fuse_transposed_lhs_in_matmul=True
        ),
        cost_estimate=pl.CostEstimate(
            flops=int(span * 1e9), bytes_accessed=2**16, transcendentals=0
        ),
    )(*operands, *after)


def coordinates():
    tok, feat = lax.axis_index("tok"), lax.axis_index("feat")
    return tok // 2, tok % 2, feat // 2, feat % 2


def chunks(half):
    return [slice(at, at + CHUNK) for at in range(0, half, CHUNK)]


def row_of(vector):
    return vector[...].astype(F32).reshape(1, vector.shape[0])


def folded(values):
    return values[:8] + values[8:]


def moment_norm(values):
    center = jnp.mean(values, axis=1, keepdims=True)
    spread = jnp.mean(values * values, axis=1, keepdims=True) - center * center
    inverse = lax.rsqrt(spread + EPSILON)
    return (values - center) * inverse, inverse


def attention_weights_kernel(wq, wk, wv, wo, b_query, b_value, b_hidden, *refs):
    own, other, both, query, value, hidden, sems = refs
    piece = own.shape[0]
    x, c, _, _ = coordinates()
    width = own.shape[1]
    copies = []
    for source, target in ((b_query, query), (b_value, value), (b_hidden, hidden)):
        copies.append(pltpu.make_async_copy(source, target, sems.at[len(copies)]))
    targets = ((own, 0, x), (other, 0, 1 - x), (both, 0, x), (both, piece, 1 - x))
    for out, first, side in targets:
        at = pl.multiple_of(c * DH + side * PART, PART)
        for m, w in enumerate((wq, wk, wv, wo)):
            copies.append(
                pltpu.make_async_copy(
                    w.at[pl.ds(at, PART)], out.at[pl.ds(first + m * PART, PART)], sems.at[len(copies)]
                )
            )
    for copy in copies:
        copy.start()
    for copy in copies[:3]:
        copy.wait()
    parts = [row_of(vector) for vector in (query, value, hidden)]
    taken = sum(part.shape[1] for part in parts)
    bias = jnp.concatenate(parts + [jnp.zeros((1, width - taken), F32)], axis=1)
    bias = jnp.broadcast_to(bias, (16, width)).astype(BF16)
    for out, first, _ in targets:
        out[first + 4 * PART : first + piece, :] = bias
    for copy in copies[3:]:
        copy.wait()


def edge_kernel(inputs, cotangent, edge):
    rows = inputs.shape[0]
    at = (rows - 8) // 16 * 16
    for i, values in enumerate((inputs, cotangent)):
        edge[8 * i : 8 * i + 8, :] = values[at:, :].astype(F32)[rows - 8 - at :].astype(BF16)


def mlp_weights_kernel(w_in, w_out, own, other, both):
    x, c, _, _ = coordinates()
    quarter = own.shape[0] // 2
    for out, first, side in ((own, 0, x), (other, 2 * quarter, 1 - x)):
        at = pl.multiple_of((2 * c + side) * quarter, quarter)
        found = w_in[:, pl.ds(at, quarter)].T
        rest = w_out[pl.ds(at, quarter), :]
        out[:quarter, :] = found
        out[quarter:, :] = rest
        both[first : first + quarter, :] = found
        both[first + quarter : first + 2 * quarter, :] = rest


def halves_of(refs, count):
    own_zero, other_zero, own_one, other_one, both, own_two, other_two = refs
    own = [own_zero, own_one, both.at[pl.ds(0, count)], own_two]
    return own, [other_zero, other_one, both.at[pl.ds(count, count)], other_two]


def entry_kernel(
    valid, inputs, cotangent, edge, gain_vector, shift_vector, stream, normed, branch, again, ext
):
    _, _, z, y = coordinates()
    rows = inputs.shape[0]
    half = stream.shape[0]
    gain, shift = row_of(gain_vector), row_of(shift_vector)
    flag = valid[z].astype(F32)

    def aligned(at):
        found = pltpu.roll(ext[at.start : at.stop + 8, :], CHUNK + z, 0)[:CHUNK]
        index = at.start + lax.broadcasted_iota(jnp.int32, (CHUNK, 1), 0)
        return jnp.where(index < rows - y, found, 0.0)

    def fill(values, first):
        ext[0:8, :] = edge[...].astype(F32)[first : first + 8]
        ext[8 : 8 + rows, :] = values[...].astype(F32)

    fill(inputs, 0)
    for at in chunks(half):
        found = aligned(at)
        stream[at, :] = found.astype(BF16)
        hat, _ = moment_norm(found)
        normed[at, :] = (hat * gain + shift).astype(BF16)
    fill(cotangent, 8)
    for at in chunks(half):
        branch[at, :] = (aligned(at) * flag).astype(BF16)
        again[at, :] = branch[at, :]


def softmax_columns(scores):
    top = jnp.max(scores, axis=0, keepdims=True)
    weights = jnp.exp(scores - top)
    return weights * (1.0 / jnp.sum(weights, axis=0, keepdims=True))


def pair_forward(rows, halves, w_in, bias, qkv, probs, mixed):
    half = halves[0].shape[0]
    _, _, _, y = coordinates()
    lanes = 2 * DH
    entry = jnp.concatenate([halves[0][...], halves[1][...]], axis=0)
    qkv[...] = (nt(entry, w_in) + bias).astype(BF16)
    key_index = lax.broadcasted_iota(jnp.int32, (2 * half, 1), 0)
    first = rows - y
    second = half + rows - 1 + y
    real = (key_index < first) | ((key_index >= half) & (key_index < second))
    penalty = jnp.where(real, 0.0, -1e30)
    outs = []
    for h in range(2):
        q = qkv[:, h * DH : (h + 1) * DH] * jnp.asarray(DH ** (-0.5), BF16)
        k = qkv[:, lanes + h * DH : lanes + (h + 1) * DH]
        v = qkv[:, 2 * lanes + h * DH : 2 * lanes + (h + 1) * DH]
        found = softmax_columns(nt(k, q) + penalty).astype(BF16)
        probs[h] = found
        outs.append(tn(v, found))
    mixed[...] = jnp.concatenate(outs, axis=0).T.astype(BF16)


def pair_weights(own, other, w_in, w_out):
    for m in range(4):
        target = w_out if m == 3 else w_in
        for i in range(2):
            at = (0 if m == 3 else m * 2 * DH) + i * DH
            target[at : at + PART, :] = own[i][m * PART : (m + 1) * PART, :]
            target[at + PART : at + DH, :] = other[i][m * PART : (m + 1) * PART, :]
    rows_of = [own[i][4 * PART : 4 * PART + 16, :].astype(F32)[0:1] for i in range(2)]
    query = jnp.concatenate([ordered_bias(r, 0) for r in rows_of], axis=1)
    value = jnp.concatenate([ordered_bias(r, 2 * DH) for r in rows_of], axis=1)
    return jnp.concatenate([query, jnp.zeros_like(query), value], axis=1)


def projected(first_mixed, second_mixed, first_out, second_out, outs):
    mixed = jnp.concatenate([first_mixed[...], second_mixed[...]], axis=1)
    weights = jnp.concatenate([first_out[...], second_out[...]], axis=0)
    found = nn(mixed, weights).astype(BF16)
    at = 0
    for out in outs:
        out[...] = found[at : at + out.shape[0]]
        at += out.shape[0]


def ordered_bias(row, first):
    x, c, _, _ = coordinates()
    block = jnp.where(c == 0, row[:, first : first + DH], row[:, first + DH : first + 2 * DH])
    swapped = jnp.concatenate([block[:, PART:], block[:, :PART]], axis=1)
    return jnp.where(x == 0, block, swapped)


def first_pair_kernel(rows, near, far, near_other, far_other, *refs):
    own_zero, other_zero, own_one, other_one, *refs = refs
    qkv_own, qkv_other, probs_own, probs_other, mixed_own, mixed_other, w_in, w_out = refs
    bias = pair_weights((own_zero, own_one), (other_zero, other_one), w_in, w_out)
    weights = w_in[...]
    pair_forward(rows, (near_other, far_other), weights, bias, qkv_other, probs_other, mixed_other)
    pair_forward(rows, (near, far), weights, bias, qkv_own, probs_own, mixed_own)


def second_pair_other_kernel(rows, near, far, both, own_two, other_two, *refs):
    first_mixed, first_out, qkv, probs, mixed, partial, w_in, w_out, bias = refs
    piece = own_two.shape[0]
    own = (both.at[pl.ds(0, piece)], own_two)
    other = (both.at[pl.ds(piece, piece)], other_two)
    found = pair_weights(own, other, w_in, w_out)
    bias[...] = jnp.broadcast_to(found, bias.shape)
    pair_forward(rows, (near, far), w_in[...], found, qkv, probs, mixed)
    projected(first_mixed, mixed, first_out, w_out, (partial,))


def second_pair_own_kernel(rows, near, far, w_in, w_out, bias, first_mixed, first_out, *refs):
    qkv, probs, mixed, *partials = refs
    pair_forward(rows, (near, far), w_in[...], bias[0:1, :], qkv, probs, mixed)
    projected(first_mixed, mixed, first_out, w_out, partials)


def joined_rows(refs, at):
    size = refs[0].shape[0]
    if at.start < size:
        return refs[0][at, :]
    return refs[1][at.start - size : at.stop - size, :]


def real_rows(at, rows, y):
    return at.start + lax.broadcasted_iota(jnp.int32, (CHUNK, 1), 0) < rows - y


def middle_kernel(
    rows,
    valid,
    partial,
    from_core,
    from_y_first,
    from_y_second,
    stream,
    bias_vector,
    gain_vector,
    shift_vector,
    middle,
    normed,
    powers,
):
    _, _, z, y = coordinates()
    bias, gain, shift = row_of(bias_vector), row_of(gain_vector), row_of(shift_vector)
    total = jnp.zeros((8, middle.shape[1]), F32)
    for at in chunks(middle.shape[0]):
        from_y = joined_rows((from_y_first, from_y_second), at)
        attn = partial[at, :].astype(F32) + from_core[at, :].astype(F32)
        attn = attn + from_y.astype(F32) + bias
        found = stream[at, :].astype(F32) + attn
        middle[at, :] = found
        hat, _ = moment_norm(found)
        normed[at, :] = (hat * gain + shift).astype(BF16)
        total = total + folded(jnp.where(real_rows(at, rows, y), attn * attn, 0.0))
    powers[...] = total * valid[z].astype(F32)


def mlp_kernel(near, far, grad_near, grad_far, *refs):
    own, other = halves_of(refs[:7], refs[0].shape[0])
    bias_of, refs = refs[7:11], refs[11:]
    active, grad_hidden, mid_near, mid_far, out_near, out_far, sums = refs
    x, c, _, _ = coordinates()
    half = near.shape[0]
    quarter = own[0].shape[0] // 2
    w_in = [ref[:quarter, :] for side in (own, other) for ref in side]
    w_out = [ref[quarter:, :] for side in (own, other) for ref in side]
    bias = []
    for side in (x, 1 - x):
        at = pl.multiple_of(4 * DH + (2 * c + side) * quarter, quarter)
        for k in range(4):
            bias.append(bias_of[k][4 * PART :, pl.ds(at, quarter)].astype(F32)[0:1])
    bias = jnp.concatenate(bias, axis=1)
    rows = jnp.concatenate([near[...], far[...]], axis=0)
    grads = jnp.concatenate([grad_near[...], grad_far[...]], axis=0)
    size = 2 * quarter
    for n in range(4):
        at = slice(n * size, (n + 1) * size)
        pair = slice(2 * n, 2 * n + 2)
        u = nt(rows, jnp.concatenate(w_in[pair], axis=0)) + bias[:, at]
        gate = jax.nn.sigmoid(SLOPE * u)
        act = u * gate
        active[:, at] = act.astype(BF16)
        slope = gate + SLOPE * act * (1.0 - gate)
        found = (nt(grads, jnp.concatenate(w_out[pair], axis=0)) * slope).astype(BF16)
        grad_hidden[:, at] = found
        sums[:, at] = jnp.broadcast_to(
            jnp.sum(found.astype(F32), axis=0, keepdims=True), (8, size)
        )
    found = nn(grad_hidden[...], jnp.concatenate(w_in, axis=0)).astype(BF16)
    mid_near[...] = found[:half]
    mid_far[...] = found[half:]
    found = nn(active[...], jnp.concatenate(w_out, axis=0)).astype(BF16)
    out_near[...] = found[:half]
    out_far[...] = found[half:]


def products_kernel(split, left_first, left_second, *refs):
    pieces, outs = refs[:4], refs[4:]
    right = jnp.concatenate([piece[...] for piece in pieces], axis=0)
    hidden = left_first.shape[1] // 2
    quarter = hidden // 4
    for side in (1, 0):
        at = slice(side * hidden, (side + 1) * hidden)
        left = jnp.concatenate([left_first[:, at], left_second[:, at]], axis=0)
        found = tn(left, right).astype(BF16)
        if split:
            for k in range(4):
                outs[k][side * quarter : (side + 1) * quarter, :] = found[
                    k * quarter : (k + 1) * quarter
                ]
        else:
            outs[side][...] = found


def far_sum_kernel(values, received, *outs):
    first = received.shape[0] - values.shape[0]
    done = 0
    for out in outs:
        for at in chunks(out.shape[0]):
            source = slice(done + at.start, done + at.stop)
            moved = slice(first + source.start, first + source.stop)
            found = values[source, :].astype(F32) + received[moved, :].astype(F32)
            out[at, :] = found.astype(BF16)
        done += out.shape[0]


def add_split_kernel(keep, received, *outs):
    at = 0
    for out in outs:
        size = out.shape[0]
        out[...] = (
            keep[at : at + size, :].astype(F32) + received[at : at + size, :].astype(F32)
        ).astype(BF16)
        at += size


def output_kernel(
    rows,
    valid,
    partial,
    from_core,
    from_y,
    middle,
    stream,
    bias_vector,
    attn_power,
    sums,
    output,
    heads,
    small,
):
    _, _, z, y = coordinates()
    bias = row_of(bias_vector)
    width = middle.shape[1]
    totals = [jnp.zeros((8, width), F32) for _ in range(3)]
    for at in chunks(middle.shape[0]):
        branch = partial[at, :].astype(F32) + from_core[at, :].astype(F32)
        branch = branch + from_y[at, :].astype(F32) + bias
        found = middle[at, :] + branch
        output[at, :] = found
        entry = stream[at, :].astype(F32)
        real = real_rows(at, rows, y)
        for i, v in enumerate((entry, branch, found)):
            totals[i] = totals[i] + folded(jnp.where(real, v * v, 0.0))
    heads[...] = output[0:8, :]
    flag = valid[z]
    lane = lax.broadcasted_iota(jnp.int32, (1, width), 1)
    entry = jnp.where(lane == 4, (flag * (rows - y)).astype(F32), 0.0)
    powers = [totals[0] * flag.astype(F32), attn_power[...]]
    powers += [total * flag.astype(F32) for total in totals[1:]]
    for i, power in enumerate(powers):
        whole = jnp.sum(jnp.sum(power, axis=0, keepdims=True), axis=1, keepdims=True)
        entry = entry + jnp.where(lane == i, whole, 0.0)
    row = lax.broadcasted_iota(jnp.int32, (8, 1), 0)
    small[...] = jnp.where(row == 6, entry, sums[...])


def norm_back(grad, hat, inverse, gain):
    scaled = grad * gain
    plain = jnp.mean(scaled, axis=1, keepdims=True)
    cross = jnp.mean(scaled * hat, axis=1, keepdims=True)
    return inverse * (scaled - plain - hat * cross)


def middle_back_kernel(
    partial, from_core, from_y, middle, branch, gain_vector, grad, low, sums
):
    width = middle.shape[1]
    gain = row_of(gain_vector)
    totals = [jnp.zeros((8, width), F32) for _ in range(4)]
    for at in chunks(middle.shape[0]):
        found = partial[at, :].astype(F32) + from_core[at, :].astype(F32)
        found = found + from_y[at, :].astype(F32)
        hat, inverse = moment_norm(middle[at, :])
        gy = branch[at, :].astype(F32)
        total = gy + norm_back(found, hat, inverse, gain)
        grad[at, :] = total
        rounded = total.astype(BF16)
        low[at, :] = rounded
        for i, v in enumerate((rounded.astype(F32), gy, found * hat, found)):
            totals[i] = totals[i] + folded(v)
    sums[...] = jnp.concatenate(
        [jnp.sum(v, axis=0, keepdims=True) for v in totals] + [jnp.zeros((4, width), F32)], axis=0
    )


def backward_kernel(pair, *refs):
    grads, normed, refs = refs[:4], refs[4:8], refs[8:]
    w_out, qkv_own, qkv_other, probs_own, probs_other = refs[:5]
    mixed_own, mixed_other, sums_chip, sums_distant = refs[5:9]
    out_own, out_other, give, keep = refs[9:]
    half = grads[0].shape[0]
    rows = 2 * half
    lanes = 2 * DH
    scale = jnp.asarray(DH ** (-0.5), BF16)
    grad_rows = jnp.concatenate([ref[...] for ref in grads], axis=0)
    wide = nt(grad_rows, w_out[...]).astype(BF16)
    hidden_sums = sums_chip[0:1, :] + sums_distant[0:1, :]
    totals = []
    images = ((qkv_own, probs_own, out_own), (qkv_other, probs_other, out_other))
    for image, (qkv, probs, out) in enumerate(images):
        dq, dk, dv = [], [], []
        for h in range(2):
            at = h * DH
            q = qkv[:, at : at + DH] * scale
            k = qkv[:, lanes + at : lanes + at + DH] * scale
            v = qkv[:, 2 * lanes + at : 2 * lanes + at + DH]
            g = wide[image * rows : (image + 1) * rows, h * DH : (h + 1) * DH]
            found = probs[h]
            grad_probs = nt(v, g)
            scores = found.astype(F32)
            product = scores * grad_probs
            inner = jnp.sum(product, axis=0, keepdims=True)
            grad_scores = (product - scores * inner).astype(BF16)
            dv.append(nn(found, g))
            dk.append(nn(grad_scores, q))
            dq.append(tn(k, grad_scores))
        query = jnp.concatenate(dq, axis=0).T.astype(BF16)
        value = jnp.concatenate(dv, axis=1).astype(BF16)
        out[:, :lanes] = query
        out[:, lanes : 2 * lanes] = jnp.concatenate(dk, axis=1).astype(BF16)
        out[:, 2 * lanes :] = value
        totals.append(
            [jnp.sum(v.astype(F32), axis=0, keepdims=True) for v in (query, value)]
        )
    query_sum, value_sum = (totals[0][i] + totals[1][i] for i in range(2))
    stacked = jnp.concatenate([out_own[...], out_other[...]], axis=0)
    grad_w = tn(stacked, jnp.concatenate([ref[...] for ref in normed], axis=0)).astype(BF16)
    mixed = jnp.concatenate([mixed_own[...], mixed_other[...]], axis=0)
    grad_o = tn(mixed, grad_rows).astype(BF16)
    size = 4 * PART + 16
    quarter = hidden_sums.shape[1] // 8
    width = give.shape[1]
    for side, out in enumerate((keep, give)):
        for i in range(2):
            for m in range(4):
                source = grad_o if m == 3 else grad_w
                at = (0 if m == 3 else m * lanes) + i * DH + side * PART
                out[i * size + m * PART : i * size + (m + 1) * PART, :] = source[at : at + PART]
            at = i * DH + side * PART
            block = (side * 4 + 2 * pair + i) * quarter
            row = jnp.concatenate(
                [
                    query_sum[:, at : at + PART],
                    value_sum[:, at : at + PART],
                    jnp.zeros((1, DH), F32),
                    hidden_sums[:, block : block + quarter],
                    jnp.zeros((1, width - lanes - quarter), F32),
                ],
                axis=1,
            )
            out[i * size + 4 * PART : (i + 1) * size, :] = jnp.broadcast_to(row, (16, width)).astype(
                BF16
            )


def entry_product_kernel(first_pair, second_pair, first_weights, second_weights, *outs):
    joined = jnp.concatenate([first_pair[...], second_pair[...]], axis=1)
    weights = jnp.concatenate([first_weights[...], second_weights[...]], axis=0)
    found = nn(joined, weights).astype(BF16)
    at = 0
    for out in outs:
        out[...] = found[at : at + out.shape[0]]
        at += out.shape[0]


def entry_back_kernel(
    rows,
    valid,
    partial,
    from_core,
    from_y,
    stream,
    grad_middle,
    gain_vector,
    middle_sums,
    grad,
    heads,
    small,
):
    width = stream.shape[1]
    gain = row_of(gain_vector)
    totals = [jnp.zeros((8, width), F32) for _ in range(2)]
    for at in chunks(stream.shape[0]):
        found = partial[at, :].astype(F32) + from_core[at, :].astype(F32)
        found = found + from_y[at, :].astype(F32)
        hat, inverse = moment_norm(stream[at, :].astype(F32))
        grad[at, :] = grad_middle[at, :] + norm_back(found, hat, inverse, gain)
        for i, v in enumerate((found * hat, found)):
            totals[i] = totals[i] + folded(v)
    heads[...] = grad[0:8, :]
    small[...] = jnp.concatenate(
        [middle_sums[0:2, :]]
        + [jnp.sum(v, axis=0, keepdims=True) for v in totals]
        + [middle_sums[2:4, :], middle_sums[6:8, :]],
        axis=0,
    )


def exit_kernel(values, after, out, ext):
    _, _, z, y = coordinates()
    half = values.shape[0]
    rows = out.shape[0]
    count = rows - y
    index = lax.broadcasted_iota(jnp.int32, (half, 1), 0)
    ext[8:, :] = jnp.zeros((half - 8, ext.shape[1]), F32)
    ext[0:8, :] = after[...]
    moved = pltpu.roll(values[...], half - z, 0)
    beyond = pltpu.roll(ext[...], count - z, 0)
    out[...] = jnp.where(index < count - z, moved, beyond)[:rows]


def attention_gradients_kernel(own, across, core, core_across, *outs):
    x, c, _, _ = coordinates()
    query, value, hidden = outs[4:]
    pieces = ((own, c, x), (across, c, 1 - x), (core, 1 - c, x), (core_across, 1 - c, 1 - x))
    for ref, c_of, x_of in pieces:
        at = pl.multiple_of(c_of * DH + x_of * PART, PART)
        for m in range(4):
            outs[m][pl.ds(at, PART), :] = ref[m * PART : (m + 1) * PART, :].astype(F32)
    rows = [ref[4 * PART :, :].astype(F32)[0:1] for ref, _, _ in pieces]
    natural = []
    for c_of in range(2):
        for x_of in range(2):
            same = jnp.where(x == x_of, rows[0], rows[1])
            changed = jnp.where(x == x_of, rows[2], rows[3])
            natural.append(jnp.where(c == c_of, same, changed))
    quarter = hidden.shape[0] // 4
    for out, at, size in ((query, 0, PART), (value, PART, PART), (hidden, 2 * DH, quarter)):
        found = jnp.concatenate([row[:, at : at + size] for row in natural], axis=1)
        out[...] = found.reshape(out.shape)


def mlp_in_gradient_kernel(own, across, core, core_across, out):
    x, c, _, _ = coordinates()
    pieces = ((own, c, x), (across, c, 1 - x), (core, 1 - c, x), (core_across, 1 - c, 1 - x))
    for ref, c_of, x_of in pieces:
        quarter = ref.shape[0]
        at = pl.multiple_of((2 * c_of + x_of) * quarter, quarter)
        out[:, pl.ds(at, quarter)] = ref[...].astype(F32).T


def swapped_sum_kernel(own, received, out):
    size = own.shape[0] // 2
    out[:size, :] = (own[:size, :].astype(F32) + received[size:, :].astype(F32)).astype(BF16)
    out[size:, :] = (own[size:, :].astype(F32) + received[:size, :].astype(F32)).astype(BF16)


def mlp_out_gradient_kernel(own, core, out):
    x, c, _, _ = coordinates()
    for ref, c_of in ((own, c), (core, 1 - c)):
        quarter = ref.shape[0] // 2
        for i, side in enumerate((x, 1 - x)):
            at = pl.multiple_of((2 * c_of + side) * quarter, quarter)
            out[pl.ds(at, quarter), :] = ref[i * quarter : (i + 1) * quarter, :].astype(F32)


def sums_kernel(small, received, *outs):
    found = small[...] + received[...]
    for i, out in enumerate(outs[:-1]):
        out[...] = found[i : i + 1].reshape(out.shape)
    lane = lax.broadcasted_iota(jnp.int32, (1, found.shape[1]), 1)
    counted = jnp.sum(jnp.where(lane == 4, found[6:7], 0.0), axis=1, keepdims=True)
    powers = jnp.sqrt(found[6:7] / (jnp.maximum(counted, 1.0) * D))
    outs[-1][...] = powers[:, : outs[-1].shape[0]].reshape(outs[-1].shape)


def copy_kernel(source, target):
    target[...] = source[...]


def add_wide_kernel(first, second, out):
    out[...] = first[...] + second[...]


def add_split_last_kernel(keep, received, last, zero, one):
    size = zero.shape[0]
    zero[...] = (keep[:size, :].astype(F32) + received[:size, :].astype(F32)).astype(BF16)
    found = keep[size:, :].astype(F32) + received[size:, :].astype(F32)
    one[...] = (found + last[...].astype(F32)).astype(BF16)


def add_three_kernel(first, second, third, out):
    out[...] = (
        first[...].astype(F32) + second[...].astype(F32) + third[...].astype(F32)
    ).astype(BF16)


def on_device(
    inputs,
    valid,
    cotangent,
    w_query,
    w_key,
    w_value,
    b_query,
    b_value,
    w_attn_out,
    b_attn_out,
    w_mlp_in,
    b_mlp_in,
    w_mlp_out,
    b_mlp_out,
    attention_norm_gain,
    attention_norm_shift,
    feedforward_norm_gain,
    feedforward_norm_shift,
):
    rows, width = inputs.shape
    images = valid.shape[0]
    heads_local = w_query.shape[0] // DH
    hidden_local = w_mlp_out.shape[0]
    shape = (lax.axis_size("tok"), lax.axis_size("feat"), images, heads_local, hidden_local, width)
    if shape != (4, 8, 4, 2, 512, 1024) or 2 * rows != SEQ + 1:
        return on_device_general(
            inputs,
            valid,
            cotangent,
            w_query,
            w_key,
            w_value,
            b_query,
            b_value,
            w_attn_out,
            b_attn_out,
            w_mlp_in,
            b_mlp_in,
            w_mlp_out,
            b_mlp_out,
            attention_norm_gain,
            attention_norm_shift,
            feedforward_norm_gain,
            feedforward_norm_shift,
        )
    half = (rows + 15) // 16 * 16
    image = 2 * half
    quarter = hidden_local // 4
    piece = 4 * PART + 16
    row_block = (half, width)
    low_rows, wide_rows = (row_block, BF16), (row_block, F32)
    last, usual = (), 0.01
    calls, sent = [], []

    def send(values, pairs):
        found = lax.ppermute(values, AXES, pairs)
        sent.append(found)
        return found


    def call(body, operands, outs, scratch=(), gate=(), specs=None, span=None, final=False):
        nonlocal last
        specs = [VMEM] * len(operands) if specs is None else specs
        number = len(calls)
        calls.append(number)
        span = SPANS.get(number, usual if span is None else span)
        gate = [g for i, g in enumerate(gate) if i not in LATE.get(number, ())]
        gate += [sent[i] for i in EARLY.get(number, ()) if i < len(sent)]
        found = kernel_call(body, operands, specs, outs, scratch, last + tuple(gate), span)
        if not final:
            last = (min(found, key=lambda v: v.size * v.dtype.itemsize),)
        return found

    def pin(values, gate=()):
        return call(copy_kernel, (values,), [(values.shape, values.dtype)], gate=gate)[0]

    def far_sum(values, received, gate=(), sizes=(half,)):
        outs = [((size, width), BF16) for size in sizes]
        found = call(far_sum_kernel, (values, received), outs, gate=gate)
        return found if len(sizes) > 1 else found[0]

    def split(values, received, sizes, gate=()):
        outs = [((size, width), BF16) for size in sizes]
        return call(add_split_kernel, (values, received), outs, gate=gate)

    def add_last(values, one, three, gate=()):
        return call(add_three_kernel, (values, one, three), [(values.shape, BF16)], gate=gate)[0]

    in_hbm = [
        pltpu.with_memory_space_constraint(w, pltpu.HBM)
        for w in (w_query, w_key, w_value, w_attn_out, b_query, b_value, b_mlp_in)
    ]
    attn_own, attn_other, attn_both = call(
        attention_weights_kernel,
        in_hbm,
        [((piece, width), BF16)] * 2 + [((2 * piece, width), BF16)],
        scratch=[
            pltpu.VMEM((2 * DH,), BF16),
            pltpu.VMEM((2 * DH,), BF16),
            pltpu.VMEM((hidden_local,), BF16),
            pltpu.SemaphoreType.DMA((19,)),
        ],
        specs=[HBM] * 7,
    )
    own_one = send(attn_own, UP_Z)
    attn_three = send(attn_both, DOWN_Z)
    (edge,) = call(edge_kernel, (inputs, cotangent), [((16, width), BF16)])
    edge = send(edge, NEXT)
    mlp_own, mlp_other, mlp_both = call(
        mlp_weights_kernel,
        (w_mlp_in, w_mlp_out),
        [((2 * quarter, width), BF16)] * 2 + [((4 * quarter, width), BF16)],
    )
    stream, normed, branch_grad, branch_again = call(
        entry_kernel,
        (valid, inputs, cotangent, edge, attention_norm_gain, attention_norm_shift),
        [low_rows] * 4,
        scratch=[pltpu.VMEM((half + 8, width), F32)],
        gate=(own_one,),
        specs=[SMEM] + [VMEM] * 5, span=30)
    own_two = send(own_one, UP_Z)
    other_one = send(own_one, SWAP_X)
    normed_y, normed_c = send(normed, SWAP_Y), send(normed, SWAP_C)
    pin(edge, (own_two, other_one))
    other_two = send(own_two, SWAP_X)
    branch_again = pin(branch_again, (normed_y,))
    normed_yc = send(normed_y, SWAP_C)
    branch_y, branch_c = send(branch_again, SWAP_Y), send(branch_again, SWAP_C)

    lanes = 2 * DH
    pair_out = [((image, 3 * lanes), BF16)], [((2, image, image), BF16)], [((image, lanes), BF16)]
    weight_out = [((3 * lanes, width), BF16), ((lanes, width), BF16)]
    first_pair = call(
        functools.partial(first_pair_kernel, rows),
        (normed, normed_y, normed_c, normed_yc, attn_own, attn_other, own_one, other_one),
        pair_out[0] * 2 + pair_out[1] * 2 + pair_out[2] * 2 + weight_out,
        span=30,
    )
    w_first, out_first = first_pair[6:]
    mlp_first = pin(mlp_own, (attn_three, normed_c))
    mlp_one = send(mlp_first, UP_Z)
    qkv_other, probs_other, mixed_other, partial_other, w_second, out_second, second_bias = call(
        functools.partial(second_pair_other_kernel, rows),
        (normed_c, normed_yc, attn_three, own_two, other_two, first_pair[5], out_first),
        pair_out[0]
        + pair_out[1]
        + pair_out[2]
        + [((image, width), BF16)]
        + weight_out
        + [((8, 3 * lanes), F32)],
        gate=(branch_c,),
        span=30,
    )
    from_core = send(partial_other, SWAP_C)
    qkv_own, probs_own, mixed_own, partial_near, partial_far = call(
        functools.partial(second_pair_own_kernel, rows),
        (normed, normed_y, w_second, out_second, second_bias, first_pair[4], out_first),
        pair_out[0] + pair_out[1] + pair_out[2] + [low_rows] * 2,
        span=30,
    )
    saved = (
        (out_first,) + tuple(first_pair[:6]),
        (out_second, qkv_own, qkv_other, probs_own, probs_other, mixed_own, mixed_other),
    )
    parts_of_half = (half // 2 + 8, half - half // 2 - 8)
    attn_far = far_sum(partial_far, from_core, (branch_y,), parts_of_half)
    from_y = tuple(send(part, SWAP_Y) for part in attn_far)
    mlp_one = pin(mlp_one)
    mlp_two = send(mlp_one, UP_Z)
    mlp_other_one = send(mlp_one, SWAP_X)
    mlp_three = send(pin(mlp_both), DOWN_Z)
    branch_yc = send(branch_y, SWAP_C)
    middle, normed_middle, attn_power = call(
        functools.partial(middle_kernel, rows),
        (valid, partial_near, from_core) + from_y + (stream,)
        + (b_attn_out, feedforward_norm_gain, feedforward_norm_shift),
        [wide_rows, low_rows, ((8, width), F32)],
        gate=(mlp_other_one, branch_yc),
        specs=[SMEM] + [VMEM] * 8, span=30)
    middle_y, middle_c = send(normed_middle, SWAP_Y), send(normed_middle, SWAP_C)
    pin(attn_power, (mlp_two, middle_c))
    mlp_other_two = send(mlp_two, SWAP_X)

    usual = 10
    middle_yc = send(middle_y, SWAP_C)
    pieces = (mlp_own, mlp_other, mlp_one, mlp_other_one, mlp_three, mlp_two, mlp_other_two)
    pieces += (attn_own, own_one, attn_three, own_two)
    mlp_out = (
        [((image, 8 * quarter), BF16)] * 2 + [low_rows] * 4 + [((8, 8 * quarter), F32)]
    )
    chip = call(
        mlp_kernel,
        (normed_middle, middle_c, branch_grad, branch_c) + pieces,
        mlp_out,
        gate=(middle_y,),
    )
    mid_core, out_core = send(chip[3], SWAP_C), send(chip[5], SWAP_C)
    distant = call(mlp_kernel, (middle_y, middle_yc, branch_y, branch_yc) + pieces, mlp_out)
    out_distant = send(distant[5], SWAP_C)
    mid_far = far_sum(distant[2], send(distant[3], SWAP_C), (mid_core, out_core))
    mid_y = send(mid_far, SWAP_Y)

    grad_out = call(
        functools.partial(products_kernel, True),
        (chip[0], distant[0], branch_grad, branch_c, branch_y, branch_yc),
        [((2 * quarter, width), BF16)] * 4,
        gate=(out_distant,),
    )
    grad_out = dict(zip(SLOTS, grad_out))
    out_two = send(grad_out[2], DOWN_Z)
    out_three = send(grad_out[3], UP_Z)
    grad_in_keep, grad_in_give = call(
        functools.partial(products_kernel, False),
        (chip[1], distant[1], normed_middle, middle_c, middle_y, middle_yc),
        [((4 * quarter, width), BF16)] * 2,
    )
    in_received = send(grad_in_give, SWAP_X)
    grad_middle, grad_attn, middle_sums = call(
        middle_back_kernel,
        (chip[2], mid_core, mid_y, middle, branch_grad, feedforward_norm_gain),
        [wide_rows, low_rows, ((8, width), F32)],
    )
    grad_y, grad_c = send(grad_attn, SWAP_Y), send(grad_attn, SWAP_C)
    out_far = far_sum(distant[4], out_distant)
    (one,) = split(grad_out[1], out_two, (2 * quarter,), (grad_c,))
    out_one = send(one, DOWN_Z)
    grad_yc = send(grad_y, SWAP_C)

    def backward(p, gate=()):
        return call(
            functools.partial(backward_kernel, p),
            (grad_attn, grad_y, grad_c, grad_yc, normed, normed_y, normed_c, normed_yc)
            + saved[p]
            + (chip[6], distant[6]),
            [((image, 6 * DH), BF16)] * 2 + [((2 * piece, width), BF16)] * 2,
            gate=gate,
        )

    second_own, second_other, give, keep = backward(1)
    received = send(give, SWAP_X)
    out_y = send(pin(out_far), SWAP_Y)
    first_own, first_other, give_first, keep_first = backward(0, (out_one, out_three))
    received_first = send(give_first, SWAP_X)
    in_pieces = split(grad_in_keep, in_received, (quarter,) * 4)
    in_pieces = dict(zip(SLOTS, in_pieces))
    in_two = send(in_pieces[2], DOWN_Z)
    in_three = send(in_pieces[3], UP_Z)
    (entry_other,) = call(
        entry_product_kernel, (first_other, second_other, w_first, w_second), [((image, width), BF16)]
    )
    entry_core = send(entry_other, SWAP_C)
    entry_near, entry_far = call(
        entry_product_kernel, (first_own, second_own, w_first, w_second), [low_rows] * 2
    )
    entry_far = far_sum(entry_far, entry_core)
    entry_y = send(entry_far, SWAP_Y)
    three, two = split(keep, received, (piece,) * 2, (in_three,))
    attn_two = send(two, DOWN_Z)
    attn_three = send(three, UP_Z)
    (one,) = split(in_pieces[1], in_two, (quarter,))
    in_one = send(one, DOWN_Z)
    output, output_heads, power_sums = call(
        functools.partial(output_kernel, rows),
        (valid, chip[4], out_core, out_y, middle, stream, b_mlp_out, attn_power, middle_sums),
        [wide_rows, ((8, width), F32), ((8, width), F32)],
        specs=[SMEM] + [VMEM] * 8,
    )
    output_after = send(output_heads, PREVIOUS)
    out_total = call(
        add_three_kernel,
        (grad_out[0], out_one, out_three),
        [((2 * quarter, width), BF16)],
        gate=(received_first,),
    )[0]
    out_across = send(out_total, SWAP_X)
    zero, one = call(
        add_split_last_kernel,
        (keep_first, received_first, attn_two),
        [((piece, width), BF16)] * 2,
    )
    attn_one = send(one, DOWN_Z)
    gradient, heads, small = call(
        functools.partial(entry_back_kernel, rows),
        (valid, entry_near, entry_core, entry_y, stream, grad_middle)
        + (attention_norm_gain, power_sums),
        [wide_rows, ((8, width), F32), ((8, width), F32)],
        gate=(attn_three,),
        specs=[SMEM] + [VMEM] * 7,
    )

    def add_small(received, gate=()):
        return call(add_wide_kernel, (small, received), [(small.shape, F32)], gate=gate)[0]

    def rows_out(values, after):
        return call(
            exit_kernel,
            (values, after),
            [((rows, width), F32)],
            scratch=[pltpu.VMEM((half, width), F32)],
            final=True,
        )[0]

    small = add_small(send(small, SWAP_C))
    small_y = send(small, SWAP_Y)
    heads_after = send(heads, PREVIOUS)
    attn_total = add_last(zero, attn_one, attn_three, (out_across,))
    attn_across, attn_core = send(attn_total, SWAP_X), send(attn_total, SWAP_C)
    (out_whole,) = call(
        swapped_sum_kernel,
        (out_total, out_across),
        [((2 * quarter, width), BF16)],
    )
    out_core = send(out_whole, SWAP_C)
    small = add_small(small_y, (attn_core,))
    small_z = send(small, FLIP_Z[1])
    output_rows = rows_out(output, output_after)
    gradient_rows = rows_out(gradient, heads_after)
    in_total = add_last(in_pieces[0], in_one, in_three, (out_core,))
    in_across, in_core = send(in_total, SWAP_X), send(in_total, SWAP_C)
    small = add_small(small_z)
    small_z = send(small, FLIP_Z[2])
    (grad_w_mlp_out,) = call(
        mlp_out_gradient_kernel,
        (out_whole, out_core),
        [((hidden_local, width), F32)],
        final=True,
    )
    attn_last = send(attn_across, SWAP_C)
    small = add_small(small_z, (in_core,))
    small_x = send(small, SWAP_X)
    attn_grads = call(
        attention_gradients_kernel,
        (attn_total, attn_across, attn_core, attn_last),
        [((2 * DH, width), F32)] * 4
        + [((2 * DH,), F32), ((2 * DH,), F32), ((hidden_local,), F32)],
        final=True,
    )
    in_last = send(in_across, SWAP_C)
    (grad_w_mlp_in,) = call(
        mlp_in_gradient_kernel,
        (in_total, in_across, in_core, in_last),
        [((width, hidden_local), F32)],
        final=True,
    )
    *vectors, stream_rms = call(
        sums_kernel,
        (small, small_x),
        [((width,), F32)] * 6 + [((4,), F32)],
        final=True,
    )
    return (
        output_rows,
        gradient_rows,
        attn_grads[0],
        attn_grads[1],
        attn_grads[2],
        attn_grads[4],
        attn_grads[5],
        attn_grads[3],
        vectors[0],
        grad_w_mlp_in,
        attn_grads[6],
        grad_w_mlp_out,
        vectors[1],
        vectors[2],
        vectors[3],
        vectors[4],
        vectors[5],
        stream_rms,
    )


def solution(mesh):
    in_specs = (
        P(("tok", "feat"), None),
        P("tok"),
        P(("tok", "feat"), None),
        P("feat", None),
        P("feat", None),
        P("feat", None),
        P("feat"),
        P("feat"),
        P("feat", None),
        P(),
        P(None, "feat"),
        P("feat"),
        P("feat", None),
        P(),
        P(),
        P(),
        P(),
        P(),
    )
    out_specs = (
        P(("tok", "feat"), None),
        P(("tok", "feat"), None),
        P("feat", None),
        P("feat", None),
        P("feat", None),
        P("feat"),
        P("feat"),
        P("feat", None),
        P(),
        P(None, "feat"),
        P("feat"),
        P("feat", None),
        P(),
        P(),
        P(),
        P(),
        P(),
        P(),
    )
    return jax.shard_map(
        on_device, mesh=mesh, in_specs=in_specs, out_specs=out_specs, check_vma=False
    )
```

```python
import functools

import jax
import jax.numpy as jnp
from jax import lax
from jax.experimental import pallas as pl
from jax.experimental.pallas import tpu as pltpu
from jax.sharding import PartitionSpec as P

D = 1024
DH = 64
SEQ = 577


EPSILON = 1e-05
SLOPE = 1.702


def gelu_slope(values):
    sigmoid = jax.nn.sigmoid(SLOPE * values)
    return sigmoid + SLOPE * values * sigmoid * (1.0 - sigmoid)


def column_sums(values):
    return jnp.sum(values.astype(jnp.float32), axis=0)


def split_heads(values):
    return values.reshape(values.shape[0], values.shape[1] // DH, DH)


def apply_layer_norm(values):
    center = jnp.mean(values, axis=1, keepdims=True)
    spread = jnp.mean(values * values, axis=1, keepdims=True) - center * center
    inverse_deviation = lax.rsqrt(spread + EPSILON)
    return ((values - center) * inverse_deviation, inverse_deviation)


def layer_norm_backward(normalized_gradient, centered_scaled, inverse_deviation, norm_gain):
    scaled_output = normalized_gradient * norm_gain.astype(jnp.float32)
    plain_output = jnp.mean(scaled_output, axis=1, keepdims=True)
    cross_term = jnp.mean(scaled_output * centered_scaled, axis=1, keepdims=True)
    return inverse_deviation * (scaled_output - plain_output - centered_scaled * cross_term)


def image_forward(blocks):
    query_img, key_img, value_img = blocks
    scale = DH ** (-0.5)
    query_heads = split_heads(query_img)
    key_heads = split_heads(key_img)
    value_heads = split_heads(value_img)
    scores = (
        jnp.einsum("qhd,khd->hqk", query_heads, key_heads, preferred_element_type=jnp.float32)
        * scale
    )
    top_score = jnp.max(scores, axis=-1, keepdims=True)
    weights = jnp.exp(scores - top_score)
    total = jnp.sum(weights, axis=-1, keepdims=True)
    probs = (weights / total).astype(jnp.bfloat16)
    mixed = jnp.einsum("hqk,khd->qhd", probs, value_heads, preferred_element_type=jnp.float32)
    log_total = top_score[..., 0] + jnp.log(total[..., 0])
    return (mixed.reshape(query_img.shape).astype(jnp.bfloat16), log_total)


def image_backward(blocks):
    query_img, key_img, value_img, grad_img, log_total = blocks
    scale = DH ** (-0.5)
    query_heads = split_heads(query_img)
    key_heads = split_heads(key_img)
    value_heads = split_heads(value_img)
    grad_heads = split_heads(grad_img)
    scores = (
        jnp.einsum("qhd,khd->hqk", query_heads, key_heads, preferred_element_type=jnp.float32)
        * scale
    )
    probs = jnp.exp(scores - log_total[..., None])
    probs_low = probs.astype(jnp.bfloat16)
    grad_probs = jnp.einsum(
        "qhd,khd->hqk", grad_heads, value_heads, preferred_element_type=jnp.float32
    )
    grad_value = jnp.einsum(
        "hqk,qhd->khd", probs_low, grad_heads, preferred_element_type=jnp.float32
    )
    inner = jnp.sum(probs * grad_probs, axis=-1, keepdims=True)
    grad_scores = (probs * (grad_probs - inner)).astype(jnp.bfloat16)
    grad_query = (
        jnp.einsum("hqk,khd->qhd", grad_scores, key_heads, preferred_element_type=jnp.float32)
        * scale
    )
    grad_key = (
        jnp.einsum("hqk,qhd->khd", grad_scores, query_heads, preferred_element_type=jnp.float32)
        * scale
    )
    shape_img = query_img.shape
    return (
        grad_query.reshape(shape_img).astype(jnp.bfloat16),
        grad_key.reshape(shape_img).astype(jnp.bfloat16),
        grad_value.reshape(shape_img).astype(jnp.bfloat16),
    )


def by_image(values, images):
    return values.reshape(images, values.shape[0] // images, values.shape[1])


def on_device_general(
    inputs,
    valid,
    cotangent,
    w_query,
    w_key,
    w_value,
    b_query,
    b_value,
    w_attn_out,
    b_attn_out,
    w_mlp_in,
    b_mlp_in,
    w_mlp_out,
    b_mlp_out,
    attention_norm_gain,
    attention_norm_shift,
    feedforward_norm_gain,
    feedforward_norm_shift,
):
    row_count, width = inputs.shape
    images = valid.shape[0]
    group_rows = images * SEQ
    parts = lax.axis_size("feat")
    extra = row_count * parts - group_rows
    width_local = w_query.shape[0]
    hidden_local = w_mlp_out.shape[0]
    global_rows = lax.axis_index("feat") * row_count + jnp.arange(row_count, dtype=jnp.int32)
    owner = global_rows // SEQ
    matches = (owner[:, None] == jnp.arange(images, dtype=jnp.int32)[None, :]).astype(jnp.float32)
    row_mask = jnp.sum(matches * valid.astype(jnp.float32)[None, :], axis=1)
    live = (global_rows < group_rows).astype(jnp.float32)[:, None]

    def padded(values):
        return jnp.pad(values, ((0, extra), (0, 0)))

    local_input_rows = inputs.astype(jnp.float32)
    first_centered_scaled, first_inverse_deviation = apply_layer_norm(local_input_rows)
    normalized_first = (
        first_centered_scaled * attention_norm_gain.astype(jnp.float32)
        + attention_norm_shift.astype(jnp.float32)
    ).astype(jnp.bfloat16)
    normed_full = lax.all_gather(normalized_first, "feat", axis=0, tiled=True)[:group_rows]
    w_qkv = jnp.concatenate([w_query, w_key, w_value], axis=0)
    projected = jnp.einsum("rd,cd->rc", normed_full, w_qkv, preferred_element_type=jnp.float32)
    queries = (projected[:, :width_local] + b_query.astype(jnp.float32)).astype(jnp.bfloat16)
    key_rows = projected[:, width_local : 2 * width_local].astype(jnp.bfloat16)
    value_rows = (projected[:, 2 * width_local :] + b_value.astype(jnp.float32)).astype(
        jnp.bfloat16
    )
    mixed, log_totals = lax.map(
        image_forward,
        (by_image(queries, images), by_image(key_rows, images), by_image(value_rows, images)),
    )
    mixed = mixed.reshape(group_rows, width_local)
    partial_out = jnp.dot(mixed, w_attn_out, preferred_element_type=jnp.float32)
    attn = lax.psum_scatter(
        padded(partial_out), "feat", scatter_dimension=0, tiled=True
    ) + b_attn_out.astype(jnp.float32)
    middle_state = local_input_rows + attn
    second_centered_scaled, second_inverse_deviation = apply_layer_norm(middle_state)
    normalized_middle = (
        second_centered_scaled * feedforward_norm_gain.astype(jnp.float32)
        + feedforward_norm_shift.astype(jnp.float32)
    ).astype(jnp.bfloat16)
    mid_full = lax.all_gather(normalized_middle, "feat", axis=0, tiled=True)[:group_rows]
    hidden = jnp.dot(mid_full, w_mlp_in, preferred_element_type=jnp.float32) + b_mlp_in.astype(
        jnp.float32
    )
    active = (hidden * jax.nn.sigmoid(SLOPE * hidden)).astype(jnp.bfloat16)
    partial_mlp = jnp.dot(active, w_mlp_out, preferred_element_type=jnp.float32)
    branch = lax.psum_scatter(
        padded(partial_mlp).astype(jnp.bfloat16), "feat", scatter_dimension=0, tiled=True
    ).astype(jnp.float32) + b_mlp_out.astype(jnp.float32)
    output = (middle_state + branch) * live
    output_gradient = cotangent.astype(jnp.float32) * row_mask[:, None]
    grad_branch = output_gradient.astype(jnp.bfloat16)
    grad_b_mlp_out = column_sums(grad_branch)
    branch_full = lax.all_gather(grad_branch, "feat", axis=0, tiled=True)[:group_rows]
    grad_w_mlp_out = jnp.einsum(
        "rf,rd->fd", active, branch_full, preferred_element_type=jnp.float32
    )
    grad_active = jnp.einsum(
        "rd,fd->rf", branch_full, w_mlp_out, preferred_element_type=jnp.float32
    )
    grad_hidden = (grad_active * gelu_slope(hidden)).astype(jnp.bfloat16)
    grad_b_mlp_in = column_sums(grad_hidden)
    grad_mlp_in_rows = jnp.einsum(
        "rf,rd->fd", grad_hidden, mid_full, preferred_element_type=jnp.float32
    )
    partial_mid = jnp.einsum("rf,df->rd", grad_hidden, w_mlp_in, preferred_element_type=jnp.float32)
    midpoint_gradient = lax.psum_scatter(
        padded(partial_mid), "feat", scatter_dimension=0, tiled=True
    )
    feedforward_gain_gradient = jnp.sum(midpoint_gradient * second_centered_scaled, axis=0)
    grad_s_mlp = jnp.sum(midpoint_gradient, axis=0)
    middle_state_gradient = output_gradient + layer_norm_backward(
        midpoint_gradient, second_centered_scaled, second_inverse_deviation, feedforward_norm_gain
    )
    grad_attn = middle_state_gradient.astype(jnp.bfloat16)
    grad_b_attn_out = column_sums(grad_attn)
    attn_full = lax.all_gather(grad_attn, "feat", axis=0, tiled=True)[:group_rows]
    grad_w_attn_out = jnp.einsum("rh,rd->hd", mixed, attn_full, preferred_element_type=jnp.float32)
    grad_mixed = jnp.einsum(
        "rd,hd->rh", attn_full, w_attn_out, preferred_element_type=jnp.float32
    ).astype(jnp.bfloat16)
    grad_query, grad_key, grad_value = lax.map(
        image_backward,
        (
            by_image(queries, images),
            by_image(key_rows, images),
            by_image(value_rows, images),
            by_image(grad_mixed, images),
            log_totals,
        ),
    )
    grad_query = grad_query.reshape(group_rows, width_local)
    grad_key = grad_key.reshape(group_rows, width_local)
    grad_value = grad_value.reshape(group_rows, width_local)
    grad_b_query = column_sums(grad_query)
    grad_b_value = column_sums(grad_value)
    grad_qkv = jnp.concatenate([grad_query, grad_key, grad_value], axis=1)
    grad_w_qkv = jnp.einsum("rc,rd->cd", grad_qkv, normed_full, preferred_element_type=jnp.float32)
    partial_in = jnp.einsum("rc,cd->rd", grad_qkv, w_qkv, preferred_element_type=jnp.float32)
    normalized_gradient = lax.psum_scatter(
        padded(partial_in).astype(jnp.bfloat16), "feat", scatter_dimension=0, tiled=True
    ).astype(jnp.float32)
    attention_gain_gradient = jnp.sum(normalized_gradient * first_centered_scaled, axis=0)
    grad_s_attn = jnp.sum(normalized_gradient, axis=0)
    layer_input_gradient = middle_state_gradient + layer_norm_backward(
        normalized_gradient, first_centered_scaled, first_inverse_deviation, attention_norm_gain
    )
    local_powers = jnp.stack(
        [
            jnp.sum(row_mask[:, None] * local_input_rows * local_input_rows),
            jnp.sum(row_mask[:, None] * attn * attn),
            jnp.sum(row_mask[:, None] * branch * branch),
            jnp.sum(row_mask[:, None] * output * output),
        ]
    )
    local_count = jnp.sum(row_mask)
    bias_entries = jnp.concatenate([grad_b_query, grad_b_value, grad_b_mlp_in])
    bias_row = jnp.pad(bias_entries, (0, width - bias_entries.shape[0]))[None, :]
    packed = jnp.concatenate(
        [grad_w_qkv, grad_w_attn_out, grad_mlp_in_rows, grad_w_mlp_out, bias_row], axis=0
    )
    packed_rows = packed.shape[0]
    tok_parts = lax.axis_size("tok")
    fill_rows = (tok_parts - packed_rows % tok_parts) % tok_parts
    packed = jnp.pad(packed, ((0, fill_rows), (0, 0)))
    shares = lax.psum_scatter(
        packed.astype(jnp.bfloat16), "tok", scatter_dimension=0, tiled=True
    ).astype(jnp.float32)
    summed = lax.all_gather(shares.astype(jnp.bfloat16), "tok", axis=0, tiled=True).astype(
        shares.dtype
    )[:packed_rows]
    offset = 0
    grad_w_query = summed[offset : offset + width_local]
    offset += width_local
    grad_w_key = summed[offset : offset + width_local]
    offset += width_local
    grad_w_value = summed[offset : offset + width_local]
    offset += width_local
    grad_w_attn_out = summed[offset : offset + width_local]
    offset += width_local
    grad_w_mlp_in = summed[offset : offset + hidden_local].T
    offset += hidden_local
    grad_w_mlp_out = summed[offset : offset + hidden_local]
    offset += hidden_local
    bias_sums = summed[offset]
    grad_b_query = bias_sums[:width_local]
    grad_b_value = bias_sums[width_local : 2 * width_local]
    grad_b_mlp_in = bias_sums[2 * width_local : 2 * width_local + hidden_local]
    (
        grad_b_attn_out,
        grad_b_mlp_out,
        attention_gain_gradient,
        grad_s_attn,
        feedforward_gain_gradient,
        grad_s_mlp,
        powers,
        counted,
    ) = lax.psum(
        (
            grad_b_attn_out,
            grad_b_mlp_out,
            attention_gain_gradient,
            grad_s_attn,
            feedforward_gain_gradient,
            grad_s_mlp,
            local_powers,
            local_count,
        ),
        ("tok", "feat"),
    )
    stream_rms = jnp.sqrt(powers / (jnp.maximum(counted, 1.0) * D))
    return (
        output,
        layer_input_gradient,
        grad_w_query,
        grad_w_key,
        grad_w_value,
        grad_b_query,
        grad_b_value,
        grad_w_attn_out,
        grad_b_attn_out,
        grad_w_mlp_in,
        grad_b_mlp_in,
        grad_w_mlp_out,
        grad_b_mlp_out,
        attention_gain_gradient,
        grad_s_attn,
        feedforward_gain_gradient,
        grad_s_mlp,
        stream_rms,
    )


BF16 = jnp.bfloat16
F32 = jnp.float32
AXES = ("tok", "feat")
SLOTS = (0, 1, 3, 2)
PAIRS = ((0, 1), (3, 2))
CHUNK = 16
PART = DH // 2


SPANS = {
    0: 6,
    1: 1,
    2: 0.01,
    4: 10,
    5: 6,
    6: 60,
    7: 6,
    8: 0.01,
    9: 30,
    10: 6,
    11: 6,
    12: 6,
    13: 1,
    14: 1,
    15: 3,
    16: 3,
    17: 10,
    18: 6,
    19: 1,
    20: 3,
    22: 10,
    24: 3,
    25: 3,
    26: 10,
    27: 1,
    28: 60,
    29: 0.01,
    30: 0.01,
    31: 3,
    32: 3,
    33: 3,
    34: 6,
    35: 60,
    36: 1,
    37: 0.01,
    38: 60,
    39: 0.01,
    41: 60,
    42: 0.01,
    43: 6,
    45: 10,
    46: 0.01,
    47: 0.01,
    48: 0.01,
}
EARLY = {
    2: (2,),
    3: (0,),
    10: (2,),
    15: (21,),
    17: (26, 22, 24),
    18: (24,),
    19: (25,),
    20: (17,),
    21: (26,),
    24: (31, 30),
    25: (17,),
    27: (32,),
    28: (36,),
    30: (29,),
    32: (39,),
    33: (37,),
    35: (43,),
    36: (42,),
    38: (47,),
    40: (53,),
    41: (53,),
    42: (45, 49),
    44: (59, 56, 34),
    45: (56, 58, 42),
}
LATE = {
    7: (0,),
    13: (1,),
    15: (0,),
    17: (1,),
    22: (0,),
    30: (0,),
    42: (0,),
    45: (0,),
}


def route(move):
    found = []
    for tok in range(4):
        for feat in range(8):
            target = move(tok // 2, tok % 2, feat // 2, feat % 2)
            if target is not None:
                x, c, z, y = target
                found.append((tok * 8 + feat, (2 * x + c) * 8 + 2 * z + y))
    return found


SWAP_X = route(lambda x, c, z, y: (1 - x, c, z, y))
SWAP_C = route(lambda x, c, z, y: (x, 1 - c, z, y))
SWAP_Y = route(lambda x, c, z, y: (x, c, z, 1 - y))
UP_Z = route(lambda x, c, z, y: (x, c, (z + 1) % 4, y))
DOWN_Z = route(lambda x, c, z, y: (x, c, (z + 3) % 4, y))
FLIP_Z = [route(lambda x, c, z, y, s=s: (x, c, z ^ s, y)) for s in range(4)]
NEXT = [(t * 8 + f, t * 8 + f + 1) for t in range(4) for f in range(7)]
PREVIOUS = [(t * 8 + f + 1, t * 8 + f) for t in range(4) for f in range(7)]


def nt(left, right):
    return lax.dot_general(left, right, (((1,), (1,)), ((), ())), preferred_element_type=F32)


def nn(left, right):
    return lax.dot_general(left, right, (((1,), (0,)), ((), ())), preferred_element_type=F32)


def tn(left, right):
    return lax.dot_general(left, right, (((0,), (0,)), ((), ())), preferred_element_type=F32)


SMEM = pl.BlockSpec(memory_space=pltpu.SMEM)
HBM = pl.BlockSpec(memory_space=pltpu.HBM)
VMEM = pl.BlockSpec(memory_space=pltpu.VMEM)


def kernel_call(body, operands, specs, outs, scratch=(), after=(), span=0.01, vmem=12):
    count, extra = len(operands), len(after)

    def kernel(*refs):
        body(*refs[:count], *refs[count + extra :])

    return pl.pallas_call(
        kernel,
        in_specs=list(specs) + [VMEM] * extra,
        out_specs=[VMEM] * len(outs),
        out_shape=[jax.ShapeDtypeStruct(shape, dtype) for shape, dtype in outs],
        scratch_shapes=list(scratch),
        compiler_params=pltpu.CompilerParams(
            vmem_limit_bytes=vmem * 2**20, fuse_transposed_lhs_in_matmul=True
        ),
        cost_estimate=pl.CostEstimate(
            flops=int(span * 1e9), bytes_accessed=2**16, transcendentals=0
        ),
    )(*operands, *after)


def coordinates():
    tok, feat = lax.axis_index("tok"), lax.axis_index("feat")
    return tok // 2, tok % 2, feat // 2, feat % 2


def chunks(half):
    return [slice(at, at + CHUNK) for at in range(0, half, CHUNK)]


def row_of(vector):
    return vector[...].astype(F32).reshape(1, vector.shape[0])


def folded(values):
    return values[:8] + values[8:]


def moment_norm(values):
    center = jnp.mean(values, axis=1, keepdims=True)
    spread = jnp.mean(values * values, axis=1, keepdims=True) - center * center
    inverse = lax.rsqrt(spread + EPSILON)
    return (values - center) * inverse, inverse


def attention_weights_kernel(wq, wk, wv, wo, b_query, b_value, b_hidden, *refs):
    own, other, both, query, value, hidden, sems = refs
    piece = own.shape[0]
    x, c, _, _ = coordinates()
    width = own.shape[1]
    copies = []
    for source, target in ((b_query, query), (b_value, value), (b_hidden, hidden)):
        copies.append(pltpu.make_async_copy(source, target, sems.at[len(copies)]))
    targets = ((own, 0, x), (other, 0, 1 - x), (both, 0, x), (both, piece, 1 - x))
    for out, first, side in targets:
        at = pl.multiple_of(c * DH + side * PART, PART)
        for m, w in enumerate((wq, wk, wv, wo)):
            copies.append(
                pltpu.make_async_copy(
                    w.at[pl.ds(at, PART)], out.at[pl.ds(first + m * PART, PART)], sems.at[len(copies)]
                )
            )
    for copy in copies:
        copy.start()
    for copy in copies[:3]:
        copy.wait()
    parts = [row_of(vector) for vector in (query, value, hidden)]
    taken = sum(part.shape[1] for part in parts)
    bias = jnp.concatenate(parts + [jnp.zeros((1, width - taken), F32)], axis=1)
    bias = jnp.broadcast_to(bias, (16, width)).astype(BF16)
    for out, first, _ in targets:
        out[first + 4 * PART : first + piece, :] = bias
    for copy in copies[3:]:
        copy.wait()


def edge_kernel(inputs, cotangent, edge):
    rows = inputs.shape[0]
    at = (rows - 8) // 16 * 16
    for i, values in enumerate((inputs, cotangent)):
        edge[8 * i : 8 * i + 8, :] = values[at:, :].astype(F32)[rows - 8 - at :].astype(BF16)


def mlp_weights_kernel(w_in, w_out, own, other, both):
    x, c, _, _ = coordinates()
    quarter = own.shape[0] // 2
    for out, first, side in ((own, 0, x), (other, 2 * quarter, 1 - x)):
        at = pl.multiple_of((2 * c + side) * quarter, quarter)
        found = w_in[:, pl.ds(at, quarter)].T
        rest = w_out[pl.ds(at, quarter), :]
        out[:quarter, :] = found
        out[quarter:, :] = rest
        both[first : first + quarter, :] = found
        both[first + quarter : first + 2 * quarter, :] = rest


def halves_of(refs, count):
    own_zero, other_zero, own_one, other_one, both, own_two, other_two = refs
    own = [own_zero, own_one, both.at[pl.ds(0, count)], own_two]
    return own, [other_zero, other_one, both.at[pl.ds(count, count)], other_two]


def entry_kernel(
    valid, inputs, cotangent, edge, gain_vector, shift_vector, stream, normed, branch, again, ext
):
    _, _, z, y = coordinates()
    rows = inputs.shape[0]
    half = stream.shape[0]
    gain, shift = row_of(gain_vector), row_of(shift_vector)
    flag = valid[z].astype(F32)

    def aligned(at):
        found = pltpu.roll(ext[at.start : at.stop + 8, :], CHUNK + z, 0)[:CHUNK]
        index = at.start + lax.broadcasted_iota(jnp.int32, (CHUNK, 1), 0)
        return jnp.where(index < rows - y, found, 0.0)

    def fill(values, first):
        ext[0:8, :] = edge[...].astype(F32)[first : first + 8]
        ext[8 : 8 + rows, :] = values[...].astype(F32)

    fill(inputs, 0)
    for at in chunks(half):
        found = aligned(at)
        stream[at, :] = found.astype(BF16)
        hat, _ = moment_norm(found)
        normed[at, :] = (hat * gain + shift).astype(BF16)
    fill(cotangent, 8)
    for at in chunks(half):
        branch[at, :] = (aligned(at) * flag).astype(BF16)
        again[at, :] = branch[at, :]


def softmax_columns(scores):
    top = jnp.max(scores, axis=0, keepdims=True)
    weights = jnp.exp(scores - top)
    return weights * (1.0 / jnp.sum(weights, axis=0, keepdims=True))


def pair_forward(rows, halves, w_in, bias, qkv, probs, mixed):
    half = halves[0].shape[0]
    _, _, _, y = coordinates()
    lanes = 2 * DH
    entry = jnp.concatenate([halves[0][...], halves[1][...]], axis=0)
    qkv[...] = (nt(entry, w_in) + bias).astype(BF16)
    key_index = lax.broadcasted_iota(jnp.int32, (2 * half, 1), 0)
    first = rows - y
    second = half + rows - 1 + y
    real = (key_index < first) | ((key_index >= half) & (key_index < second))
    penalty = jnp.where(real, 0.0, -1e30)
    outs = []
    for h in range(2):
        q = qkv[:, h * DH : (h + 1) * DH] * jnp.asarray(DH ** (-0.5), BF16)
        k = qkv[:, lanes + h * DH : lanes + (h + 1) * DH]
        v = qkv[:, 2 * lanes + h * DH : 2 * lanes + (h + 1) * DH]
        found = softmax_columns(nt(k, q) + penalty).astype(BF16)
        probs[h] = found
        outs.append(tn(v, found))
    mixed[...] = jnp.concatenate(outs, axis=0).T.astype(BF16)


def pair_weights(own, other, w_in, w_out):
    for m in range(4):
        target = w_out if m == 3 else w_in
        for i in range(2):
            at = (0 if m == 3 else m * 2 * DH) + i * DH
            target[at : at + PART, :] = own[i][m * PART : (m + 1) * PART, :]
            target[at + PART : at + DH, :] = other[i][m * PART : (m + 1) * PART, :]
    rows_of = [own[i][4 * PART : 4 * PART + 16, :].astype(F32)[0:1] for i in range(2)]
    query = jnp.concatenate([ordered_bias(r, 0) for r in rows_of], axis=1)
    value = jnp.concatenate([ordered_bias(r, 2 * DH) for r in rows_of], axis=1)
    return jnp.concatenate([query, jnp.zeros_like(query), value], axis=1)


def projected(first_mixed, second_mixed, first_out, second_out, outs):
    mixed = jnp.concatenate([first_mixed[...], second_mixed[...]], axis=1)
    weights = jnp.concatenate([first_out[...], second_out[...]], axis=0)
    found = nn(mixed, weights).astype(BF16)
    at = 0
    for out in outs:
        out[...] = found[at : at + out.shape[0]]
        at += out.shape[0]


def ordered_bias(row, first):
    x, c, _, _ = coordinates()
    block = jnp.where(c == 0, row[:, first : first + DH], row[:, first + DH : first + 2 * DH])
    swapped = jnp.concatenate([block[:, PART:], block[:, :PART]], axis=1)
    return jnp.where(x == 0, block, swapped)


def first_pair_kernel(rows, near, far, near_other, far_other, *refs):
    own_zero, other_zero, own_one, other_one, *refs = refs
    qkv_own, qkv_other, probs_own, probs_other, mixed_own, mixed_other, w_in, w_out = refs
    bias = pair_weights((own_zero, own_one), (other_zero, other_one), w_in, w_out)
    weights = w_in[...]
    pair_forward(rows, (near_other, far_other), weights, bias, qkv_other, probs_other, mixed_other)
    pair_forward(rows, (near, far), weights, bias, qkv_own, probs_own, mixed_own)


def second_pair_other_kernel(rows, near, far, both, own_two, other_two, *refs):
    first_mixed, first_out, qkv, probs, mixed, partial, w_in, w_out, bias = refs
    piece = own_two.shape[0]
    own = (both.at[pl.ds(0, piece)], own_two)
    other = (both.at[pl.ds(piece, piece)], other_two)
    found = pair_weights(own, other, w_in, w_out)
    bias[...] = jnp.broadcast_to(found, bias.shape)
    pair_forward(rows, (near, far), w_in[...], found, qkv, probs, mixed)
    projected(first_mixed, mixed, first_out, w_out, (partial,))


def second_pair_own_kernel(rows, near, far, w_in, w_out, bias, first_mixed, first_out, *refs):
    qkv, probs, mixed, *partials = refs
    pair_forward(rows, (near, far), w_in[...], bias[0:1, :], qkv, probs, mixed)
    projected(first_mixed, mixed, first_out, w_out, partials)


def joined_rows(refs, at):
    size = refs[0].shape[0]
    if at.start < size:
        return refs[0][at, :]
    return refs[1][at.start - size : at.stop - size, :]


def real_rows(at, rows, y):
    return at.start + lax.broadcasted_iota(jnp.int32, (CHUNK, 1), 0) < rows - y


def middle_kernel(
    rows,
    valid,
    partial,
    from_core,
    from_y_first,
    from_y_second,
    stream,
    bias_vector,
    gain_vector,
    shift_vector,
    middle,
    normed,
    powers,
):
    _, _, z, y = coordinates()
    bias, gain, shift = row_of(bias_vector), row_of(gain_vector), row_of(shift_vector)
    total = jnp.zeros((8, middle.shape[1]), F32)
    for at in chunks(middle.shape[0]):
        from_y = joined_rows((from_y_first, from_y_second), at)
        attn = partial[at, :].astype(F32) + from_core[at, :].astype(F32)
        attn = attn + from_y.astype(F32) + bias
        found = stream[at, :].astype(F32) + attn
        middle[at, :] = found
        hat, _ = moment_norm(found)
        normed[at, :] = (hat * gain + shift).astype(BF16)
        total = total + folded(jnp.where(real_rows(at, rows, y), attn * attn, 0.0))
    powers[...] = total * valid[z].astype(F32)


def mlp_kernel(near, far, grad_near, grad_far, *refs):
    own, other = halves_of(refs[:7], refs[0].shape[0])
    bias_of, refs = refs[7:11], refs[11:]
    active, grad_hidden, mid_near, mid_far, out_near, out_far, sums = refs
    x, c, _, _ = coordinates()
    half = near.shape[0]
    quarter = own[0].shape[0] // 2
    w_in = [ref[:quarter, :] for side in (own, other) for ref in side]
    w_out = [ref[quarter:, :] for side in (own, other) for ref in side]
    bias = []
    for side in (x, 1 - x):
        at = pl.multiple_of(4 * DH + (2 * c + side) * quarter, quarter)
        for k in range(4):
            bias.append(bias_of[k][4 * PART :, pl.ds(at, quarter)].astype(F32)[0:1])
    bias = jnp.concatenate(bias, axis=1)
    rows = jnp.concatenate([near[...], far[...]], axis=0)
    grads = jnp.concatenate([grad_near[...], grad_far[...]], axis=0)
    size = 2 * quarter
    for n in range(4):
        at = slice(n * size, (n + 1) * size)
        pair = slice(2 * n, 2 * n + 2)
        u = nt(rows, jnp.concatenate(w_in[pair], axis=0)) + bias[:, at]
        gate = jax.nn.sigmoid(SLOPE * u)
        act = u * gate
        active[:, at] = act.astype(BF16)
        slope = gate + SLOPE * act * (1.0 - gate)
        found = (nt(grads, jnp.concatenate(w_out[pair], axis=0)) * slope).astype(BF16)
        grad_hidden[:, at] = found
        sums[:, at] = jnp.broadcast_to(
            jnp.sum(found.astype(F32), axis=0, keepdims=True), (8, size)
        )
    found = nn(grad_hidden[...], jnp.concatenate(w_in, axis=0)).astype(BF16)
    mid_near[...] = found[:half]
    mid_far[...] = found[half:]
    found = nn(active[...], jnp.concatenate(w_out, axis=0)).astype(BF16)
    out_near[...] = found[:half]
    out_far[...] = found[half:]


def products_kernel(split, left_first, left_second, *refs):
    pieces, outs = refs[:4], refs[4:]
    right = jnp.concatenate([piece[...] for piece in pieces], axis=0)
    hidden = left_first.shape[1] // 2
    quarter = hidden // 4
    for side in (1, 0):
        at = slice(side * hidden, (side + 1) * hidden)
        left = jnp.concatenate([left_first[:, at], left_second[:, at]], axis=0)
        found = tn(left, right).astype(BF16)
        if split:
            for k in range(4):
                outs[k][side * quarter : (side + 1) * quarter, :] = found[
                    k * quarter : (k + 1) * quarter
                ]
        else:
            outs[side][...] = found


def far_sum_kernel(values, received, *outs):
    first = received.shape[0] - values.shape[0]
    done = 0
    for out in outs:
        for at in chunks(out.shape[0]):
            source = slice(done + at.start, done + at.stop)
            moved = slice(first + source.start, first + source.stop)
            found = values[source, :].astype(F32) + received[moved, :].astype(F32)
            out[at, :] = found.astype(BF16)
        done += out.shape[0]


def add_split_kernel(keep, received, *outs):
    at = 0
    for out in outs:
        size = out.shape[0]
        out[...] = (
            keep[at : at + size, :].astype(F32) + received[at : at + size, :].astype(F32)
        ).astype(BF16)
        at += size


def output_kernel(
    rows,
    valid,
    partial,
    from_core,
    from_y,
    middle,
    stream,
    bias_vector,
    attn_power,
    sums,
    output,
    heads,
    small,
):
    _, _, z, y = coordinates()
    bias = row_of(bias_vector)
    width = middle.shape[1]
    totals = [jnp.zeros((8, width), F32) for _ in range(3)]
    for at in chunks(middle.shape[0]):
        branch = partial[at, :].astype(F32) + from_core[at, :].astype(F32)
        branch = branch + from_y[at, :].astype(F32) + bias
        found = middle[at, :] + branch
        output[at, :] = found
        entry = stream[at, :].astype(F32)
        real = real_rows(at, rows, y)
        for i, v in enumerate((entry, branch, found)):
            totals[i] = totals[i] + folded(jnp.where(real, v * v, 0.0))
    heads[...] = output[0:8, :]
    flag = valid[z]
    lane = lax.broadcasted_iota(jnp.int32, (1, width), 1)
    entry = jnp.where(lane == 4, (flag * (rows - y)).astype(F32), 0.0)
    powers = [totals[0] * flag.astype(F32), attn_power[...]]
    powers += [total * flag.astype(F32) for total in totals[1:]]
    for i, power in enumerate(powers):
        whole = jnp.sum(jnp.sum(power, axis=0, keepdims=True), axis=1, keepdims=True)
        entry = entry + jnp.where(lane == i, whole, 0.0)
    row = lax.broadcasted_iota(jnp.int32, (8, 1), 0)
    small[...] = jnp.where(row == 6, entry, sums[...])


def norm_back(grad, hat, inverse, gain):
    scaled = grad * gain
    plain = jnp.mean(scaled, axis=1, keepdims=True)
    cross = jnp.mean(scaled * hat, axis=1, keepdims=True)
    return inverse * (scaled - plain - hat * cross)


def middle_back_kernel(
    partial, from_core, from_y, middle, branch, gain_vector, grad, low, sums
):
    width = middle.shape[1]
    gain = row_of(gain_vector)
    totals = [jnp.zeros((8, width), F32) for _ in range(4)]
    for at in chunks(middle.shape[0]):
        found = partial[at, :].astype(F32) + from_core[at, :].astype(F32)
        found = found + from_y[at, :].astype(F32)
        hat, inverse = moment_norm(middle[at, :])
        gy = branch[at, :].astype(F32)
        total = gy + norm_back(found, hat, inverse, gain)
        grad[at, :] = total
        rounded = total.astype(BF16)
        low[at, :] = rounded
        for i, v in enumerate((rounded.astype(F32), gy, found * hat, found)):
            totals[i] = totals[i] + folded(v)
    sums[...] = jnp.concatenate(
        [jnp.sum(v, axis=0, keepdims=True) for v in totals] + [jnp.zeros((4, width), F32)], axis=0
    )


def backward_kernel(pair, *refs):
    grads, normed, refs = refs[:4], refs[4:8], refs[8:]
    w_out, qkv_own, qkv_other, probs_own, probs_other = refs[:5]
    mixed_own, mixed_other, sums_chip, sums_distant = refs[5:9]
    out_own, out_other, give, keep = refs[9:]
    half = grads[0].shape[0]
    rows = 2 * half
    lanes = 2 * DH
    scale = jnp.asarray(DH ** (-0.5), BF16)
    grad_rows = jnp.concatenate([ref[...] for ref in grads], axis=0)
    wide = nt(grad_rows, w_out[...]).astype(BF16)
    hidden_sums = sums_chip[0:1, :] + sums_distant[0:1, :]
    totals = []
    images = ((qkv_own, probs_own, out_own), (qkv_other, probs_other, out_other))
    for image, (qkv, probs, out) in enumerate(images):
        dq, dk, dv = [], [], []
        for h in range(2):
            at = h * DH
            q = qkv[:, at : at + DH] * scale
            k = qkv[:, lanes + at : lanes + at + DH] * scale
            v = qkv[:, 2 * lanes + at : 2 * lanes + at + DH]
            g = wide[image * rows : (image + 1) * rows, h * DH : (h + 1) * DH]
            found = probs[h]
            grad_probs = nt(v, g)
            scores = found.astype(F32)
            product = scores * grad_probs
            inner = jnp.sum(product, axis=0, keepdims=True)
            grad_scores = (product - scores * inner).astype(BF16)
            dv.append(nn(found, g))
            dk.append(nn(grad_scores, q))
            dq.append(tn(k, grad_scores))
        query = jnp.concatenate(dq, axis=0).T.astype(BF16)
        value = jnp.concatenate(dv, axis=1).astype(BF16)
        out[:, :lanes] = query
        out[:, lanes : 2 * lanes] = jnp.concatenate(dk, axis=1).astype(BF16)
        out[:, 2 * lanes :] = value
        totals.append(
            [jnp.sum(v.astype(F32), axis=0, keepdims=True) for v in (query, value)]
        )
    query_sum, value_sum = (totals[0][i] + totals[1][i] for i in range(2))
    stacked = jnp.concatenate([out_own[...], out_other[...]], axis=0)
    grad_w = tn(stacked, jnp.concatenate([ref[...] for ref in normed], axis=0)).astype(BF16)
    mixed = jnp.concatenate([mixed_own[...], mixed_other[...]], axis=0)
    grad_o = tn(mixed, grad_rows).astype(BF16)
    size = 4 * PART + 16
    quarter = hidden_sums.shape[1] // 8
    width = give.shape[1]
    for side, out in enumerate((keep, give)):
        for i in range(2):
            for m in range(4):
                source = grad_o if m == 3 else grad_w
                at = (0 if m == 3 else m * lanes) + i * DH + side * PART
                out[i * size + m * PART : i * size + (m + 1) * PART, :] = source[at : at + PART]
            at = i * DH + side * PART
            block = (side * 4 + 2 * pair + i) * quarter
            row = jnp.concatenate(
                [
                    query_sum[:, at : at + PART],
                    value_sum[:, at : at + PART],
                    jnp.zeros((1, DH), F32),
                    hidden_sums[:, block : block + quarter],
                    jnp.zeros((1, width - lanes - quarter), F32),
                ],
                axis=1,
            )
            out[i * size + 4 * PART : (i + 1) * size, :] = jnp.broadcast_to(row, (16, width)).astype(
                BF16
            )


def entry_product_kernel(first_pair, second_pair, first_weights, second_weights, *outs):
    joined = jnp.concatenate([first_pair[...], second_pair[...]], axis=1)
    weights = jnp.concatenate([first_weights[...], second_weights[...]], axis=0)
    found = nn(joined, weights).astype(BF16)
    at = 0
    for out in outs:
        out[...] = found[at : at + out.shape[0]]
        at += out.shape[0]


def entry_back_kernel(
    rows,
    valid,
    partial,
    from_core,
    from_y,
    stream,
    grad_middle,
    gain_vector,
    middle_sums,
    grad,
    heads,
    small,
):
    width = stream.shape[1]
    gain = row_of(gain_vector)
    totals = [jnp.zeros((8, width), F32) for _ in range(2)]
    for at in chunks(stream.shape[0]):
        found = partial[at, :].astype(F32) + from_core[at, :].astype(F32)
        found = found + from_y[at, :].astype(F32)
        hat, inverse = moment_norm(stream[at, :].astype(F32))
        grad[at, :] = grad_middle[at, :] + norm_back(found, hat, inverse, gain)
        for i, v in enumerate((found * hat, found)):
            totals[i] = totals[i] + folded(v)
    heads[...] = grad[0:8, :]
    small[...] = jnp.concatenate(
        [middle_sums[0:2, :]]
        + [jnp.sum(v, axis=0, keepdims=True) for v in totals]
        + [middle_sums[2:4, :], middle_sums[6:8, :]],
        axis=0,
    )


def exit_kernel(values, after, out, ext):
    _, _, z, y = coordinates()
    half = values.shape[0]
    rows = out.shape[0]
    count = rows - y
    index = lax.broadcasted_iota(jnp.int32, (half, 1), 0)
    ext[8:, :] = jnp.zeros((half - 8, ext.shape[1]), F32)
    ext[0:8, :] = after[...]
    moved = pltpu.roll(values[...], half - z, 0)
    beyond = pltpu.roll(ext[...], count - z, 0)
    out[...] = jnp.where(index < count - z, moved, beyond)[:rows]


def attention_gradients_kernel(own, across, core, core_across, *outs):
    x, c, _, _ = coordinates()
    query, value, hidden = outs[4:]
    pieces = ((own, c, x), (across, c, 1 - x), (core, 1 - c, x), (core_across, 1 - c, 1 - x))
    for ref, c_of, x_of in pieces:
        at = pl.multiple_of(c_of * DH + x_of * PART, PART)
        for m in range(4):
            outs[m][pl.ds(at, PART), :] = ref[m * PART : (m + 1) * PART, :].astype(F32)
    rows = [ref[4 * PART :, :].astype(F32)[0:1] for ref, _, _ in pieces]
    natural = []
    for c_of in range(2):
        for x_of in range(2):
            same = jnp.where(x == x_of, rows[0], rows[1])
            changed = jnp.where(x == x_of, rows[2], rows[3])
            natural.append(jnp.where(c == c_of, same, changed))
    quarter = hidden.shape[0] // 4
    for out, at, size in ((query, 0, PART), (value, PART, PART), (hidden, 2 * DH, quarter)):
        found = jnp.concatenate([row[:, at : at + size] for row in natural], axis=1)
        out[...] = found.reshape(out.shape)


def mlp_in_gradient_kernel(own, across, core, core_across, out):
    x, c, _, _ = coordinates()
    pieces = ((own, c, x), (across, c, 1 - x), (core, 1 - c, x), (core_across, 1 - c, 1 - x))
    for ref, c_of, x_of in pieces:
        quarter = ref.shape[0]
        at = pl.multiple_of((2 * c_of + x_of) * quarter, quarter)
        out[:, pl.ds(at, quarter)] = ref[...].T.astype(F32)


def swapped_sum_kernel(own, received, out):
    size = own.shape[0] // 2
    out[:size, :] = (own[:size, :].astype(F32) + received[size:, :].astype(F32)).astype(BF16)
    out[size:, :] = (own[size:, :].astype(F32) + received[:size, :].astype(F32)).astype(BF16)


def mlp_out_gradient_kernel(own, core, out):
    x, c, _, _ = coordinates()
    for ref, c_of in ((own, c), (core, 1 - c)):
        quarter = ref.shape[0] // 2
        for i, side in enumerate((x, 1 - x)):
            at = pl.multiple_of((2 * c_of + side) * quarter, quarter)
            out[pl.ds(at, quarter), :] = ref[i * quarter : (i + 1) * quarter, :].astype(F32)


def sums_kernel(small, received, *outs):
    found = small[...] + received[...]
    for i, out in enumerate(outs[:-1]):
        out[...] = found[i : i + 1].reshape(out.shape)
    lane = lax.broadcasted_iota(jnp.int32, (1, found.shape[1]), 1)
    counted = jnp.sum(jnp.where(lane == 4, found[6:7], 0.0), axis=1, keepdims=True)
    powers = jnp.sqrt(found[6:7] / (jnp.maximum(counted, 1.0) * D))
    outs[-1][...] = powers[:, : outs[-1].shape[0]].reshape(outs[-1].shape)


def copy_kernel(source, target):
    target[...] = source[...]


def add_wide_kernel(first, second, out):
    out[...] = first[...] + second[...]


def add_split_last_kernel(keep, received, last, zero, one):
    size = zero.shape[0]
    zero[...] = (keep[:size, :].astype(F32) + received[:size, :].astype(F32)).astype(BF16)
    found = keep[size:, :].astype(F32) + received[size:, :].astype(F32)
    one[...] = (found + last[...].astype(F32)).astype(BF16)


def add_three_kernel(first, second, third, out):
    out[...] = (
        first[...].astype(F32) + second[...].astype(F32) + third[...].astype(F32)
    ).astype(BF16)


def on_device(
    inputs,
    valid,
    cotangent,
    w_query,
    w_key,
    w_value,
    b_query,
    b_value,
    w_attn_out,
    b_attn_out,
    w_mlp_in,
    b_mlp_in,
    w_mlp_out,
    b_mlp_out,
    attention_norm_gain,
    attention_norm_shift,
    feedforward_norm_gain,
    feedforward_norm_shift,
):
    rows, width = inputs.shape
    images = valid.shape[0]
    heads_local = w_query.shape[0] // DH
    hidden_local = w_mlp_out.shape[0]
    shape = (lax.axis_size("tok"), lax.axis_size("feat"), images, heads_local, hidden_local, width)
    if shape != (4, 8, 4, 2, 512, 1024) or 2 * rows != SEQ + 1:
        return on_device_general(
            inputs,
            valid,
            cotangent,
            w_query,
            w_key,
            w_value,
            b_query,
            b_value,
            w_attn_out,
            b_attn_out,
            w_mlp_in,
            b_mlp_in,
            w_mlp_out,
            b_mlp_out,
            attention_norm_gain,
            attention_norm_shift,
            feedforward_norm_gain,
            feedforward_norm_shift,
        )
    half = (rows + 15) // 16 * 16
    image = 2 * half
    quarter = hidden_local // 4
    piece = 4 * PART + 16
    row_block = (half, width)
    low_rows, wide_rows = (row_block, BF16), (row_block, F32)
    last, usual = (), 0.01
    calls, sent = [], []

    def send(values, pairs):
        found = lax.ppermute(values, AXES, pairs)
        sent.append(found)
        return found


    def call(body, operands, outs, scratch=(), gate=(), specs=None, span=None, final=False):
        nonlocal last
        specs = [VMEM] * len(operands) if specs is None else specs
        number = len(calls)
        calls.append(number)
        span = SPANS.get(number, usual if span is None else span)
        gate = [g for i, g in enumerate(gate) if i not in LATE.get(number, ())]
        gate += [sent[i] for i in EARLY.get(number, ()) if i < len(sent)]
        found = kernel_call(body, operands, specs, outs, scratch, last + tuple(gate), span)
        if not final:
            last = (min(found, key=lambda v: v.size * v.dtype.itemsize),)
        return found

    def pin(values, gate=()):
        return call(copy_kernel, (values,), [(values.shape, values.dtype)], gate=gate)[0]

    def far_sum(values, received, gate=(), sizes=(half,)):
        outs = [((size, width), BF16) for size in sizes]
        found = call(far_sum_kernel, (values, received), outs, gate=gate)
        return found if len(sizes) > 1 else found[0]

    def split(values, received, sizes, gate=()):
        outs = [((size, width), BF16) for size in sizes]
        return call(add_split_kernel, (values, received), outs, gate=gate)

    def add_last(values, one, three, gate=()):
        return call(add_three_kernel, (values, one, three), [(values.shape, BF16)], gate=gate)[0]

    in_hbm = [
        pltpu.with_memory_space_constraint(w, pltpu.HBM)
        for w in (w_query, w_key, w_value, w_attn_out, b_query, b_value, b_mlp_in)
    ]
    attn_own, attn_other, attn_both = call(
        attention_weights_kernel,
        in_hbm,
        [((piece, width), BF16)] * 2 + [((2 * piece, width), BF16)],
        scratch=[
            pltpu.VMEM((2 * DH,), BF16),
            pltpu.VMEM((2 * DH,), BF16),
            pltpu.VMEM((hidden_local,), BF16),
            pltpu.SemaphoreType.DMA((19,)),
        ],
        specs=[HBM] * 7,
    )
    own_one = send(attn_own, UP_Z)
    attn_three = send(attn_both, DOWN_Z)
    (edge,) = call(edge_kernel, (inputs, cotangent), [((16, width), BF16)])
    edge = send(edge, NEXT)
    mlp_own, mlp_other, mlp_both = call(
        mlp_weights_kernel,
        (w_mlp_in, w_mlp_out),
        [((2 * quarter, width), BF16)] * 2 + [((4 * quarter, width), BF16)],
    )
    stream, normed, branch_grad, branch_again = call(
        entry_kernel,
        (valid, inputs, cotangent, edge, attention_norm_gain, attention_norm_shift),
        [low_rows] * 4,
        scratch=[pltpu.VMEM((half + 8, width), F32)],
        gate=(own_one,),
        specs=[SMEM] + [VMEM] * 5, span=30)
    own_two = send(own_one, UP_Z)
    other_one = send(own_one, SWAP_X)
    normed_y, normed_c = send(normed, SWAP_Y), send(normed, SWAP_C)
    pin(edge, (own_two, other_one))
    other_two = send(own_two, SWAP_X)
    branch_again = pin(branch_again, (normed_y,))
    normed_yc = send(normed_y, SWAP_C)
    branch_y, branch_c = send(branch_again, SWAP_Y), send(branch_again, SWAP_C)

    lanes = 2 * DH
    pair_out = [((image, 3 * lanes), BF16)], [((2, image, image), BF16)], [((image, lanes), BF16)]
    weight_out = [((3 * lanes, width), BF16), ((lanes, width), BF16)]
    first_pair = call(
        functools.partial(first_pair_kernel, rows),
        (normed, normed_y, normed_c, normed_yc, attn_own, attn_other, own_one, other_one),
        pair_out[0] * 2 + pair_out[1] * 2 + pair_out[2] * 2 + weight_out,
        span=30,
    )
    w_first, out_first = first_pair[6:]
    mlp_first = pin(mlp_own, (attn_three, normed_c))
    mlp_one = send(mlp_first, UP_Z)
    qkv_other, probs_other, mixed_other, partial_other, w_second, out_second, second_bias = call(
        functools.partial(second_pair_other_kernel, rows),
        (normed_c, normed_yc, attn_three, own_two, other_two, first_pair[5], out_first),
        pair_out[0]
        + pair_out[1]
        + pair_out[2]
        + [((image, width), BF16)]
        + weight_out
        + [((8, 3 * lanes), F32)],
        gate=(branch_c,),
        span=30,
    )
    from_core = send(partial_other, SWAP_C)
    qkv_own, probs_own, mixed_own, partial_near, partial_far = call(
        functools.partial(second_pair_own_kernel, rows),
        (normed, normed_y, w_second, out_second, second_bias, first_pair[4], out_first),
        pair_out[0] + pair_out[1] + pair_out[2] + [low_rows] * 2,
        span=30,
    )
    saved = (
        (out_first,) + tuple(first_pair[:6]),
        (out_second, qkv_own, qkv_other, probs_own, probs_other, mixed_own, mixed_other),
    )
    parts_of_half = (half // 2 + 8, half - half // 2 - 8)
    attn_far = far_sum(partial_far, from_core, (branch_y,), parts_of_half)
    from_y = tuple(send(part, SWAP_Y) for part in attn_far)
    mlp_one = pin(mlp_one)
    mlp_two = send(mlp_one, UP_Z)
    mlp_other_one = send(mlp_one, SWAP_X)
    mlp_three = send(pin(mlp_both), DOWN_Z)
    branch_yc = send(branch_y, SWAP_C)
    middle, normed_middle, attn_power = call(
        functools.partial(middle_kernel, rows),
        (valid, partial_near, from_core) + from_y + (stream,)
        + (b_attn_out, feedforward_norm_gain, feedforward_norm_shift),
        [wide_rows, low_rows, ((8, width), F32)],
        gate=(mlp_other_one, branch_yc),
        specs=[SMEM] + [VMEM] * 8, span=30)
    middle_y, middle_c = send(normed_middle, SWAP_Y), send(normed_middle, SWAP_C)
    pin(attn_power, (mlp_two, middle_c))
    mlp_other_two = send(mlp_two, SWAP_X)

    usual = 10
    middle_yc = send(middle_y, SWAP_C)
    pieces = (mlp_own, mlp_other, mlp_one, mlp_other_one, mlp_three, mlp_two, mlp_other_two)
    pieces += (attn_own, own_one, attn_three, own_two)
    mlp_out = (
        [((image, 8 * quarter), BF16)] * 2 + [low_rows] * 4 + [((8, 8 * quarter), F32)]
    )
    chip = call(
        mlp_kernel,
        (normed_middle, middle_c, branch_grad, branch_c) + pieces,
        mlp_out,
        gate=(middle_y,),
    )
    mid_core, out_core = send(chip[3], SWAP_C), send(chip[5], SWAP_C)
    distant = call(mlp_kernel, (middle_y, middle_yc, branch_y, branch_yc) + pieces, mlp_out)
    out_distant = send(distant[5], SWAP_C)
    mid_far = far_sum(distant[2], send(distant[3], SWAP_C), (mid_core, out_core))
    mid_y = send(mid_far, SWAP_Y)

    grad_out = call(
        functools.partial(products_kernel, True),
        (chip[0], distant[0], branch_grad, branch_c, branch_y, branch_yc),
        [((2 * quarter, width), BF16)] * 4,
        gate=(out_distant,),
    )
    grad_out = dict(zip(SLOTS, grad_out))
    out_two = send(grad_out[2], DOWN_Z)
    out_three = send(grad_out[3], UP_Z)
    grad_in_keep, grad_in_give = call(
        functools.partial(products_kernel, False),
        (chip[1], distant[1], normed_middle, middle_c, middle_y, middle_yc),
        [((4 * quarter, width), BF16)] * 2,
    )
    in_received = send(grad_in_give, SWAP_X)
    grad_middle, grad_attn, middle_sums = call(
        middle_back_kernel,
        (chip[2], mid_core, mid_y, middle, branch_grad, feedforward_norm_gain),
        [wide_rows, low_rows, ((8, width), F32)],
    )
    grad_y, grad_c = send(grad_attn, SWAP_Y), send(grad_attn, SWAP_C)
    out_far = far_sum(distant[4], out_distant)
    (one,) = split(grad_out[1], out_two, (2 * quarter,), (grad_c,))
    out_one = send(one, DOWN_Z)
    grad_yc = send(grad_y, SWAP_C)

    def backward(p, gate=()):
        return call(
            functools.partial(backward_kernel, p),
            (grad_attn, grad_y, grad_c, grad_yc, normed, normed_y, normed_c, normed_yc)
            + saved[p]
            + (chip[6], distant[6]),
            [((image, 6 * DH), BF16)] * 2 + [((2 * piece, width), BF16)] * 2,
            gate=gate,
        )

    second_own, second_other, give, keep = backward(1)
    received = send(give, SWAP_X)
    out_y = send(pin(out_far), SWAP_Y)
    first_own, first_other, give_first, keep_first = backward(0, (out_one, out_three))
    received_first = send(give_first, SWAP_X)
    in_pieces = split(grad_in_keep, in_received, (quarter,) * 4)
    in_pieces = dict(zip(SLOTS, in_pieces))
    in_two = send(in_pieces[2], DOWN_Z)
    in_three = send(in_pieces[3], UP_Z)
    (entry_other,) = call(
        entry_product_kernel, (first_other, second_other, w_first, w_second), [((image, width), BF16)]
    )
    entry_core = send(entry_other, SWAP_C)
    entry_near, entry_far = call(
        entry_product_kernel, (first_own, second_own, w_first, w_second), [low_rows] * 2
    )
    entry_far = far_sum(entry_far, entry_core)
    entry_y = send(entry_far, SWAP_Y)
    three, two = split(keep, received, (piece,) * 2, (in_three,))
    attn_two = send(two, DOWN_Z)
    attn_three = send(three, UP_Z)
    (one,) = split(in_pieces[1], in_two, (quarter,))
    in_one = send(one, DOWN_Z)
    output, output_heads, power_sums = call(
        functools.partial(output_kernel, rows),
        (valid, chip[4], out_core, out_y, middle, stream, b_mlp_out, attn_power, middle_sums),
        [wide_rows, ((8, width), F32), ((8, width), F32)],
        specs=[SMEM] + [VMEM] * 8,
    )
    output_after = send(output_heads, PREVIOUS)
    out_total = call(
        add_three_kernel,
        (grad_out[0], out_one, out_three),
        [((2 * quarter, width), BF16)],
        gate=(received_first,),
    )[0]
    out_across = send(out_total, SWAP_X)
    zero, one = call(
        add_split_last_kernel,
        (keep_first, received_first, attn_two),
        [((piece, width), BF16)] * 2,
    )
    attn_one = send(one, DOWN_Z)
    gradient, heads, small = call(
        functools.partial(entry_back_kernel, rows),
        (valid, entry_near, entry_core, entry_y, stream, grad_middle)
        + (attention_norm_gain, power_sums),
        [wide_rows, ((8, width), F32), ((8, width), F32)],
        gate=(attn_three,),
        specs=[SMEM] + [VMEM] * 7,
    )

    def add_small(received, gate=()):
        return call(add_wide_kernel, (small, received), [(small.shape, F32)], gate=gate)[0]

    def rows_out(values, after):
        return call(
            exit_kernel,
            (values, after),
            [((rows, width), F32)],
            scratch=[pltpu.VMEM((half, width), F32)],
            final=True,
        )[0]

    small = add_small(send(small, SWAP_C))
    small_y = send(small, SWAP_Y)
    heads_after = send(heads, PREVIOUS)
    attn_total = add_last(zero, attn_one, attn_three, (out_across,))
    attn_across, attn_core = send(attn_total, SWAP_X), send(attn_total, SWAP_C)
    (out_whole,) = call(
        swapped_sum_kernel,
        (out_total, out_across),
        [((2 * quarter, width), BF16)],
    )
    out_core = send(out_whole, SWAP_C)
    small = add_small(small_y, (attn_core,))
    small_z = send(small, FLIP_Z[1])
    output_rows = rows_out(output, output_after)
    gradient_rows = rows_out(gradient, heads_after)
    in_total = add_last(in_pieces[0], in_one, in_three, (out_core,))
    in_across, in_core = send(in_total, SWAP_X), send(in_total, SWAP_C)
    small = add_small(small_z)
    small_z = send(small, FLIP_Z[2])
    (grad_w_mlp_out,) = call(
        mlp_out_gradient_kernel,
        (out_whole, out_core),
        [((hidden_local, width), F32)],
        final=True,
    )
    attn_last = send(attn_across, SWAP_C)
    small = add_small(small_z, (in_core,))
    small_x = send(small, SWAP_X)
    attn_grads = call(
        attention_gradients_kernel,
        (attn_total, attn_across, attn_core, attn_last),
        [((2 * DH, width), F32)] * 4
        + [((2 * DH,), F32), ((2 * DH,), F32), ((hidden_local,), F32)],
        final=True,
    )
    in_last = send(in_across, SWAP_C)
    (grad_w_mlp_in,) = call(
        mlp_in_gradient_kernel,
        (in_total, in_across, in_core, in_last),
        [((width, hidden_local), F32)],
        final=True,
    )
    *vectors, stream_rms = call(
        sums_kernel,
        (small, small_x),
        [((width,), F32)] * 6 + [((4,), F32)],
        final=True,
    )
    return (
        output_rows,
        gradient_rows,
        attn_grads[0],
        attn_grads[1],
        attn_grads[2],
        attn_grads[4],
        attn_grads[5],
        attn_grads[3],
        vectors[0],
        grad_w_mlp_in,
        attn_grads[6],
        grad_w_mlp_out,
        vectors[1],
        vectors[2],
        vectors[3],
        vectors[4],
        vectors[5],
        stream_rms,
    )


def solution(mesh):
    in_specs = (
        P(("tok", "feat"), None),
        P("tok"),
        P(("tok", "feat"), None),
        P("feat", None),
        P("feat", None),
        P("feat", None),
        P("feat"),
        P("feat"),
        P("feat", None),
        P(),
        P(None, "feat"),
        P("feat"),
        P("feat", None),
        P(),
        P(),
        P(),
        P(),
        P(),
    )
    out_specs = (
        P(("tok", "feat"), None),
        P(("tok", "feat"), None),
        P("feat", None),
        P("feat", None),
        P("feat", None),
        P("feat"),
        P("feat"),
        P("feat", None),
        P(),
        P(None, "feat"),
        P("feat"),
        P("feat", None),
        P(),
        P(),
        P(),
        P(),
        P(),
        P(),
    )
    return jax.shard_map(
        on_device, mesh=mesh, in_specs=in_specs, out_specs=out_specs, check_vma=False
    )
```
